32 devices in a mesh: dp: 8 (over z, y), fsdp: 4 (over x, core).
Axes of the slice: x: 2, y: 2, z: 4, core: 2. Of those that a mesh axis runs over, the one named last changes fastest.
Arguments:
- inputs: bfloat16 [64, 512, 768], P(('dp', 'fsdp')), may hold values from -6 to 6
- segment_ids: int32 [64, 512], P(('dp', 'fsdp')), may hold values from 0 to 5, as said below
- compressed_segment: int32 [64, 256], P(('dp', 'fsdp')), may hold values from 0 to 5, as said below
- out_grad: bfloat16 [64, 512, 768], P(('dp', 'fsdp')), may hold values from -6 to 6
- attn_weight: float32 [4, 768, 768], P(None, ('dp', 'fsdp')), may hold values from -1.1549411 to 1.1549411
- attn_first: float32 [4, 768, 768], P(None, ('dp', 'fsdp')), may hold values from -68.787348 to 68.787348
- attn_second: float32 [4, 768, 768], P(None, ('dp', 'fsdp')), may hold values from 0.32768 to 64.22528
- up_weight: float32 [768, 3072], P(('dp', 'fsdp')), may hold values from -0.17681352 to 0.17681352
- up_first: float32 [768, 3072], P(('dp', 'fsdp')), may hold values from -30.773287 to 30.773287
- up_second: float32 [768, 3072], P(('dp', 'fsdp')), may hold values from 2.94912 to 11.79648
- down_weight: float32 [3072, 768], P(('dp', 'fsdp')), may hold values from -0.125026039 to 0.125026039
- down_first: float32 [3072, 768], P(('dp', 'fsdp')), may hold values from -45.254834 to 45.254834
- down_second: float32 [3072, 768], P(('dp', 'fsdp')), may hold values from 6.5536 to 26.2144
- compress_weight: float32 [256, 512], P(('dp', 'fsdp')), may hold values from -0.4331029 to 0.4331029
- compress_first: float32 [256, 512], P(('dp', 'fsdp')), may hold values from -86.4 to 86.4
- compress_second: float32 [256, 512], P(('dp', 'fsdp')), may hold values from 25.6 to 102.4
- norm_params: float32 [4, 768], P(None, ('dp', 'fsdp')), may hold values from -1.2 to 1.5
- norm_first: float32 [4, 768], P(None, ('dp', 'fsdp')), may hold values from -128 to 128
- norm_second: float32 [4, 768], P(None, ('dp', 'fsdp')), may hold values from 32.768 to 131.072
Outputs:
- block_output: bfloat16 [64, 512, 768], P(('dp', 'fsdp'))
- input_grad: float32 [64, 512, 768], P(('dp', 'fsdp'))
- attn_first_new: float32 [4, 768, 768], P(None, ('dp', 'fsdp'))
- attn_second_new: float32 [3, 768, 768], P(None, ('dp', 'fsdp'))
- out_second_new: float32 [768, 768], P(('dp', 'fsdp'))
- attn_new: float32 [4, 768, 768], P(None, ('dp', 'fsdp'))
- attn_copy: bfloat16 [4, 768, 768], P(None, ('dp', 'fsdp'))
- up_first_new: float32 [768, 3072], P(('dp', 'fsdp'))
- up_second_new: float32 [768, 3072], P(('dp', 'fsdp'))
- up_new: float32 [768, 3072], P(('dp', 'fsdp'))
- up_copy: bfloat16 [768, 3072], P(('dp', 'fsdp'))
- down_first_new: float32 [3072, 768], P(('dp', 'fsdp'))
- down_second_new: float32 [3072, 768], P(('dp', 'fsdp'))
- down_new: float32 [3072, 768], P(('dp', 'fsdp'))
- down_copy: bfloat16 [3072, 768], P(('dp', 'fsdp'))
- compress_first_new: float32 [256, 512], P(('dp', 'fsdp'))
- compress_second_new: float32 [256, 512], P(('dp', 'fsdp'))
- compress_new: float32 [256, 512], P(('dp', 'fsdp'))
- compress_copy: bfloat16 [256, 512], P(('dp', 'fsdp'))
- norm_first_new: float32 [4, 768], P(None, ('dp', 'fsdp'))
- norm_second_new: float32 [4, 768], P(None, ('dp', 'fsdp'))
- norm_new: float32 [4, 768], P(None, ('dp', 'fsdp'))
- norms: float32 [2, 7], replicated
The draws below stay inside these ranges and needn't reach their ends.
Inputs may be any that keep to these rules, and one draw needn't show every extreme that they name: `segment_ids`: along each row the ids start at 0 and never fall; each segment is one run of tokens whose start and length are multiples of 8. `compressed_segment`: along each row the values start at 0, never fall and end at the largest segment id of the same row; every segment of a row owns one or more compressed rows.
All inputs are finite; a program needn't handle non-finite values.
Results may differ from the reference program's by a relative error of at most 0.015.
The reference program's roundings to bfloat16 on the way count: a program that leaves them out, or rounds other values in their place, can miss the bound.
Values may be sent and summed in bfloat16 or wider, within the bound.
No kernel may reach another device: no remote copies, remote signals or barrier semaphores. Data moves between devices by JAX's collectives and lax.ppermute only.
A program may use at most 192 MiB of HBM per device.

```python
import math
import jax
import jax.numpy as jnp
from jax import lax

D = 768
HEAD_DIM = 64
FF = 3072
COMPRESSED = 256
SEQ = 512
SEGS = 6
STEP = 10
ROWS = 64
TOKENS = 32768


def rising(count, low_end):
    position = jnp.arange(count, dtype=jnp.float32) / max(count - 1, 1)
    return jnp.sqrt(low_end + position)


def shaped_normal(key, shape, entry_scale, axis, low_end):
    standard = jnp.clip(jax.random.normal(key, shape, jnp.float32), -4.0, 4.0)
    factor = rising(shape[axis], low_end)
    view_shape = [1] * len(shape)
    view_shape[axis] = shape[axis]
    return standard * entry_scale * factor.reshape(view_shape)


def second_moment(key, shape, grad_scale):
    spread = jax.random.uniform(key, shape, jnp.float32, 0.0, math.log(4.0))
    return 0.001 * grad_scale * grad_scale * jnp.exp(spread)


def attn_scales():
    return jnp.array([0.7, 0.7, 0.7, 0.1], jnp.float32).reshape(4, 1, 1) * TOKENS ** 0.5


def segment_counts(key):
    counts = jax.random.randint(jax.random.fold_in(key, 5), (ROWS,), 2, SEGS + 1)
    return counts.at[0].set(SEGS)


def boundary_ids(key, counts, slot_count):
    shuffled = jax.vmap(lambda subkey: jax.random.permutation(subkey, slot_count))(jax.random.split(key, ROWS))
    inverse = jnp.argsort(shuffled, axis=1, stable=True)
    chosen = (inverse < counts[:, None] - 1).astype(jnp.int32)
    starts = jnp.concatenate([jnp.zeros((ROWS, 1), jnp.int32), chosen], axis=1)
    return jnp.cumsum(starts, axis=1).astype(jnp.int32)


def draw_segment_ids(key, part):
    counts = segment_counts(key)
    key = jax.random.fold_in(key, 21)
    blocks = boundary_ids(key, counts, SEQ // 8 - 1)
    return jnp.repeat(blocks, 8, axis=1).astype(jnp.int32)


def draw_compressed_segment(key, part):
    counts = segment_counts(key)
    key = jax.random.fold_in(key, 22)
    return boundary_ids(key, counts, COMPRESSED - 1)


def draw_attn_weight(key, part):
    key = jax.random.fold_in(key, 31)
    low_end = 0.5
    entry_scale = jnp.array([1.0, 1.0, 1.0, (COMPRESSED / SEGS) ** 0.5], jnp.float32).reshape(4, 1, 1) * D ** (-0.5)
    return shaped_normal(key, (4, D, D), entry_scale, 1, low_end)


def draw_attn_first(key, part):
    key = jax.random.fold_in(key, 32)
    low_end = 0.5
    return shaped_normal(key, (4, D, D), 0.11 * attn_scales(), 1, low_end)


def draw_attn_second(key, part):
    key = jax.random.fold_in(key, 33)
    return second_moment(key, (4, D, D), attn_scales())


def draw_up_weight(key, part):
    key = jax.random.fold_in(key, 41)
    low_end = 0.5
    return shaped_normal(key, (D, FF), D ** (-0.5), 0, low_end)


def draw_up_first(key, part):
    key = jax.random.fold_in(key, 42)
    low_end = 0.5
    return shaped_normal(key, (D, FF), 0.11 * 0.3 * TOKENS ** 0.5, 0, low_end)


def draw_down_weight(key, part):
    key = jax.random.fold_in(key, 51)
    low_end = 0.5
    return shaped_normal(key, (FF, D), (FF // 2) ** (-0.5), 0, low_end)


def draw_down_first(key, part):
    key = jax.random.fold_in(key, 52)
    low_end = 0.5
    return shaped_normal(key, (FF, D), 0.11 * 0.45 * TOKENS ** 0.5, 0, low_end)


def draw_compress_weight(key, part):
    key = jax.random.fold_in(key, 61)
    low_end = 0.5
    return shaped_normal(key, (COMPRESSED, SEQ), (SEQ // 4) ** (-0.5), 0, low_end)


def draw_compress_first(key, part):
    key = jax.random.fold_in(key, 62)
    low_end = 0.5
    return shaped_normal(key, (COMPRESSED, SEQ), 0.11 * 20.0 * ROWS ** 0.5, 0, low_end)


def draw_norm_params(key, part):
    key = jax.random.fold_in(key, 71)
    gain_top = 1.4
    bias_scale = 0.3
    gains = jax.random.uniform(jax.random.fold_in(key, 1), (2, D), jnp.float32, 0.6, gain_top)
    biases = bias_scale * jnp.clip(jax.random.normal(jax.random.fold_in(key, 2), (2, D), jnp.float32), -4.0, 4.0)
    return jnp.stack([gains[0], biases[0], gains[1], biases[1]])


def level_of(own_key, shape, cuts, smallest, high):
    gain = 1.0
    for dim, shards_of in cuts:
        draws = jax.random.uniform(jax.random.fold_in(jax.random.fold_in(own_key, 6), dim), (shards_of,), jnp.float32, smallest / len(cuts), high / len(cuts))
        gain = gain * jnp.repeat(jnp.exp(draws), shape[dim] // shards_of).reshape((-1,) + (1,) * (len(shape) - 1 - dim))
    return gain


def centred(rng, shape, deviation, reach, cuts=(), kind=jnp.bfloat16):
    result = deviation * jax.random.normal(rng, shape, jnp.float32)
    if cuts:
        result = result * level_of(rng, shape, cuts, -0.22, 0.18)
    return jnp.clip(result, -reach, reach).astype(kind)


def setup_inputs(seed: int = 0) -> dict:
    arg_keys = jax.random.split(jax.random.key(seed), 20)
    return {
        "inputs": centred(arg_keys[0], (ROWS, SEQ, D), 1.0, 6.0, ((0, 32),)),
        "segment_ids": draw_segment_ids(jax.random.fold_in(arg_keys[19], 71), 0),
        "compressed_segment": draw_compressed_segment(jax.random.fold_in(arg_keys[19], 71), 0),
        "out_grad": centred(arg_keys[3], (ROWS, SEQ, D), 1.0, 6.0, ((0, 32),)),
        "attn_weight": draw_attn_weight(jax.random.fold_in(arg_keys[19], 71), 0),
        "attn_first": draw_attn_first(jax.random.fold_in(arg_keys[19], 71), 0),
        "attn_second": draw_attn_second(jax.random.fold_in(arg_keys[19], 71), 0),
        "up_weight": draw_up_weight(jax.random.fold_in(arg_keys[19], 71), 0),
        "up_first": draw_up_first(jax.random.fold_in(arg_keys[19], 71), 0),
        "up_second": jnp.clip(jnp.exp(math.log(11.79648) - 1.3862944 * jax.random.uniform(arg_keys[9], (D, FF), jnp.float32) ** level_of(arg_keys[9], (D, FF), ((0, 32),), -0.2, 0.2)), 2.94912, 11.79648),
        "down_weight": draw_down_weight(jax.random.fold_in(arg_keys[19], 71), 0),
        "down_first": draw_down_first(jax.random.fold_in(arg_keys[19], 71), 0),
        "down_second": jnp.clip(jnp.exp(math.log(26.2144) - 1.3862944 * jax.random.uniform(arg_keys[12], (FF, D), jnp.float32) ** level_of(arg_keys[12], (FF, D), ((0, 32),), -0.2, 0.2)), 6.5536, 26.2144),
        "compress_weight": draw_compress_weight(jax.random.fold_in(arg_keys[19], 71), 0),
        "compress_first": draw_compress_first(jax.random.fold_in(arg_keys[19], 71), 0),
        "compress_second": jnp.clip(jnp.exp(math.log(102.4) - 1.3862944 * jax.random.uniform(arg_keys[15], (COMPRESSED, SEQ), jnp.float32) ** level_of(arg_keys[15], (COMPRESSED, SEQ), ((0, 32),), -0.2, 0.2)), 25.6, 102.4),
        "norm_params": draw_norm_params(jax.random.fold_in(arg_keys[19], 71), 0),
        "norm_first": centred(arg_keys[17], (4, D), (0.11 * TOKENS ** 0.5), 128.0, ((1, 32),), jnp.float32),
        "norm_second": jnp.clip(jnp.exp(math.log(131.072) - 1.3862944 * jax.random.uniform(arg_keys[18], (4, D), jnp.float32) ** level_of(arg_keys[18], (4, D), ((1, 32),), -0.2, 0.2)), 32.768, 131.072),
    }


BETA_ONE = 0.9
BETA_TWO = 0.999
EPSILON = 1e-06
DECAY = 0.01
RATE = 0.5
NORM_EPS = 1e-05
MASKED = -1e+30

@jax.custom_vjp
def low(v):
    return lax.optimization_barrier(v.astype(jnp.bfloat16)).astype(jnp.float32)

@jax.custom_vjp
def low_back(v):
    return v

def low_keep(v):
    return (low(v), None)

def low_pass(kept, grad):
    return (grad,)

def back_keep(v):
    return (v, None)

def back_low(kept, grad):
    return (low(grad),)
low.defvjp(low_keep, low_pass)
low_back.defvjp(back_keep, back_low)

def product(form, left, right):
    return jnp.einsum(form, left, right, precision=lax.Precision.HIGHEST)

def layer_norm(mixed, gain_row, bias_row):
    average = lax.optimization_barrier(jnp.mean(mixed, axis=-1, keepdims=True))
    centered = mixed - average
    inv_std = lax.rsqrt(lax.optimization_barrier(jnp.mean(centered * centered, axis=-1, keepdims=True)) + NORM_EPS)
    return centered * inv_std * gain_row + bias_row

def gelu_exact(argument):
    return jax.nn.gelu(argument, approximate=False)

def block_forward(params, values, segments, compressed):
    attn_all, up_matrix, down_matrix, compress_matrix, norm_all = params
    attn_all = low(attn_all)
    up_matrix = low(up_matrix)
    down_matrix = low(down_matrix)
    compress_matrix = low(compress_matrix)
    norm_all = low(norm_all)
    row_count, length, model_width = values.shape
    head_count = model_width // HEAD_DIM
    queries = low_back(low(product('rsd,de->rse', values, attn_all[0])))
    keys_full = low_back(low(product('rsd,de->rse', values, attn_all[1])))
    values_full = low_back(low(product('rsd,de->rse', values, attn_all[2])))
    member = compressed[:, :, None] == segments[:, None, :]
    masked_proj = jnp.where(member, compress_matrix[None], 0.0)
    comp_keys = low_back(low(product('rks,rsd->rkd', masked_proj, keys_full)))
    comp_values = low_back(low(product('rks,rsd->rkd', masked_proj, values_full)))
    query_heads = queries.reshape(row_count, length, head_count, HEAD_DIM)
    key_heads = comp_keys.reshape(row_count, -1, head_count, HEAD_DIM)
    value_heads = comp_values.reshape(row_count, -1, head_count, HEAD_DIM)
    scores = low_back(product('rshe,rkhe->rhsk', query_heads, key_heads) * HEAD_DIM ** (-0.5))
    allowed = segments[:, None, :, None] == compressed[:, None, None, :]
    scores = jnp.where(allowed, scores, MASKED)
    probability = jax.nn.softmax(scores, axis=-1)
    context = product('rhsk,rkhe->rshe', low(probability), value_heads).reshape(row_count, length, model_width)
    context = low_back(low(context))
    attended = low_back(product('rsd,de->rse', context, attn_all[3]))
    first = layer_norm(values + attended, norm_all[0], norm_all[1])
    hidden = low_back(product('rsd,df->rsf', low(first), up_matrix))
    active = low(gelu_exact(hidden))
    branch = low_back(product('rsf,fd->rsd', active, down_matrix))
    return layer_norm(first + branch, norm_all[2], norm_all[3])

def adaptive(first, second, grad):
    first_new = BETA_ONE * first + (1.0 - BETA_ONE) * grad
    second_new = BETA_TWO * second + (1.0 - BETA_TWO) * grad * grad
    direction = first_new / (1.0 - BETA_ONE ** STEP) / (jnp.sqrt(second_new / (1.0 - BETA_TWO ** STEP)) + EPSILON)
    return (first_new, second_new, direction)

def reference(inputs, segment_ids, compressed_segment, out_grad, attn_weight, attn_first, attn_second, up_weight, up_first, up_second, down_weight, down_first, down_second, compress_weight, compress_first, compress_second, norm_params, norm_first, norm_second):
    params = (attn_weight, up_weight, down_weight, compress_weight, norm_params)
    group_rows = max(1, 4096 // SEQ)
    while ROWS % group_rows:
        group_rows -= 1
    batches = ROWS // group_rows

    def regroup(array):
        return array.reshape((batches, group_rows) + array.shape[1:])

    def one_group(totals, pieces):
        block_in, block_seg, block_comp, block_cot = pieces
        output, pull_back = jax.vjp(lambda weights, values: block_forward(weights, values, block_seg, block_comp), params, block_in.astype(jnp.float32))
        weight_grads, value_grad = pull_back(block_cot.astype(jnp.float32))
        return (jax.tree.map(jnp.add, totals, weight_grads), (output.astype(jnp.bfloat16), value_grad))
    zero_grads = jax.tree.map(jnp.zeros_like, params)
    totals, (outputs, grads) = lax.scan(one_group, zero_grads, (regroup(inputs), regroup(segment_ids), regroup(compressed_segment), regroup(out_grad)))
    attn_grad, up_grad, down_grad, compress_grad, norm_grad = totals
    attn_first_new, attn_second_new, attn_direction = adaptive(attn_first, attn_second, attn_grad)
    up_first_new, up_second_new, up_direction = adaptive(up_first, up_second, up_grad)
    down_first_new, down_second_new, down_direction = adaptive(down_first, down_second, down_grad)
    compress_first_new, compress_second_new, compress_direction = adaptive(compress_first, compress_second, compress_grad)
    norm_first_new, norm_second_new, norm_direction = adaptive(norm_first, norm_second, norm_grad)
    attn_direction = attn_direction + DECAY * attn_weight
    up_direction = up_direction + DECAY * up_weight
    down_direction = down_direction + DECAY * down_weight
    compress_direction = compress_direction + DECAY * compress_weight
    weight_sq = jnp.concatenate([lax.optimization_barrier(jnp.sum(attn_weight * attn_weight, axis=(1, 2))), jnp.stack([jnp.sum(up_weight * up_weight), jnp.sum(down_weight * down_weight), jnp.sum(compress_weight * compress_weight)])])
    update_sq = jnp.concatenate([lax.optimization_barrier(jnp.sum(attn_direction * attn_direction, axis=(1, 2))), jnp.stack([jnp.sum(up_direction * up_direction), jnp.sum(down_direction * down_direction), jnp.sum(compress_direction * compress_direction)])])
    weight_norm = jnp.sqrt(weight_sq)
    update_norm = jnp.sqrt(update_sq)
    trust_ratio = weight_norm / (update_norm + EPSILON)
    attn_new = attn_weight - RATE * trust_ratio[:4].reshape(4, 1, 1) * attn_direction
    up_new = up_weight - RATE * trust_ratio[4] * up_direction
    down_new = down_weight - RATE * trust_ratio[5] * down_direction
    compress_new = compress_weight - RATE * trust_ratio[6] * compress_direction
    norm_new = norm_params - RATE * norm_direction
    norms = jnp.stack([weight_norm, update_norm])
    return (outputs.reshape(ROWS, SEQ, D), grads.reshape(ROWS, SEQ, D), attn_first_new, attn_second_new[:3], attn_second_new[3], attn_new, attn_new.astype(jnp.bfloat16), up_first_new, up_second_new, up_new, up_new.astype(jnp.bfloat16), down_first_new, down_second_new, down_new, down_new.astype(jnp.bfloat16), compress_first_new, compress_second_new, compress_new, compress_new.astype(jnp.bfloat16), norm_first_new, norm_second_new, norm_new, norms)
```

```python
import jax
import jax.numpy as jnp
from jax import lax
from jax.sharding import PartitionSpec as P

HEAD_DIM = 64
STEP = 10


BETA_ONE = 0.9
BETA_TWO = 0.999
EPSILON = 1e-06
DECAY = 0.01
RATE = 0.5
NORM_EPS = 1e-05
MASKED = -1e30

AXES = ("dp", "fsdp")
LOW = jnp.bfloat16
FULL = jnp.float32


class Exchange:
    def __init__(self, dp, fsdp):
        self.count = dp * fsdp
        self.bits = self.count.bit_length() - 1
        self.x_bit = 1
        self.y_bit = fsdp.bit_length() - 1
        self.rest = [b for b in range(1, self.bits) if b not in (self.x_bit, self.y_bit)]
        index = lax.axis_index(AXES)
        self.values = [(index >> b) & 1 for b in range(self.bits)]
        self.core = self.values[0]

    def flip(self, array, even_bit, odd_bit):
        pairs = [(i, i ^ (1 << (odd_bit if i & 1 else even_bit))) for i in range(self.count)]
        return lax.ppermute(array, AXES, pairs)

    def by_core(self, even, odd):
        return jnp.where(self.core == 0, even, odd)

    def joined(self, own, other, value, axis):
        return jnp.where(
            value == 0, jnp.stack([own, other], axis), jnp.stack([other, own], axis)
        )

    def gather(self, shard):
        have = shard
        for place, bit in enumerate(reversed(self.rest)):
            have = self.joined(have, self.flip(have, bit, bit), self.values[bit], place)
        x_value, y_value = self.values[self.x_bit], self.values[self.y_bit]
        got = self.flip(have, self.y_bit, self.x_bit)
        have = self.joined(have, got, self.by_core(y_value, x_value), 0)
        got = self.flip(have, self.x_bit, self.y_bit)
        have = self.joined(have, got, self.by_core(x_value, y_value), 0)
        got = self.flip(have, 0, 0)
        even, odd = self.by_core(have, got), self.by_core(got, have)
        now_even = [self.x_bit, self.y_bit] + self.rest[::-1]
        now_odd = [self.y_bit, self.x_bit] + self.rest[::-1]
        wanted = list(range(self.bits - 1, 0, -1))
        tail = [len(wanted), len(wanted) + 1]
        even = even.transpose([now_even.index(b) for b in wanted] + tail)
        odd = odd.transpose([now_odd.index(b) for b in wanted] + tail)
        whole = jnp.stack([even, odd], axis=len(wanted))
        return whole.reshape((self.count,) + shard.shape)

    def scatter(self, blocks):
        shape = blocks.shape[1:]
        view = blocks.reshape((2,) * self.bits + shape)

        def pick(array, dim, value):
            return lax.dynamic_index_in_dim(array, value, dim, keepdims=False)

        dim = self.bits - 1
        got = self.flip(pick(view, dim, 1 - self.core).astype(LOW), 0, 0)
        view = (pick(view, dim, self.core).astype(FULL) + got.astype(FULL)).astype(LOW)
        bits = list(range(self.bits - 1, 0, -1))
        dim_x, dim_y = bits.index(self.x_bit), bits.index(self.y_bit)
        x_value, y_value = self.values[self.x_bit], self.values[self.y_bit]

        def halves(x_now, y_now):
            even = pick(jnp.moveaxis(view, (dim_x, dim_y), (0, 1)), 0, x_now)
            odd = pick(jnp.moveaxis(view, (dim_y, dim_x), (0, 1)), 0, y_now)
            return self.by_core(even, odd)

        got = self.flip(halves(1 - x_value, 1 - y_value), self.x_bit, self.y_bit)
        view = halves(x_value, y_value).astype(FULL) + got.astype(FULL)
        value = self.by_core(y_value, x_value)
        got = self.flip(pick(view, 0, 1 - value).astype(LOW), self.y_bit, self.x_bit)
        view = pick(view, 0, value) + got.astype(FULL)
        for dim, bit in reversed(list(enumerate(self.rest[::-1]))):
            value = self.values[bit]
            got = self.flip(pick(view, dim, 1 - value).astype(LOW), bit, bit)
            view = pick(view, dim, value) + got.astype(FULL)
        return view

    def total(self, vector):
        row = jnp.zeros((8, 128), FULL).at[0, : vector.shape[0]].set(vector)
        sent = jnp.broadcast_to(row[None], (self.count, 8, 128))
        got = lax.all_to_all(sent, AXES, split_axis=0, concat_axis=0, tiled=True)
        return jnp.sum(got, axis=0)[0, : vector.shape[0]]


def gelu_exact(argument):
    return jax.nn.gelu(argument, approximate=False)


def norm_forward(mixed, gain_row, bias_row):
    average = jnp.mean(mixed, axis=-1, keepdims=True)
    centered = mixed - average
    inv_std = lax.rsqrt(jnp.mean(centered * centered, axis=-1, keepdims=True) + NORM_EPS)
    normalized = centered * inv_std
    return (normalized * gain_row + bias_row, normalized, inv_std)


def norm_backward(grad_out, normalized, inv_std, gain_row):
    scaled = grad_out * gain_row
    grad_in = inv_std * (
        scaled
        - jnp.mean(scaled, axis=-1, keepdims=True)
        - normalized * jnp.mean(scaled * normalized, axis=-1, keepdims=True)
    )
    return (grad_in, jnp.sum(grad_out * normalized, axis=0), jnp.sum(grad_out, axis=0))


def adaptive(first, second, grad):
    first_new = BETA_ONE * first + (1.0 - BETA_ONE) * grad
    second_new = BETA_TWO * second + (1.0 - BETA_TWO) * grad * grad
    direction = (
        first_new
        / (1.0 - BETA_ONE**STEP)
        / (jnp.sqrt(second_new / (1.0 - BETA_TWO**STEP)) + EPSILON)
    )
    return (first_new, second_new, direction)


def matrix_squares(attn_part, up_part, down_part, compress_part):
    return jnp.concatenate(
        [
            jnp.sum(attn_part * attn_part, axis=(1, 2)),
            jnp.stack(
                [
                    jnp.sum(up_part * up_part),
                    jnp.sum(down_part * down_part),
                    jnp.sum(compress_part * compress_part),
                ]
            ),
        ]
    )


def local(
    dp,
    fsdp,
    inputs,
    segment_ids,
    compressed_segment,
    out_grad,
    attn_weight,
    attn_first,
    attn_second,
    up_weight,
    up_first,
    up_second,
    down_weight,
    down_first,
    down_second,
    compress_weight,
    compress_first,
    compress_second,
    norm_params,
    norm_first,
    norm_second,
):
    low_type = LOW
    full_type = FULL
    exchange = Exchange(dp, fsdp)
    devices = dp * fsdp
    row_count, length, model_width = inputs.shape
    norm_kinds, norm_own = norm_params.shape
    attn_kinds, attn_own, _ = attn_weight.shape
    compress_own = compress_weight.shape[0]
    spare = model_width - length
    side_rows = max(compress_own, norm_kinds)

    def side_block(compress_part, norm_part):
        none = [(0, 0)] * (compress_part.ndim - 2)
        left = jnp.pad(compress_part, none + [(0, side_rows - compress_own), (0, 0)])
        right = jnp.pad(norm_part, none + [(0, side_rows - norm_kinds), (0, spare - norm_own)])
        return jnp.concatenate([left, right], axis=-1)

    attn_pack = jnp.concatenate(
        [
            attn_weight.astype(low_type).reshape(attn_kinds * attn_own, model_width),
            side_block(compress_weight.astype(low_type), norm_params.astype(low_type)),
        ]
    )
    attn_blocks = exchange.gather(attn_pack)
    up_full = exchange.gather(up_weight.astype(low_type)).reshape(model_width, -1)
    down_full = exchange.gather(down_weight.astype(low_type)).reshape(-1, model_width)
    attn_full = (
        attn_blocks[:, : attn_kinds * attn_own]
        .reshape(devices, attn_kinds, attn_own, model_width)
        .transpose(1, 0, 2, 3)
        .reshape(attn_kinds, model_width, model_width)
    )
    side = attn_blocks[:, attn_kinds * attn_own :]
    compress_full = side[:, :compress_own, :length].reshape(-1, length)
    norm_full = (
        side[:, :norm_kinds, length : length + norm_own]
        .transpose(1, 0, 2)
        .reshape(norm_kinds, model_width)
    )
    gains = norm_full.astype(full_type)
    head_count = model_width // HEAD_DIM
    token_count = row_count * length
    score_scale = HEAD_DIM ** (-0.5)
    flat_in = inputs.reshape(token_count, model_width)
    projected = jnp.einsum(
        "td,jde->jte", flat_in, attn_full[:3], preferred_element_type=full_type
    ).astype(low_type)
    queries = projected[0].reshape(row_count, length, head_count, HEAD_DIM)
    kv_low = projected[1:3].reshape(2, row_count, length, model_width)
    member = compressed_segment[:, :, None] == segment_ids[:, None, :]
    masked_proj = jnp.where(member, compress_full[None], jnp.zeros((), low_type))
    compressed = jnp.einsum(
        "rks,jrsd->jrkd", masked_proj, kv_low, preferred_element_type=full_type
    ).astype(low_type)
    comp_keys = compressed[0].reshape(row_count, -1, head_count, HEAD_DIM)
    comp_values = compressed[1].reshape(row_count, -1, head_count, HEAD_DIM)
    allowed = segment_ids[:, None, :, None] == compressed_segment[:, None, None, :]
    scores = (
        jnp.einsum("rshe,rkhe->rhsk", queries, comp_keys, preferred_element_type=full_type)
        * score_scale
    )
    scores = jnp.where(allowed, scores, MASKED)
    highest = jnp.max(scores, axis=-1, keepdims=True)
    weights = jnp.exp(scores - highest)
    totals = jnp.sum(weights, axis=-1, keepdims=True)
    log_total = highest + jnp.log(totals)
    probs_low = (weights / totals).astype(low_type)
    context = (
        jnp.einsum("rhsk,rkhe->rshe", probs_low, comp_values, preferred_element_type=full_type)
        .astype(low_type)
        .reshape(token_count, model_width)
    )
    attended = jnp.dot(context, attn_full[3], preferred_element_type=full_type)
    first_out, first_normed, first_inv = norm_forward(
        flat_in.astype(full_type) + attended, gains[0], gains[1]
    )
    first_low = first_out.astype(low_type)
    hidden = jnp.dot(first_low, up_full, preferred_element_type=full_type)
    gelu_value, gelu_pull = jax.vjp(gelu_exact, hidden)
    active = gelu_value.astype(low_type)
    branch = jnp.dot(active, down_full, preferred_element_type=full_type)
    second_out, second_normed, second_inv = norm_forward(first_out + branch, gains[2], gains[3])
    result = second_out.astype(low_type).reshape(row_count, length, model_width)
    grad_top = out_grad.reshape(token_count, model_width).astype(full_type)
    grad_second, gain_two, bias_two = norm_backward(grad_top, second_normed, second_inv, gains[2])
    grad_second_low = grad_second.astype(low_type)
    down_grad = jnp.einsum(
        "tf,td->fd", active, grad_second_low, preferred_element_type=full_type
    ).astype(low_type)
    down_owned = exchange.scatter(down_grad.reshape((devices,) + down_weight.shape))
    grad_active = jnp.einsum(
        "td,fd->tf", grad_second_low, down_full, preferred_element_type=full_type
    )
    grad_hidden_low = gelu_pull(grad_active)[0].astype(low_type)
    up_grad = jnp.einsum(
        "td,tf->df", first_low, grad_hidden_low, preferred_element_type=full_type
    ).astype(low_type)
    up_owned = exchange.scatter(up_grad.reshape((devices,) + up_weight.shape))
    grad_first_out = grad_second + jnp.einsum(
        "tf,df->td", grad_hidden_low, up_full, preferred_element_type=full_type
    )
    grad_first, gain_one, bias_one = norm_backward(
        grad_first_out, first_normed, first_inv, gains[0]
    )
    grad_first_low = grad_first.astype(low_type)
    out_proj_grad = jnp.einsum(
        "td,te->de", context, grad_first_low, preferred_element_type=full_type
    ).astype(low_type)
    grad_context = (
        jnp.einsum("te,de->td", grad_first_low, attn_full[3], preferred_element_type=full_type)
        .astype(low_type)
        .reshape(row_count, length, head_count, HEAD_DIM)
    )
    scores_again = (
        jnp.einsum("rshe,rkhe->rhsk", queries, comp_keys, preferred_element_type=full_type)
        * score_scale
    )
    probability = jnp.exp(jnp.where(allowed, scores_again - log_total, MASKED))
    probs_again = probability.astype(low_type)
    grad_probs = jnp.einsum(
        "rshe,rkhe->rhsk", grad_context, comp_values, preferred_element_type=full_type
    )
    row_delta = jnp.sum(probability * grad_probs, axis=-1, keepdims=True)
    grad_scores = (probability * (grad_probs - row_delta)).astype(low_type)
    grad_queries = (
        jnp.einsum("rhsk,rkhe->rshe", grad_scores, comp_keys, preferred_element_type=full_type)
        * score_scale
    ).astype(low_type)
    grad_comp_keys = (
        jnp.einsum("rhsk,rshe->rkhe", grad_scores, queries, preferred_element_type=full_type)
        * score_scale
    ).astype(low_type)
    grad_comp_values = jnp.einsum(
        "rhsk,rshe->rkhe", probs_again, grad_context, preferred_element_type=full_type
    ).astype(low_type)
    grad_comp = jnp.stack(
        [
            grad_comp_keys.reshape(row_count, -1, model_width),
            grad_comp_values.reshape(row_count, -1, model_width),
        ]
    )
    grad_kv = jnp.einsum(
        "rks,jrkd->jrsd", masked_proj, grad_comp, preferred_element_type=full_type
    ).astype(low_type)
    comp_grad = jnp.sum(
        jnp.where(
            member,
            jnp.einsum("jrkd,jrsd->rks", grad_comp, kv_low, preferred_element_type=full_type),
            0.0,
        ),
        axis=0,
    )
    grad_qkv = jnp.concatenate(
        [
            grad_queries.reshape(1, token_count, model_width),
            grad_kv.reshape(2, token_count, model_width),
        ]
    )
    qkv_grad = jnp.einsum(
        "td,jte->jde", flat_in, grad_qkv, preferred_element_type=full_type
    ).astype(low_type)
    input_grad = grad_first + jnp.einsum(
        "jte,jde->td", grad_qkv, attn_full[:3], preferred_element_type=full_type
    )
    attn_grad = jnp.concatenate([qkv_grad, out_proj_grad[None]])
    norm_grad = jnp.stack([gain_one, bias_one, gain_two, bias_two])
    grad_pack = jnp.concatenate(
        [
            attn_grad.reshape(attn_kinds, devices, attn_own, model_width)
            .transpose(1, 0, 2, 3)
            .reshape(devices, attn_kinds * attn_own, model_width),
            side_block(
                comp_grad.reshape(devices, compress_own, length),
                norm_grad.reshape(norm_kinds, devices, norm_own).transpose(1, 0, 2),
            ).astype(low_type),
        ],
        axis=1,
    )
    owned = exchange.scatter(grad_pack)
    attn_owned = owned[: attn_kinds * attn_own].reshape(attn_weight.shape)
    compress_owned = owned[attn_kinds * attn_own :, :length][:compress_own]
    norm_owned = owned[attn_kinds * attn_own :, length:][:norm_kinds, :norm_own]
    attn_first_new, attn_second_new, attn_direction = adaptive(attn_first, attn_second, attn_owned)
    up_first_new, up_second_new, up_direction = adaptive(up_first, up_second, up_owned)
    down_first_new, down_second_new, down_direction = adaptive(down_first, down_second, down_owned)
    compress_first_new, compress_second_new, compress_direction = adaptive(
        compress_first, compress_second, compress_owned
    )
    norm_first_new, norm_second_new, norm_direction = adaptive(norm_first, norm_second, norm_owned)
    attn_direction = attn_direction + DECAY * attn_weight
    up_direction = up_direction + DECAY * up_weight
    down_direction = down_direction + DECAY * down_weight
    compress_direction = compress_direction + DECAY * compress_weight
    squares = exchange.total(
        jnp.concatenate(
            [
                matrix_squares(attn_weight, up_weight, down_weight, compress_weight),
                matrix_squares(attn_direction, up_direction, down_direction, compress_direction),
            ]
        )
    )
    weight_norm, update_norm = jnp.sqrt(squares[:7]), jnp.sqrt(squares[7:])
    trust_ratio = weight_norm / (update_norm + EPSILON)
    attn_new = attn_weight - RATE * trust_ratio[:4].reshape(4, 1, 1) * attn_direction
    up_new = up_weight - RATE * trust_ratio[4] * up_direction
    down_new = down_weight - RATE * trust_ratio[5] * down_direction
    compress_new = compress_weight - RATE * trust_ratio[6] * compress_direction
    norm_new = norm_params - RATE * norm_direction
    norms = jnp.stack([weight_norm, update_norm])
    return (
        result,
        input_grad.reshape(row_count, length, model_width),
        attn_first_new,
        attn_second_new[:3],
        attn_second_new[3],
        attn_new,
        attn_new.astype(low_type),
        up_first_new,
        up_second_new,
        up_new,
        up_new.astype(low_type),
        down_first_new,
        down_second_new,
        down_new,
        down_new.astype(low_type),
        compress_first_new,
        compress_second_new,
        compress_new,
        compress_new.astype(low_type),
        norm_first_new,
        norm_second_new,
        norm_new,
        norms,
    )


def solution(mesh):
    rows, mid, flat = P(AXES, None), P(None, AXES, None), P(None, AXES)
    deep = P(AXES, None, None)

    def step(*args):
        return local(mesh.shape["dp"], mesh.shape["fsdp"], *args)

    return jax.shard_map(
        step,
        mesh=mesh,
        in_specs=(deep, rows, rows, deep) + (mid,) * 3 + (rows,) * 9 + (flat,) * 3,
        out_specs=(deep, deep, mid, mid, rows, mid, mid)
        + (rows,) * 12
        + (flat,) * 3
        + (P(),),
        check_vma=False,
    )
```

```python
import jax
import jax.numpy as jnp
from jax import lax
from jax.experimental import pallas as pl
from jax.experimental.pallas import tpu as pltpu
from jax.sharding import PartitionSpec as P

HEAD_DIM = 64
STEP = 10


BETA_ONE = 0.9
BETA_TWO = 0.999
EPSILON = 1e-06
DECAY = 0.01
RATE = 0.5
NORM_EPS = 1e-05
MASKED = -1e30

AXES = ("dp", "fsdp")
LOW = jnp.bfloat16
FULL = jnp.float32
ROOM = 56 * 1024 * 1024
LANES = 128


class Exchange:
    def __init__(self, dp, fsdp):
        self.count = dp * fsdp
        self.bits = self.count.bit_length() - 1
        self.x_bit = 1
        self.y_bit = fsdp.bit_length() - 1
        self.rest = [b for b in range(1, self.bits) if b not in (self.x_bit, self.y_bit)]
        self.index = lax.axis_index(AXES).astype(jnp.int32).reshape(1)

    def value(self, bit):
        return (self.index[0] >> bit) & 1

    def flip(self, array, even_bit, odd_bit):
        pairs = [(i, i ^ (1 << (odd_bit if i & 1 else even_bit))) for i in range(self.count)]
        return lax.ppermute(array, AXES, pairs)

    def by_core(self, even, odd):
        return jnp.where(self.value(0) == 0, even, odd)

    def joined(self, own, other, value, axis):
        return jnp.where(
            value == 0, jnp.stack([own, other], axis), jnp.stack([other, own], axis)
        )

    def groups(self, step, size):
        return [
            [base + low + step * i for i in range(size)]
            for base in range(0, self.count, step * size)
            for low in range(step)
        ]

    def pick(self, array, dim, value):
        return lax.dynamic_index_in_dim(array, value, dim, keepdims=False)


class Gather:
    def __init__(self, exchange, left, right):
        self.exchange = exchange
        self.left, self.right = left, right
        self.hops = ["pair"] + exchange.rest[::-1] + ["near", "last", "core"]
        self.place = 0

    def spread(self):
        ex = self.exchange
        self.hops = ["core"]
        self.have = lax.all_gather(
            self.have, AXES, axis=0, axis_index_groups=ex.groups(2, ex.count // 2), tiled=True
        )

    def begin(self):
        ex = self.exchange
        hop = self.hops[0]
        if hop == "pair":
            self.mine = ex.by_core(self.left, self.right)
            self.got = ex.flip(ex.by_core(self.right, self.left), 0, 0)
        elif hop == "near":
            self.got = ex.flip(self.have, ex.y_bit, ex.x_bit)
        elif hop == "last":
            self.got = ex.flip(self.have, ex.x_bit, ex.y_bit)
        elif hop == "core":
            self.got = ex.flip(self.have, 0, 0)
        else:
            self.got = ex.flip(self.have, hop, hop)

    def finish(self):
        ex = self.exchange
        hop = self.hops.pop(0)
        x_value, y_value = ex.value(ex.x_bit), ex.value(ex.y_bit)
        if hop == "pair":
            self.have = ex.joined(self.mine, self.got, ex.value(0), 0)
            self.have = self.have.reshape((-1,) + self.mine.shape[1:])
            self.block = self.have.shape
        elif hop == "near":
            self.have = ex.joined(self.have, self.got, ex.by_core(y_value, x_value), 0)
        elif hop == "last":
            have = ex.joined(self.have, self.got, ex.by_core(x_value, y_value), 0)
            wanted = list(range(ex.bits - 1, 0, -1))
            tail = [len(wanted), len(wanted) + 1]
            forms = []
            for first, second in ((ex.x_bit, ex.y_bit), (ex.y_bit, ex.x_bit)):
                now = [first, second] + ex.rest[::-1]
                forms.append(have.transpose([now.index(b) for b in wanted] + tail))
            self.have = ex.by_core(*forms).reshape((ex.count // 2) * self.block[0], self.block[1])
        elif hop == "core":
            self.halves = self.have, self.got
        else:
            self.have = ex.joined(self.have, self.got, ex.value(hop), self.place)
            self.place += 1

    def hop(self):
        self.begin()
        self.finish()


class Scatter:
    def __init__(self, exchange):
        self.exchange = exchange
        self.own, self.sent = [], []
        self.hops = ["near", "next"] + exchange.rest + ["last"]
        self.place = len(exchange.rest)

    def add(self, own, other):
        self.own.append(own)
        self.sent.append(self.exchange.flip(other, 0, 0))

    def merge(self):
        parts = [(a.astype(FULL) + b.astype(FULL)).astype(LOW) for a, b in zip(self.own, self.sent)]
        view = parts[0] if len(parts) == 1 else jnp.concatenate(parts, axis=1)
        self.have = view.reshape((2,) * (self.exchange.bits - 1) + (-1, view.shape[1]))

    def part(self, x_now, y_now):
        ex = self.exchange
        bits = list(range(ex.bits - 1, 0, -1))
        dim_x, dim_y = bits.index(ex.x_bit), bits.index(ex.y_bit)
        even = ex.pick(jnp.moveaxis(self.have, (dim_x, dim_y), (0, 1)), 0, x_now)
        odd = ex.pick(jnp.moveaxis(self.have, (dim_y, dim_x), (0, 1)), 0, y_now)
        return ex.by_core(even, odd)

    def begin(self):
        ex = self.exchange
        hop = self.hops[0]
        x_value, y_value = ex.value(ex.x_bit), ex.value(ex.y_bit)
        if hop == "near":
            self.sent_now = self.part(1 - x_value, 1 - y_value)
            self.got = ex.flip(self.sent_now, ex.x_bit, ex.y_bit)
        elif hop == "next":
            value = ex.by_core(y_value, x_value)
            self.sent_now = ex.pick(self.have, 0, 1 - value).astype(LOW)
            self.got = ex.flip(self.sent_now, ex.y_bit, ex.x_bit)
        elif hop == "last":
            view = self.have.reshape(2, -1, self.have.shape[-1])
            self.sent_now = ex.pick(view, 0, 1 - ex.value(0)).astype(LOW)
            self.got = ex.flip(self.sent_now, 0, 0)
        else:
            self.place -= 1
            self.sent_now = ex.pick(self.have, self.place, 1 - ex.value(hop)).astype(LOW)
            self.got = ex.flip(self.sent_now, hop, hop)

    def finish(self):
        ex = self.exchange
        hop = self.hops.pop(0)
        x_value, y_value = ex.value(ex.x_bit), ex.value(ex.y_bit)
        if hop == "last":
            self.mine = ex.pick(self.have.reshape(2, -1, self.have.shape[-1]), 0, ex.value(0))
            return
        got = self.got.astype(FULL)
        if hop == "near":
            self.have = self.part(x_value, y_value).astype(FULL) + got
        elif hop == "next":
            self.have = ex.pick(self.have, 0, ex.by_core(y_value, x_value)) + got
        else:
            self.have = ex.pick(self.have, self.place, ex.value(hop)) + got

    def hop(self):
        self.begin()
        self.finish()


class Reduce:
    def __init__(self, exchange):
        self.exchange = exchange
        self.own, self.sent, self.planes = [], [], []
        self.far = 4
        self.near = exchange.count // 2 // self.far
        self.hops = [exchange.bits - 2, exchange.bits - 1, "last"]

    def add(self, own, other):
        self.own.append(own)
        self.sent.append(self.exchange.flip(other, 0, 0))

    def merge(self):
        parts = [a.astype(FULL) + b.astype(FULL) for a, b in zip(self.own, self.sent)]
        self.own, self.sent = [], []
        view = parts[0] if len(parts) == 1 else jnp.concatenate(parts, axis=1)
        rows, width = view.shape
        view = view.astype(LOW).reshape(self.far, self.near, -1, width).transpose(1, 0, 2, 3)
        self.merged = view.reshape(rows, width)

    def plane(self):
        groups = self.exchange.groups(2, self.near)
        self.planes.append(
            lax.psum_scatter(self.merged, AXES, scatter_dimension=0, axis_index_groups=groups, tiled=True)
        )

    def begin(self):
        ex = self.exchange
        hop = self.hops[0]
        if self.planes:
            views = [p.reshape(2, 2, p.shape[0] // 4, p.shape[1]) for p in self.planes]
            self.have = views[0] if len(views) == 1 else jnp.concatenate(views, axis=3)
            self.planes = []
        if hop == "last":
            view = self.have.reshape(2, -1, self.have.shape[-1])
            self.sent_now = ex.pick(view, 0, 1 - ex.value(0)).astype(LOW)
            self.mine = ex.pick(view, 0, ex.value(0))
            self.got = ex.flip(self.sent_now, 0, 0)
        else:
            self.sent_now = ex.pick(self.have, len(self.hops) - 2, 1 - ex.value(hop)).astype(LOW)
            self.got = ex.flip(self.sent_now, hop, hop)

    def finish(self):
        ex = self.exchange
        hop = self.hops.pop(0)
        if hop != "last":
            self.have = ex.pick(self.have, len(self.hops) - 1, ex.value(hop)).astype(FULL) + self.got.astype(FULL)


def matmul(left, right, left_dim=1, right_dim=0):
    return lax.dot_general(
        left, right, (((left_dim,), (right_dim,)), ((), ())), preferred_element_type=FULL
    )


def cost(flops, moved, transcendentals=0):
    return pl.CostEstimate(flops=flops, bytes_accessed=moved, transcendentals=transcendentals)


def whole(shape):
    return pl.BlockSpec(shape, lambda *_: (0,) * len(shape), pipeline_mode=pl.Buffered(1))


def kept_block(shape):
    return pl.BlockSpec(shape, lambda *_: (0,) * len(shape))


def anywhere():
    return pl.BlockSpec(memory_space=pl.ANY)


def call(exchange, name, body, grid, ins, outs, scratch=(), work=None, onto=(), later_than=()):
    count_in, count_gone = len(ins), len(onto) + len(later_than)

    def kernel(index_ref, *refs):
        given = refs[:count_in]
        rest = refs[count_in + count_gone :]
        token_ref, results = rest[0], rest[1:]
        token_ref[0] = index_ref[0]
        body(index_ref, *given, *results)

    results = pl.pallas_call(
        kernel,
        grid_spec=pltpu.PrefetchScalarGridSpec(
            num_scalar_prefetch=1,
            grid=grid,
            in_specs=[spec for _, spec in ins] + [anywhere()] * count_gone,
            out_specs=[pl.BlockSpec(memory_space=pltpu.SMEM)] + [spec for _, _, spec in outs],
            scratch_shapes=list(scratch),
        ),
        out_shape=[jax.ShapeDtypeStruct((1,), jnp.int32)] + [jax.ShapeDtypeStruct(s, t) for s, t, _ in outs],
        input_output_aliases={1 + count_in + i: 1 + i for i in range(len(onto))},
        compiler_params=pltpu.CompilerParams(vmem_limit_bytes=ROOM),
        cost_estimate=work,
        name=name,
    )(exchange.index, *[a for a, _ in ins], *onto, *later_than)
    exchange.index = results[0]
    return results[1:]


def gate(exchange, *arrays):
    call(exchange, "gate", lambda index_ref: None, (1,), [], [], work=cost(1, 1), later_than=arrays)


def hold(exchange, array):
    return call(
        exchange, "hold", lambda index_ref, array_ref: None, (1,), [], [(array.shape, array.dtype, anywhere())],
        work=cost(1, 1), onto=[array],
    )[0]


def norm_stats(mixed):
    average = jnp.mean(mixed, axis=-1, keepdims=True)
    centered = mixed - average
    inv_std = lax.rsqrt(jnp.mean(centered * centered, axis=-1, keepdims=True) + NORM_EPS)
    return centered * inv_std, inv_std


def norm_pull(grad_out, normed, inv_std, gain):
    scaled = grad_out * gain
    return inv_std * (
        scaled
        - jnp.mean(scaled, axis=-1, keepdims=True)
        - normed * jnp.mean(scaled * normed, axis=-1, keepdims=True)
    )


def head_lanes(pair, head):
    lane = lax.broadcasted_iota(jnp.int32, pair.shape, 1)
    mine = (lane < HEAD_DIM) if head % 2 == 0 else (lane >= HEAD_DIM)
    return jnp.where(mine, pair, jnp.zeros((), pair.dtype))


def column_copies(core, own, other, first, target, sems):
    half = target.shape[1] // 2
    copies = []
    for i, (source, place) in enumerate(((own, core), (other, 1 - core))):
        at = pl.multiple_of(place * half, LANES)
        copies.append(
            pltpu.make_async_copy(
                source.at[:, first : first + half], target.at[:, pl.ds(at, half)], sems.at[i]
            )
        )
    return copies


def attend_kernel(index_ref, own_ref, other_ref, x_ref, seg_ref, comp_ref, proj_ref,
                  q_ref, k_ref, v_ref, ck_ref, cv_ref, lse_ref, ctx_ref, ctx_t, weights, sems):
    width = x_ref.shape[2]
    heads = width // HEAD_DIM
    copies = [
        column_copies(index_ref[0] & 1, own_ref, other_ref, kind * (width // 2), weights.at[kind], sems.at[kind])
        for kind in range(3)
    ]
    first = pl.program_id(0) == 0

    @pl.when(first)
    def _():
        for copy in sum(copies, []):
            copy.start()

    def arrive(kind):
        @pl.when(first)
        def _():
            for copy in copies[kind]:
                copy.wait()

    x = x_ref[0]
    arrive(0)
    q_ref[0] = matmul(x, weights[0]).astype(LOW)
    arrive(1)
    k_ref[0] = matmul(x, weights[1]).astype(LOW)
    arrive(2)
    v_ref[0] = matmul(x, weights[2]).astype(LOW)
    member = comp_ref[0] == seg_ref[0]
    masked = jnp.where(member, proj_ref[...], jnp.zeros((), LOW))
    ck_ref[0] = (matmul(masked, k_ref[0])).astype(LOW)
    cv = matmul(masked, v_ref[0])
    cv_ref[0] = cv.astype(LOW)
    cv_t = cv.T.astype(LOW)
    for head in range(heads):
        lanes = slice(head // 2 * LANES, head // 2 * LANES + LANES)
        rows = slice(head * HEAD_DIM, (head + 1) * HEAD_DIM)
        keys = head_lanes(ck_ref[0, :, lanes], head) * (HEAD_DIM ** -0.5)
        scores = matmul(keys.astype(LOW), q_ref[0, :, lanes], 1, 1)
        scores = jnp.where(member, scores, MASKED)
        highest = jnp.max(scores, axis=0, keepdims=True)
        weight = jnp.exp(scores - highest)
        total = jnp.sum(weight, axis=0, keepdims=True)
        lse_ref[0, head : head + 1, :] = highest + jnp.log(total)
        probs = (weight * (1.0 / total)).astype(LOW)
        ctx_t[rows, :] = matmul(cv_t[rows, :], probs)
    ctx_ref[0] = ctx_t[...].T.astype(LOW)


def attend(exchange, halves, x, seg, comp, proj, later_than):
    rows, length, width = x.shape
    slots = comp.shape[1]
    heads = width // HEAD_DIM

    def at(*shape):
        return pl.BlockSpec((1,) + shape, lambda i, _: (i, 0, 0))

    tokens = ((rows, length, width), LOW, at(length, width))
    comps = ((rows, slots, width), LOW, at(slots, width))
    flops = rows * (length * width * (2 * 3 * width + 4 * slots * 4) + slots * length * width * 4)
    return call(
        exchange, "attend", attend_kernel, (rows,),
        [(halves[0], anywhere()), (halves[1], anywhere()), (x, at(length, width)), (seg[:, None, :], at(1, length)),
         (comp[:, :, None], at(slots, 1)), (proj, whole((slots, length)))],
        [tokens] * 3 + [comps] * 2 + [((rows, heads, length), FULL, at(heads, length)), tokens],
        [pltpu.VMEM((width, length), FULL), pltpu.VMEM((3, width, width), LOW), pltpu.SemaphoreType.DMA((3, 2))],
        cost(flops, 20 * 10**6, rows * heads * slots * length), (), later_than,
    )


def mix_kernel(index_ref, own_ref, other_ref, x_ref, ctx_ref, gains_ref, normed_ref, inv_ref, low_ref, weight, sems):
    @pl.when(pl.program_id(0) == 0)
    def _():
        first = own_ref.shape[1] - weight.shape[1] // 2
        copies = column_copies(index_ref[0] & 1, own_ref, other_ref, first, weight, sems)
        for copy in copies:
            copy.start()
        for copy in copies:
            copy.wait()

    mixed = x_ref[...].astype(FULL) + matmul(ctx_ref[...], weight[...])
    normed, inv_std = norm_stats(mixed)
    normed_ref[...] = normed
    inv_ref[...] = inv_std
    low_ref[...] = (normed * gains_ref[0:1] + gains_ref[1:2]).astype(LOW)


def mix(exchange, halves, x, ctx, gains, later_than, tile=256):
    tokens, width = x.shape

    def some(n):
        return pl.BlockSpec((tile, n), lambda i, _: (i, 0))

    return call(
        exchange, "mix", mix_kernel, (tokens // tile,),
        [(halves[0], anywhere()), (halves[1], anywhere()), (x, some(width)), (ctx, some(width)),
         (gains, whole(gains.shape))],
        [((tokens, width), FULL, some(width)), ((tokens, 1), FULL, some(1)), ((tokens, width), LOW, some(width))],
        [pltpu.VMEM((width, width), LOW), pltpu.SemaphoreType.DMA((2,))],
        cost(2 * tokens * width * width, 10 * 10**6), (), later_than,
    )


def gelu_pair(h):
    below = 1.0 + (0.3275911 * 0.5 ** 0.5) * jnp.abs(h)
    t = pl.reciprocal(below, approx=True)
    t = t * (2.0 - below * t)
    bell = jnp.exp(h * h * -0.5)
    poly = 0.127414796 + t * (-0.142248368 + t * (0.7107068705 + t * (-0.7265760135 + t * 0.5307027145)))
    tail = poly * (t * bell)
    cdf = jnp.where(h >= 0, 1.0 - tail, tail)
    return h * cdf, cdf + h * (bell * 0.3989422804014327)


def up_kernel(index_ref, f_ref, own_ref, other_ref, act_ref, slope_ref):
    def body(w_ref):
        value, slope = gelu_pair(matmul(f_ref[...], w_ref[...]))
        act_ref[...] = value.astype(LOW)
        slope_ref[...] = slope

    own = pl.program_id(0) < pl.num_programs(0) // 2
    pl.when(own)(lambda: body(own_ref))
    pl.when(jnp.logical_not(own))(lambda: body(other_ref))


def up_part(exchange, f, halves, ff, later_than, tile=768):
    tokens, width = f.shape
    half = ff // tile // 2

    def place(j, index_ref):
        core = index_ref[0] & 1
        return (0, jnp.where(j < half, core * half + j, (1 - core) * half + j - half))

    out = pl.BlockSpec((tokens, tile), place)
    return call(
        exchange, "up_part", up_kernel, (2 * half,),
        [(f, whole((tokens, width))),
         (halves[0], pl.BlockSpec((width, tile), lambda j, _: (0, jnp.minimum(j, half - 1)))),
         (halves[1], pl.BlockSpec((width, tile), lambda j, _: (0, jnp.maximum(j - half, 0))))],
        [((tokens, ff), LOW, out), ((tokens, ff), FULL, out)],
        (), cost(2 * tokens * width * ff, 26 * 10**6, tokens * ff), (), later_than,
    )


def down_kernel(index_ref, own_ref, other_ref, act_ref, normed_ref, og_ref, gains_ref,
                out_ref, g_ref, low_ref, sums_ref, weight, sems):
    @pl.when(pl.program_id(0) == 0)
    def _():
        sums_ref[...] = jnp.zeros_like(sums_ref)
        copies = column_copies(index_ref[0] & 1, own_ref, other_ref, 0, weight, sems)
        for copy in copies:
            copy.start()
        for copy in copies:
            copy.wait()

    first = normed_ref[...] * gains_ref[0:1] + gains_ref[1:2]
    normed, inv_std = norm_stats(first + matmul(act_ref[...], weight[...]))
    out_ref[...] = (normed * gains_ref[2:3] + gains_ref[3:4]).astype(LOW)
    top = og_ref[...].astype(FULL)
    grad = norm_pull(top, normed, inv_std, gains_ref[2:3])
    g_ref[...] = grad
    low_ref[...] = grad.astype(LOW)
    sums_ref[0:1] += jnp.sum(top * normed, axis=0, keepdims=True)
    sums_ref[1:2] += jnp.sum(top, axis=0, keepdims=True)


def down_part(exchange, halves, act, normed, og, gains, later_than, tile=256):
    tokens, ff = act.shape
    width = normed.shape[1]

    def some(n):
        return pl.BlockSpec((tile, n), lambda i, _: (i, 0))

    return call(
        exchange, "down_part", down_kernel, (tokens // tile,),
        [(halves[0], anywhere()), (halves[1], anywhere()), (act, some(ff)), (normed, some(width)), (og, some(width)),
         (gains, whole(gains.shape))],
        [((tokens, width), LOW, some(width)), ((tokens, width), FULL, some(width)), ((tokens, width), LOW, some(width)),
         ((8, width), FULL, kept_block((8, width)))],
        [pltpu.VMEM((ff, width), LOW), pltpu.SemaphoreType.DMA((2,))],
        cost(2 * tokens * width * ff, 23 * 10**6), (), later_than,
    )


def split_columns(index_ref, total, own_ref, other_ref):
    half = total.shape[1] // 2
    left, right = total[:, :half].astype(LOW), total[:, half:].astype(LOW)
    even = (index_ref[0] & 1) == 0
    own_ref[...] = jnp.where(even, left, right)
    other_ref[...] = jnp.where(even, right, left)


def outer_kernel(index_ref, left_ref, *refs):
    *right_refs, own_ref, other_ref = refs
    for kind, right_ref in enumerate(right_refs):

        @pl.when(pl.program_id(0) == kind)
        def _(right_ref=right_ref):
            split_columns(index_ref, matmul(left_ref[...], right_ref[...], 0, 0), own_ref, other_ref)


def outer_part(exchange, left, rights, name, later_than):
    tokens, depth = left.shape
    width = rights[0].shape[1]
    half = ((depth, len(rights) * width // 2), LOW, pl.BlockSpec((depth, width // 2), lambda j, _: (0, j)))
    return call(
        exchange, name, outer_kernel, (len(rights),),
        [(left, whole((tokens, depth)))] + [(r, whole((tokens, width))) for r in rights],
        [half] * 2, (), cost(2 * tokens * depth * width * len(rights), 9 * 10**6), (), later_than,
    )


def down_grad_kernel(index_ref, act_ref, g_ref, own_ref, other_ref):
    split_columns(index_ref, matmul(act_ref[...], g_ref[...], 0, 0), own_ref, other_ref)


def down_grad_part(exchange, act, g, later_than, tile=768):
    tokens, ff = act.shape
    width = g.shape[1]
    half = ((ff, width // 2), LOW, pl.BlockSpec((tile, width // 2), lambda j, _: (j, 0)))
    return call(
        exchange, "down_grad_part", down_grad_kernel, (ff // tile,),
        [(act, pl.BlockSpec((tokens, tile), lambda j, _: (0, j))), (g, whole((tokens, width)))],
        [half] * 2, (), cost(2 * tokens * width * ff, 13 * 10**6), (), later_than,
    )


def ff_back_kernel(index_ref, down_own, down_other, up_own, up_other, slope_ref, low_ref, f_ref, start_ref, normed_ref,
                   inv_ref, gains_ref, *refs):
    *grad_refs, g_one_ref, g_one_low_ref, sums_ref, total, w_down, sems = refs
    step = pl.program_id(0)
    steps = pl.num_programs(0)
    half = steps // 2
    core = index_ref[0] & 1
    tile = slope_ref.shape[1]

    def copies(at):
        place = jnp.where(at < half, (1 - core) * half + at, core * half + at - half)
        rows = pl.ds(pl.multiple_of(place * tile, tile), tile)
        return column_copies(core, down_own.at[rows], down_other.at[rows], 0, w_down.at[at % 2], sems.at[at % 2])

    @pl.when(step == 0)
    def _():
        for copy in copies(step):
            copy.start()
        total[...] = start_ref[...]

    @pl.when(step < steps - 1)
    def _():
        for copy in copies(step + 1):
            copy.start()

    for copy in copies(step):
        copy.wait()

    back = (matmul(low_ref[...], w_down[step % 2], 1, 1) * slope_ref[...]).astype(LOW)
    grads = matmul(f_ref[...], back, 0, 0).astype(LOW)
    for at, grad_ref in enumerate(grad_refs):

        @pl.when(step == at)
        def _(grad_ref=grad_ref):
            grad_ref[...] = grads

    def add(up_ref):
        total[...] += matmul(back, up_ref[...], 1, 1)

    pl.when(step < half)(lambda: add(up_other))
    pl.when(step >= half)(lambda: add(up_own))

    @pl.when(step == steps - 1)
    def _():
        top = total[...]
        normed = normed_ref[...]
        grad = norm_pull(top, normed, inv_ref[...], gains_ref[0:1])
        g_one_ref[...] = grad
        g_one_low_ref[...] = grad.astype(LOW)
        sums_ref[...] = jnp.zeros_like(sums_ref)
        sums_ref[0:1] = jnp.sum(top * normed, axis=0, keepdims=True)
        sums_ref[1:2] = jnp.sum(top, axis=0, keepdims=True)


def ff_back(exchange, down, up, slope, low, f, start, normed, inv, gains, later_than, tile=768):
    tokens, ff = slope.shape
    width = f.shape[1]
    steps = ff // tile
    half = steps // 2

    def place(j, index_ref):
        core = index_ref[0] & 1
        return (0, jnp.where(j < half, (1 - core) * half + j, core * half + j - half))

    full = whole((tokens, width))
    result = kept_block((tokens, width))
    return call(
        exchange, "ff_back", ff_back_kernel, (steps,),
        [(down[0], anywhere()), (down[1], anywhere()),
         (up[0], pl.BlockSpec((width, tile), lambda j, _: (0, jnp.maximum(j - half, 0)))),
         (up[1], pl.BlockSpec((width, tile), lambda j, _: (0, jnp.minimum(j, half - 1)))),
         (slope, pl.BlockSpec((tokens, tile), place)),
         (low, full), (f, full), (start, full), (normed, full), (inv, whole(inv.shape)), (gains, whole(gains.shape))],
        [((width, tile), LOW, whole((width, tile)))] * steps
        + [((tokens, width), FULL, result), ((tokens, width), LOW, result), ((8, width), FULL, kept_block((8, width)))],
        [pltpu.VMEM((tokens, width), FULL), pltpu.VMEM((2, tile, width), LOW), pltpu.SemaphoreType.DMA((2, 2))],
        cost(6 * tokens * width * ff, 40 * 10**6), (), later_than,
    )


def attend_back_kernel(index_ref, own_ref, other_ref, g_ref, q_ref, k_ref, v_ref, ck_ref, cv_ref, lse_ref,
                       seg_ref, comp_ref, proj_ref,
                       gq_ref, gk_ref, gv_ref, grad_ref, gctx, gq_t, gck, gcv, weight, sems):
    width = q_ref.shape[2]
    heads = width // HEAD_DIM
    scale = HEAD_DIM ** -0.5

    @pl.when(pl.program_id(0) == 0)
    def _():
        copies = column_copies(
            index_ref[0] & 1, own_ref, other_ref, own_ref.shape[1] - width // 2, weight, sems
        )
        for copy in copies:
            copy.start()
        for copy in copies:
            copy.wait()

    gctx[...] = matmul(g_ref[0], weight[...], 1, 1).astype(LOW)
    member = comp_ref[0] == seg_ref[0]
    ck_t = ck_ref[0].astype(FULL).T.astype(LOW)
    for pair in range(heads // 2):
        lanes = slice(pair * LANES, pair * LANES + LANES)
        queries, grads = q_ref[0, :, lanes], gctx[:, lanes]
        key_parts, value_parts = [], []
        for head in (2 * pair, 2 * pair + 1):
            rows = slice(head * HEAD_DIM, (head + 1) * HEAD_DIM)
            keys = head_lanes(ck_ref[0, :, lanes], head) * scale
            scores = matmul(keys.astype(LOW), queries, 1, 1)
            probs = jnp.exp(jnp.where(member, scores - lse_ref[0, head : head + 1, :], MASKED))
            grad_probs = matmul(head_lanes(cv_ref[0, :, lanes], head), grads, 1, 1)
            delta = jnp.sum(probs * grad_probs, axis=0, keepdims=True)
            grad_scores = (probs * (grad_probs - delta)).astype(LOW)
            gq_t[rows, :] = matmul(ck_t[rows, :], grad_scores) * scale
            key_parts.append(matmul(grad_scores, queries))
            value_parts.append(matmul(probs.astype(LOW), grads))
        lane = lax.broadcasted_iota(jnp.int32, key_parts[0].shape, 1) < HEAD_DIM
        gck[:, lanes] = (jnp.where(lane, *key_parts) * scale).astype(LOW)
        gcv[:, lanes] = jnp.where(lane, *value_parts).astype(LOW)
    gq_ref[...] = gq_t[...].T.astype(LOW)
    masked = jnp.where(member, proj_ref[...], jnp.zeros((), LOW))
    gk_ref[...] = matmul(masked, gck[...], 0, 0).astype(LOW)
    gv_ref[...] = matmul(masked, gcv[...], 0, 0).astype(LOW)
    part = matmul(gck[...], k_ref[0], 1, 1) + matmul(gcv[...], v_ref[0], 1, 1)
    part = jnp.where(member, part, 0.0)

    @pl.when(pl.program_id(0) == 0)
    def _():
        grad_ref[...] = part

    @pl.when(pl.program_id(0) > 0)
    def _():
        grad_ref[...] += part


def attend_back(exchange, halves, g, kept, seg, comp, proj, later_than):
    q, k, v, ck, cv, lse = kept
    rows, length, width = q.shape
    slots = comp.shape[1]
    heads = width // HEAD_DIM

    def at(*shape):
        return pl.BlockSpec((1,) + shape, lambda i, _: (i, 0, 0))

    tokens = ((rows * length, width), LOW, pl.BlockSpec((length, width), lambda i, _: (i, 0)))
    flops = rows * length * width * (2 * width + 4 * slots * 10)
    return call(
        exchange, "attend_back", attend_back_kernel, (rows,),
        [(halves[0], anywhere()), (halves[1], anywhere())] + [(a, at(length, width)) for a in (g, q, k, v)]
        + [(a, at(slots, width)) for a in (ck, cv)]
        + [(lse, at(heads, length)), (seg[:, None, :], at(1, length)), (comp[:, :, None], at(slots, 1)),
           (proj, whole((slots, length)))],
        [tokens] * 3 + [((slots, length), FULL, kept_block((slots, length)))],
        [pltpu.VMEM((length, width), LOW), pltpu.VMEM((width, length), FULL),
         pltpu.VMEM((slots, width), LOW), pltpu.VMEM((slots, width), LOW),
         pltpu.VMEM((width, width), LOW), pltpu.SemaphoreType.DMA((2,))],
        cost(flops, 15 * 10**6, rows * heads * slots * length), (), later_than,
    )


def input_kernel(index_ref, own_ref, other_ref, g_ref, gq_ref, gk_ref, gv_ref, out_ref, weights, sems):
    width = g_ref.shape[1]

    @pl.when(pl.program_id(0) == 0)
    def _():
        copies = []
        for kind in range(3):
            copies += column_copies(
                index_ref[0] & 1, own_ref, other_ref, kind * (width // 2), weights.at[kind], sems.at[kind]
            )
        for copy in copies:
            copy.start()
        for copy in copies:
            copy.wait()

    out_ref[...] = (
        g_ref[...]
        + matmul(gq_ref[...], weights[0], 1, 1)
        + matmul(gk_ref[...], weights[1], 1, 1)
        + matmul(gv_ref[...], weights[2], 1, 1)
    )


def input_part(exchange, halves, g, gq, gk, gv, later_than, tile=256):
    tokens, width = g.shape
    some = pl.BlockSpec((tile, width), lambda i, _: (i, 0))
    return call(
        exchange, "input_part", input_kernel, (tokens // tile,),
        [(halves[0], anywhere()), (halves[1], anywhere())] + [(a, some) for a in (g, gq, gk, gv)],
        [((tokens, width), FULL, some)],
        [pltpu.VMEM((3, width, width), LOW), pltpu.SemaphoreType.DMA((3, 2))],
        cost(6 * tokens * width * width, 15 * 10**6), (), later_than,
    )[0]


def adaptive(first, second, grad):
    first_new = BETA_ONE * first + (1.0 - BETA_ONE) * grad
    second_new = BETA_TWO * second + (1.0 - BETA_TWO) * grad * grad
    direction = (
        first_new
        / (1.0 - BETA_ONE**STEP)
        / (jnp.sqrt(second_new / (1.0 - BETA_TWO**STEP)) + EPSILON)
    )
    return (first_new, second_new, direction)


def pack_attn_kernel(index_ref, weight_ref, comp_ref, norm_ref, left_ref, right_ref, side):
    kinds = weight_ref.shape[0] - 1
    half = weight_ref.shape[2] // 2
    rows, length = comp_ref.shape
    pieces = length // side.shape[1]
    own, own_columns = norm_ref.shape
    side[...] = jnp.zeros_like(side)
    for i in range(pieces):
        side[i * rows : (i + 1) * rows, :] = comp_ref[:, i * side.shape[1] : (i + 1) * side.shape[1]]
    side[pieces * rows : pieces * rows + own, :own_columns] = norm_ref[...]
    for i, ref in enumerate((left_ref, right_ref)):
        for kind in range(kinds):
            ref[:, kind * half : (kind + 1) * half] = weight_ref[kind, :, i * half : (i + 1) * half].astype(LOW)
        middle = side.shape[1] // 2
        ref[:, kinds * half :] = side[:, i * middle : (i + 1) * middle].astype(LOW)


def pack_up_kernel(index_ref, weight_ref, out_ref, left_ref, right_ref):
    split, half = weight_ref.shape[1] // 2, out_ref.shape[2] // 2
    for i, ref in enumerate((left_ref, right_ref)):
        ref[:, :split] = weight_ref[:, i * split : (i + 1) * split].astype(LOW)
        ref[:, split:] = out_ref[0, :, i * half : (i + 1) * half].astype(LOW)


def pack_down_kernel(index_ref, weight_ref, left_ref, right_ref):
    half = left_ref.shape[1]
    left_ref[...] = weight_ref[:, :half].astype(LOW)
    right_ref[...] = weight_ref[:, half:].astype(LOW)


def squares_row(array):
    total = jnp.sum(jnp.sum(array * array, axis=0, keepdims=True), axis=1, keepdims=True)
    return jnp.broadcast_to(total, (1, LANES))


def step_matrix(weight, first, second, grad, first_ref, second_ref, direction_ref, sums_ref, row):
    first_new, second_new, direction = adaptive(first, second, grad)
    direction = direction + DECAY * weight
    first_ref[...] = first_new
    second_ref[...] = second_new
    direction_ref[...] = direction
    sums_ref[row : row + 1] = squares_row(weight)
    sums_ref[row + 8 : row + 9] = squares_row(direction)


def joined_halves(index_ref, mine, got):
    even = (index_ref[0] & 1) == 0
    return jnp.concatenate([jnp.where(even, mine, got), jnp.where(even, got, mine)], axis=1)


def down_step_kernel(index_ref, mine_ref, got_ref, weight_ref, first_ref, second_ref,
                     first_new, second_new, direction, sums_ref):
    sums_ref[...] = jnp.zeros_like(sums_ref)
    grad = joined_halves(index_ref, mine_ref[...].astype(FULL), got_ref[...].astype(FULL))
    step_matrix(weight_ref[...], first_ref[...], second_ref[...], grad, first_new, second_new, direction, sums_ref, 5)


def up_step_kernel(index_ref, mine_ref, got_ref, weight_ref, first_ref, second_ref, out_weight, out_first, out_second,
                   first_new, second_new, direction, out_first_new, out_second_new, out_direction, sums_ref):
    sums_ref[...] = jnp.zeros_like(sums_ref)
    split = weight_ref.shape[1] // 2
    mine, got = mine_ref[...].astype(FULL), got_ref[...].astype(FULL)
    grad = joined_halves(index_ref, mine[:, :split], got[:, :split])
    step_matrix(weight_ref[...], first_ref[...], second_ref[...], grad, first_new, second_new, direction, sums_ref, 4)
    grad = joined_halves(index_ref, mine[:, split:], got[:, split:])
    step_matrix(out_weight[0], out_first[0], out_second[0], grad,
                out_first_new, out_second_new, out_direction, sums_ref, 3)


def attn_step_kernel(index_ref, mine_ref, got_ref, weight_ref, first_ref, second_ref,
                     comp_weight, comp_first, comp_second, norm_weight, norm_first, norm_second,
                     out_first_new, up_sums, down_sums,
                     first_new, second_new, direction, comp_first_new, comp_second_new, comp_direction,
                     norm_first_new, norm_second_new, norm_new, sent_ref, sums_ref):
    sums_ref[...] = up_sums[...] + down_sums[...]
    kinds = weight_ref.shape[0] - 1
    width = weight_ref.shape[2]
    half = width // 2
    mine, got = mine_ref[...].astype(FULL), got_ref[...].astype(FULL)
    for kind in range(kinds):
        columns = slice(kind * half, (kind + 1) * half)
        grad = joined_halves(index_ref, mine[:, columns], got[:, columns])
        step_matrix(weight_ref[kind], first_ref[kind], second_ref[kind], grad,
                    first_new.at[kind], second_new.at[kind], direction.at[kind], sums_ref, kind)
    first_new[kinds] = out_first_new[...]
    side = joined_halves(index_ref, mine[:, kinds * half :], got[:, kinds * half :])
    rows, length = comp_weight.shape
    pieces = length // side.shape[1]
    grad = jnp.concatenate([side[i * rows : (i + 1) * rows] for i in range(pieces)], axis=1)
    step_matrix(comp_weight[...], comp_first[...], comp_second[...], grad,
                comp_first_new, comp_second_new, comp_direction, sums_ref, 6)
    own, own_columns = norm_weight.shape
    grad = side[pieces * rows : pieces * rows + own, :own_columns]
    new, newer, way = adaptive(norm_first[...], norm_second[...], grad)
    norm_first_new[...] = new
    norm_second_new[...] = newer
    norm_new[...] = norm_weight[...] - RATE * way
    sent_ref[...] = jnp.broadcast_to(sums_ref[...][None], sent_ref.shape)


def finish_kernel(index_ref, got_ref, weight_ref, direction_ref, out_direction, up_weight, up_direction,
                  down_weight, down_direction, comp_weight, comp_direction,
                  attn_new, attn_copy, up_new, up_copy, down_new, down_copy, comp_new, comp_copy, norms_ref):
    totals = jnp.sqrt(jnp.sum(got_ref[...], axis=0))
    lane = lax.broadcasted_iota(jnp.int32, (1, LANES), 1)
    count = norms_ref.shape[1]
    for i in range(2):
        row = sum(jnp.where(lane == m, totals[8 * i + m : 8 * i + m + 1], 0.0) for m in range(count))
        norms_ref[i : i + 1, :] = row[:, :count]
    ratio = totals[:8] / (totals[8:] + EPSILON)

    def move(weight, direction, matrix, new_ref, copy_ref):
        new = weight - RATE * ratio[matrix : matrix + 1, :1] * direction
        new_ref[...] = new
        copy_ref[...] = new.astype(LOW)

    for kind in range(4):
        way = direction_ref[kind] if kind < 3 else out_direction[...]
        move(weight_ref[kind], way, kind, attn_new.at[kind], attn_copy.at[kind])
    move(up_weight[...], up_direction[...], 4, up_new, up_copy)
    move(down_weight[...], down_direction[...], 5, down_new, down_copy)
    move(comp_weight[...], comp_direction[...], 6, comp_new, comp_copy)


def elementwise(exchange, name, body, ins, shapes, later_than=(), scratch=()):
    pairs = []
    for a in ins:
        if isinstance(a, tuple):
            shape, kind = (1,) + a[0].shape[1:], a[1]
            pairs.append((a[0], pl.BlockSpec(shape, lambda *_, kind=kind: (kind, 0, 0))))
        else:
            pairs.append((a, whole(a.shape)))
    return call(
        exchange, name, body, (1,), pairs, [(shape, kind, whole(shape)) for shape, kind in shapes], scratch,
        cost(10**6, sum(a.size * 4 for a, _ in pairs)), (), later_than,
    )


def local(
    dp,
    fsdp,
    inputs,
    segment_ids,
    compressed_segment,
    out_grad,
    attn_weight,
    attn_first,
    attn_second,
    up_weight,
    up_first,
    up_second,
    down_weight,
    down_first,
    down_second,
    compress_weight,
    compress_first,
    compress_second,
    norm_params,
    norm_first,
    norm_second,
):
    exchange = Exchange(dp, fsdp)
    devices = dp * fsdp
    row_count, length, model_width = inputs.shape
    half_width = model_width // 2
    token_count = row_count * length
    norm_kinds, norm_own = norm_params.shape
    attn_kinds, attn_own, _ = attn_weight.shape
    compress_own = compress_weight.shape[0]
    pieces = 2 if 2 * compress_own + norm_kinds <= attn_own else 1
    side_width = length // pieces

    def side_rows(compress_part, norm_part):
        none = [(0, 0)] * (compress_part.ndim - 2)
        spare = attn_own - pieces * compress_own - norm_kinds
        norm_part = jnp.pad(norm_part, none + [(0, spare), (0, side_width - norm_own)])
        parts = [compress_part[..., i * side_width : (i + 1) * side_width] for i in range(pieces)]
        return jnp.concatenate(parts + [norm_part], axis=-2)

    def halves(array):
        middle = array.shape[-1] // 2
        return array[..., :middle], array[..., middle:]

    flat_in = inputs.reshape(token_count, model_width)
    ff = up_weight.shape[1]
    out_kind = attn_kinds - 1
    out_at = [(a, out_kind) for a in (attn_weight, attn_first, attn_second)]
    attn = Gather(
        exchange,
        *elementwise(
            exchange, "pack_attn", pack_attn_kernel, [attn_weight, compress_weight, norm_params],
            [((attn_own, out_kind * half_width + side_width // 2), LOW)] * 2, (),
            [pltpu.VMEM((attn_own, side_width), FULL)],
        ),
    )
    attn.begin()
    up = Gather(
        exchange,
        *elementwise(
            exchange, "pack_up", pack_up_kernel, [up_weight, out_at[0]],
            [((attn_own, (ff + model_width) // 2), LOW)] * 2, [attn.mine],
        ),
    )
    up.hop()
    up.spread()
    attn.finish()
    attn.begin()
    down = Gather(
        exchange,
        *elementwise(
            exchange, "pack_down", pack_down_kernel, [down_weight], [((down_weight.shape[0], half_width), LOW)] * 2,
            [attn.have],
        ),
    )
    down.begin()
    attn.finish()
    for _ in exchange.rest[1:]:
        attn.hop()
    gate(exchange, attn.have)
    down.finish()
    attn.begin()
    down.begin()
    attn.finish()
    down.finish()
    gate(exchange, attn.have, down.have)
    attn.begin()
    for _ in exchange.rest[1:]:
        down.hop()
    attn.finish()
    gate(exchange, attn.have, down.have)
    attn.begin()
    down.begin()
    attn.finish()
    side_own, side_other = [part[:, -side_width // 2 :] for part in attn.halves]
    side = jnp.concatenate(
        [exchange.by_core(side_own, side_other), exchange.by_core(side_other, side_own)], axis=1
    ).reshape(devices, attn_own, side_width)
    compress_full = jnp.concatenate(
        [side[:, i * compress_own : (i + 1) * compress_own] for i in range(pieces)], axis=2
    ).reshape(-1, length)
    gains = (
        side[:, pieces * compress_own : pieces * compress_own + norm_kinds, :norm_own]
        .transpose(1, 0, 2)
        .reshape(norm_kinds, model_width)
        .astype(FULL)
    )
    gains = jnp.pad(gains, [(0, 8 - norm_kinds), (0, 0)])

    *kept, context = attend(
        exchange, attn.halves, inputs, segment_ids, compressed_segment, compress_full, [down.have]
    )
    context = context.reshape(token_count, model_width)
    up.have = hold(exchange, up.have)
    up.begin()
    down.finish()
    down.begin()
    up.finish()
    first_normed, first_inv, first_low = mix(exchange, up.halves, flat_in, context, gains, [down.have])
    active, slope = up_part(exchange, first_low, up.halves, ff, [])
    down.finish()
    down.begin()
    down.finish()
    result, grad_second, grad_second_low, sums_two = down_part(
        exchange, down.halves, active, first_normed, out_grad.reshape(token_count, model_width), gains, []
    )

    down_sum, up_sum, attn_sum = Reduce(exchange), Reduce(exchange), Scatter(exchange)
    down_own, down_other = down_grad_part(exchange, active, grad_second_low, [])
    down_sum.add(down_own, down_other)
    down_sum.merge()
    *up_grads, grad_first, grad_first_low, sums_one = ff_back(
        exchange, down.halves, up.halves, slope, grad_second_low, first_low, grad_second,
        first_normed, first_inv, gains, [down_sum.merged],
    )
    down_sum.plane()
    middle = len(up_grads) // 2
    for own, other in zip(up_grads[middle:], up_grads[:middle]):
        up_sum.add(own, other)
    out_own, out_other = outer_part(exchange, context, [grad_first_low], "out_grad_part", [])
    up_sum.add(out_own, out_other)
    up_sum.merge()
    *grads, comp_grad = attend_back(
        exchange, up.halves, grad_first_low.reshape(inputs.shape), kept,
        segment_ids, compressed_segment, compress_full, [up_sum.merged] + down_sum.planes,
    )
    up_sum.plane()
    qkv_own, qkv_other = outer_part(exchange, flat_in, grads, "qkv_grad_part", [])
    norm_grad = jnp.concatenate([sums_one[:2], sums_two[:2]])
    side_grad = side_rows(
        comp_grad.reshape(devices, compress_own, length),
        norm_grad.reshape(norm_kinds, devices, norm_own).transpose(1, 0, 2),
    ).reshape(model_width, side_width).astype(LOW)
    side_left, side_right = halves(side_grad)
    attn_sum.add(qkv_own, qkv_other)
    attn_sum.add(exchange.by_core(side_left, side_right), exchange.by_core(side_right, side_left))
    attn_sum.merge()
    attn_sum.begin()
    down_sum.begin()
    input_grad = input_part(
        exchange, attn.halves, grad_first, *grads,
        [attn_sum.sent_now, down_sum.sent_now] + up_sum.planes,
    )

    attn_sum.finish()
    attn_sum.begin()
    down_sum.finish()
    down_sum.begin()
    up_sum.begin()
    gate(exchange, attn_sum.sent_now, down_sum.sent_now, up_sum.sent_now)
    attn_sum.finish()
    attn_sum.begin()
    down_sum.finish()
    down_sum.begin()
    up_sum.finish()
    up_sum.begin()
    down_first_new, down_second_new, down_direction, down_squares = elementwise(
        exchange, "down_step", down_step_kernel,
        [down_sum.mine, down_sum.got, down_weight, down_first, down_second],
        [(down_weight.shape, FULL)] * 3 + [((16, LANES), FULL)], [attn_sum.sent_now, up_sum.sent_now],
    )
    attn_sum.finish()
    attn_sum.begin()
    up_sum.finish()
    up_sum.begin()
    out_shape = attn_weight.shape[1:]
    up_first_new, up_second_new, up_direction, out_first_new, out_second_new, out_direction, up_squares = elementwise(
        exchange, "up_step", up_step_kernel,
        [up_sum.mine, up_sum.got, up_weight, up_first, up_second] + out_at,
        [(up_weight.shape, FULL)] * 3 + [(out_shape, FULL)] * 3 + [((16, LANES), FULL)], [attn_sum.sent_now],
    )
    attn_sum.finish()
    while attn_sum.hops:
        attn_sum.hop()
    three = (out_kind,) + out_shape
    (
        attn_first_new, attn_second_new, attn_direction,
        compress_first_new, compress_second_new, compress_direction,
        norm_first_new, norm_second_new, norm_new, sent, _,
    ) = elementwise(
        exchange, "attn_step", attn_step_kernel,
        [attn_sum.mine, attn_sum.got, attn_weight, attn_first, attn_second,
         compress_weight, compress_first, compress_second, norm_params, norm_first, norm_second,
         out_first_new, up_squares, down_squares],
        [(attn_weight.shape, FULL), (three, FULL), (three, FULL)] + [(compress_weight.shape, FULL)] * 3
        + [(norm_params.shape, FULL)] * 3 + [((devices, 16, LANES), FULL), ((16, LANES), FULL)],
    )
    got = lax.all_to_all(sent, AXES, split_axis=0, concat_axis=0, tiled=True)
    attn_new, attn_copy, up_new, up_copy, down_new, down_copy, compress_new, compress_copy, norms = elementwise(
        exchange, "finish", finish_kernel,
        [got, attn_weight, attn_direction, out_direction, up_weight, up_direction, down_weight, down_direction,
         compress_weight, compress_direction],
        [(a.shape, t) for a in (attn_weight, up_weight, down_weight, compress_weight) for t in (FULL, LOW)]
        + [((2, attn_kinds + 3), FULL)],
    )
    return (
        result.reshape(row_count, length, model_width),
        input_grad.reshape(row_count, length, model_width),
        attn_first_new,
        attn_second_new,
        out_second_new,
        attn_new,
        attn_copy,
        up_first_new,
        up_second_new,
        up_new,
        up_copy,
        down_first_new,
        down_second_new,
        down_new,
        down_copy,
        compress_first_new,
        compress_second_new,
        compress_new,
        compress_copy,
        norm_first_new,
        norm_second_new,
        norm_new,
        norms,
    )


def solution(mesh):
    rows, mid, flat = P(AXES, None), P(None, AXES, None), P(None, AXES)
    deep = P(AXES, None, None)

    def step(*args):
        return local(mesh.shape["dp"], mesh.shape["fsdp"], *args)

    return jax.shard_map(
        step,
        mesh=mesh,
        in_specs=(deep, rows, rows, deep) + (mid,) * 3 + (rows,) * 9 + (flat,) * 3,
        out_specs=(deep, deep, mid, mid, rows, mid, mid)
        + (rows,) * 12
        + (flat,) * 3
        + (P(),),
        check_vma=False,
    )
```

```python
import jax
import jax.numpy as jnp
from jax import lax
from jax.experimental import pallas as pl
from jax.experimental.pallas import tpu as pltpu
from jax.sharding import PartitionSpec as P

HEAD_DIM = 64
STEP = 10


BETA_ONE = 0.9
BETA_TWO = 0.999
EPSILON = 1e-06
DECAY = 0.01
RATE = 0.5
NORM_EPS = 1e-05
MASKED = -1e30

AXES = ("dp", "fsdp")
LOW = jnp.bfloat16
FULL = jnp.float32
MEGA = 1024 * 1024
ROOM = {"attend": 22, "attend_back": 22, "up_part": 26, "ff_back": 44, "down_part": 20}
LANES = 128


class Exchange:
    def __init__(self, dp, fsdp):
        self.count = dp * fsdp
        self.bits = self.count.bit_length() - 1
        self.x_bit = 1
        self.y_bit = fsdp.bit_length() - 1
        self.rest = [b for b in range(1, self.bits) if b not in (self.x_bit, self.y_bit)]
        self.index = lax.axis_index(AXES).astype(jnp.int32).reshape(1)

    def value(self, bit):
        return (self.index[0] >> bit) & 1

    def flip(self, array, even_bit, odd_bit):
        pairs = [(i, i ^ (1 << (odd_bit if i & 1 else even_bit))) for i in range(self.count)]
        return lax.ppermute(array, AXES, pairs)

    def by_core(self, even, odd):
        return jnp.where(self.value(0) == 0, even, odd)

    def joined(self, own, other, value, axis):
        return jnp.where(
            value == 0, jnp.stack([own, other], axis), jnp.stack([other, own], axis)
        )

    def groups(self, step, size):
        return [
            [base + low + step * i for i in range(size)]
            for base in range(0, self.count, step * size)
            for low in range(step)
        ]

    def pick(self, array, dim, value):
        return lax.dynamic_index_in_dim(array, value, dim, keepdims=False)


class Gather:
    def __init__(self, exchange, mine, sent):
        self.exchange = exchange
        self.mine, self.sent = mine, sent
        self.hops = ["pair"] + exchange.rest[::-1] + ["near", "last", "core"]
        self.place = 0

    def spread(self):
        ex = self.exchange
        self.hops = ["core"]
        self.have = lax.all_gather(
            self.have, AXES, axis=0, axis_index_groups=ex.groups(2, ex.count // 2), tiled=True
        )

    def begin(self):
        ex = self.exchange
        hop = self.hops[0]
        if hop == "pair":
            self.got = ex.flip(self.sent, 0, 0)
        elif hop == "near":
            self.got = ex.flip(self.have, ex.y_bit, ex.x_bit)
        elif hop == "last":
            self.got = ex.flip(self.have, ex.x_bit, ex.y_bit)
        elif hop == "core":
            self.got = ex.flip(self.have, 0, 0)
        else:
            self.got = ex.flip(self.have, hop, hop)

    def finish(self):
        ex = self.exchange
        hop = self.hops.pop(0)
        x_value, y_value = ex.value(ex.x_bit), ex.value(ex.y_bit)
        if hop == "pair":
            self.have = ex.joined(self.mine, self.got, ex.value(0), 0)
            self.have = self.have.reshape((-1,) + self.mine.shape[1:])
            self.block = self.have.shape
        elif hop == "near":
            self.have = ex.joined(self.have, self.got, ex.by_core(y_value, x_value), 0)
        elif hop == "last":
            have = ex.joined(self.have, self.got, ex.by_core(x_value, y_value), 0)
            wanted = list(range(ex.bits - 1, 0, -1))
            tail = [len(wanted), len(wanted) + 1]
            forms = []
            for first, second in ((ex.x_bit, ex.y_bit), (ex.y_bit, ex.x_bit)):
                now = [first, second] + ex.rest[::-1]
                forms.append(have.transpose([now.index(b) for b in wanted] + tail))
            self.have = ex.by_core(*forms).reshape((ex.count // 2) * self.block[0], self.block[1])
        elif hop == "core":
            self.halves = self.have, self.got
        else:
            self.have = ex.joined(self.have, self.got, ex.value(hop), self.place)
            self.place += 1

    def hop(self):
        self.begin()
        self.finish()


class Scatter:
    def __init__(self, exchange):
        self.exchange = exchange
        self.own, self.sent = [], []
        self.hops = ["near", "next"] + exchange.rest + ["last"]
        self.place = len(exchange.rest)

    def add(self, own, other):
        self.own.append(own)
        self.sent.append(self.exchange.flip(other, 0, 0))

    def merge(self):
        parts = [(a.astype(FULL) + b.astype(FULL)).astype(LOW) for a, b in zip(self.own, self.sent)]
        view = parts[0] if len(parts) == 1 else jnp.concatenate(parts, axis=1)
        self.have = view.reshape((2,) * (self.exchange.bits - 1) + (-1, view.shape[1]))

    def part(self, x_now, y_now):
        ex = self.exchange
        bits = list(range(ex.bits - 1, 0, -1))
        dim_x, dim_y = bits.index(ex.x_bit), bits.index(ex.y_bit)
        even = ex.pick(jnp.moveaxis(self.have, (dim_x, dim_y), (0, 1)), 0, x_now)
        odd = ex.pick(jnp.moveaxis(self.have, (dim_y, dim_x), (0, 1)), 0, y_now)
        return ex.by_core(even, odd)

    def begin(self):
        ex = self.exchange
        hop = self.hops[0]
        x_value, y_value = ex.value(ex.x_bit), ex.value(ex.y_bit)
        if hop == "near":
            self.sent_now = self.part(1 - x_value, 1 - y_value)
            self.got = ex.flip(self.sent_now, ex.x_bit, ex.y_bit)
        elif hop == "next":
            value = ex.by_core(y_value, x_value)
            self.sent_now = ex.pick(self.have, 0, 1 - value).astype(LOW)
            self.got = ex.flip(self.sent_now, ex.y_bit, ex.x_bit)
        elif hop == "last":
            view = self.have.reshape(2, -1, self.have.shape[-1])
            self.sent_now = ex.pick(view, 0, 1 - ex.value(0)).astype(LOW)
            self.got = ex.flip(self.sent_now, 0, 0)
        else:
            self.place -= 1
            self.sent_now = ex.pick(self.have, self.place, 1 - ex.value(hop)).astype(LOW)
            self.got = ex.flip(self.sent_now, hop, hop)

    def finish(self):
        ex = self.exchange
        hop = self.hops.pop(0)
        x_value, y_value = ex.value(ex.x_bit), ex.value(ex.y_bit)
        if hop == "last":
            self.mine = ex.pick(self.have.reshape(2, -1, self.have.shape[-1]), 0, ex.value(0))
            return
        got = self.got.astype(FULL)
        if hop == "near":
            self.have = self.part(x_value, y_value).astype(FULL) + got
        elif hop == "next":
            self.have = ex.pick(self.have, 0, ex.by_core(y_value, x_value)) + got
        else:
            self.have = ex.pick(self.have, self.place, ex.value(hop)) + got

    def hop(self):
        self.begin()
        self.finish()


class Reduce:
    def __init__(self, exchange):
        self.exchange = exchange
        self.own, self.sent, self.planes = [], [], []
        self.far = 4
        self.near = exchange.count // 2 // self.far
        self.hops = [exchange.bits - 2, exchange.bits - 1, "last"]

    def add(self, own, other):
        self.own.append(own)
        self.sent.append(self.exchange.flip(other, 0, 0))

    def merge(self):
        parts = [a.astype(FULL) + b.astype(FULL) for a, b in zip(self.own, self.sent)]
        self.own, self.sent = [], []
        view = parts[0] if len(parts) == 1 else jnp.concatenate(parts, axis=1)
        rows, width = view.shape
        view = view.astype(LOW).reshape(self.far, self.near, -1, width).transpose(1, 0, 2, 3)
        self.merged = view.reshape(rows, width)

    def plane(self):
        groups = self.exchange.groups(2, self.near)
        self.planes.append(
            lax.psum_scatter(self.merged, AXES, scatter_dimension=0, axis_index_groups=groups, tiled=True)
        )

    def line(self):
        ex = self.exchange
        self.hops = ["last"]
        groups = ex.groups(2 * self.near, self.far)
        self.have = lax.psum_scatter(
            self.planes.pop(), AXES, scatter_dimension=0, axis_index_groups=groups, tiled=True
        )

    def begin(self):
        ex = self.exchange
        hop = self.hops[0]
        if self.planes:
            views = [p.reshape(2, 2, p.shape[0] // 4, p.shape[1]) for p in self.planes]
            self.have = views[0] if len(views) == 1 else jnp.concatenate(views, axis=3)
            self.planes = []
        if hop == "last":
            view = self.have.reshape(2, -1, self.have.shape[-1])
            self.sent_now = ex.pick(view, 0, 1 - ex.value(0)).astype(LOW)
            self.mine = ex.pick(view, 0, ex.value(0))
            self.got = ex.flip(self.sent_now, 0, 0)
        else:
            self.sent_now = ex.pick(self.have, len(self.hops) - 2, 1 - ex.value(hop)).astype(LOW)
            self.got = ex.flip(self.sent_now, hop, hop)

    def finish(self):
        ex = self.exchange
        hop = self.hops.pop(0)
        if hop != "last":
            self.have = ex.pick(self.have, len(self.hops) - 1, ex.value(hop)).astype(FULL) + self.got.astype(FULL)


def matmul(left, right, left_dim=1, right_dim=0):
    return lax.dot_general(
        left, right, (((left_dim,), (right_dim,)), ((), ())), preferred_element_type=FULL
    )


def cost(flops, moved, transcendentals=0):
    return pl.CostEstimate(flops=flops, bytes_accessed=moved, transcendentals=transcendentals)


def whole(shape):
    return pl.BlockSpec(shape, lambda *_: (0,) * len(shape), pipeline_mode=pl.Buffered(1))


def kept_block(shape):
    return pl.BlockSpec(shape, lambda *_: (0,) * len(shape))


def anywhere():
    return pl.BlockSpec(memory_space=pl.ANY)


def call(exchange, name, body, grid, ins, outs, scratch=(), work=None, onto=(), later_than=()):
    count_in, count_gone = len(ins), len(onto) + len(later_than)

    def kernel(index_ref, *refs):
        given = refs[:count_in]
        rest = refs[count_in + count_gone :]
        token_ref, results = rest[0], rest[1:]
        token_ref[0] = index_ref[0]
        body(index_ref, *given, *results)

    def out(shape, kind, place=None):
        return jax.ShapeDtypeStruct(shape, kind) if place is None else place(shape, kind)

    results = pl.pallas_call(
        kernel,
        grid_spec=pltpu.PrefetchScalarGridSpec(
            num_scalar_prefetch=1,
            grid=grid,
            in_specs=[spec for _, spec in ins] + [anywhere()] * count_gone,
            out_specs=[pl.BlockSpec(memory_space=pltpu.SMEM)] + [o[2] for o in outs],
            scratch_shapes=list(scratch),
        ),
        out_shape=[out((1,), jnp.int32)] + [out(o[0], o[1], *o[3:]) for o in outs],
        input_output_aliases={1 + count_in + i: 1 + i for i in range(len(onto))},
        compiler_params=pltpu.CompilerParams(vmem_limit_bytes=ROOM.get(name, 18) * MEGA),
        cost_estimate=work,
        name=name,
    )(exchange.index, *[a for a, _ in ins], *onto, *later_than)
    exchange.index = results[0]
    return results[1:]


def far(array):
    return pltpu.with_memory_space_constraint(array, pltpu.HBM)


def gate(exchange, *arrays):
    call(exchange, "gate", lambda index_ref: None, (1,), [], [], work=cost(1, 1), later_than=arrays)


def hold(exchange, array, later_than=()):
    return call(
        exchange, "hold", lambda index_ref, array_ref: None, (1,), [], [(array.shape, array.dtype, anywhere())],
        work=cost(1, 1), onto=[array], later_than=later_than,
    )[0]


def norm_stats(mixed):
    average = jnp.mean(mixed, axis=-1, keepdims=True)
    centered = mixed - average
    inv_std = lax.rsqrt(jnp.mean(centered * centered, axis=-1, keepdims=True) + NORM_EPS)
    return centered * inv_std, inv_std


def norm_pull(grad_out, normed, inv_std, gain):
    scaled = grad_out * gain
    return inv_std * (
        scaled
        - jnp.mean(scaled, axis=-1, keepdims=True)
        - normed * jnp.mean(scaled * normed, axis=-1, keepdims=True)
    )


def head_lanes(pair, head):
    lane = lax.broadcasted_iota(jnp.int32, pair.shape, 1)
    mine = (lane < HEAD_DIM) if head % 2 == 0 else (lane >= HEAD_DIM)
    return jnp.where(mine, pair, jnp.zeros((), pair.dtype))


def column_copies(core, own, other, first, target, sems):
    half = target.shape[1] // 2
    copies = []
    for i, (source, place) in enumerate(((own, core), (other, 1 - core))):
        at = pl.multiple_of(place * half, LANES)
        copies.append(
            pltpu.make_async_copy(
                source.at[:, first : first + half], target.at[:, pl.ds(at, half)], sems.at[i]
            )
        )
    return copies


def attend_kernel(index_ref, own_ref, other_ref, x_ref, seg_ref, comp_ref, proj_ref,
                  q_ref, k_ref, v_ref, ck_ref, cv_ref, lse_ref, ctx_ref, ctx_t, weights, sems):
    width = x_ref.shape[2]
    heads = width // HEAD_DIM
    copies = [
        column_copies(index_ref[0] & 1, own_ref, other_ref, kind * (width // 2), weights.at[kind], sems.at[kind])
        for kind in range(3)
    ]
    first = pl.program_id(0) == 0

    @pl.when(first)
    def _():
        for copy in sum(copies, []):
            copy.start()

    def arrive(kind):
        @pl.when(first)
        def _():
            for copy in copies[kind]:
                copy.wait()

    x = x_ref[0]
    arrive(0)
    q_ref[0] = matmul(x, weights[0]).astype(LOW)
    arrive(1)
    k_ref[0] = matmul(x, weights[1]).astype(LOW)
    arrive(2)
    v_ref[0] = matmul(x, weights[2]).astype(LOW)
    member = comp_ref[0] == seg_ref[0]
    masked = jnp.where(member, proj_ref[...], jnp.zeros((), LOW))
    ck_ref[0] = (matmul(masked, k_ref[0])).astype(LOW)
    cv = matmul(masked, v_ref[0])
    cv_ref[0] = cv.astype(LOW)
    cv_t = cv.T.astype(LOW)
    for head in range(heads):
        lanes = slice(head // 2 * LANES, head // 2 * LANES + LANES)
        rows = slice(head * HEAD_DIM, (head + 1) * HEAD_DIM)
        keys = head_lanes(ck_ref[0, :, lanes], head) * (HEAD_DIM ** -0.5)
        scores = matmul(keys.astype(LOW), q_ref[0, :, lanes], 1, 1)
        scores = jnp.where(member, scores, MASKED)
        highest = jnp.max(scores, axis=0, keepdims=True)
        weight = jnp.exp(scores - highest)
        total = jnp.sum(weight, axis=0, keepdims=True)
        lse_ref[0, head : head + 1, :] = highest + jnp.log(total)
        probs = (weight * (1.0 / total)).astype(LOW)
        ctx_t[rows, :] = matmul(cv_t[rows, :], probs)
    ctx_ref[0] = ctx_t[...].T.astype(LOW)


def attend(exchange, halves, x, seg, comp, proj, later_than):
    rows, length, width = x.shape
    slots = comp.shape[1]
    heads = width // HEAD_DIM

    def at(*shape):
        return pl.BlockSpec((1,) + shape, lambda i, _: (i, 0, 0))

    tokens = ((rows, length, width), LOW, at(length, width), pltpu.HBM)
    comps = ((rows, slots, width), LOW, at(slots, width), pltpu.HBM)
    flops = rows * (length * width * (2 * 3 * width + 4 * slots * 4) + slots * length * width * 4)
    return call(
        exchange, "attend", attend_kernel, (rows,),
        [(far(halves[0]), anywhere()), (far(halves[1]), anywhere()), (far(x), at(length, width)), (seg[:, None, :], at(1, length)),
         (comp[:, :, None], at(slots, 1)), (proj, whole((slots, length)))],
        [tokens] * 3 + [comps] * 2 + [((rows, heads, length), FULL, at(heads, length), pltpu.HBM), tokens],
        [pltpu.VMEM((width, length), FULL), pltpu.VMEM((3, width, width), LOW), pltpu.SemaphoreType.DMA((3, 2))],
        cost(flops, 20 * 10**6, rows * heads * slots * length), (), later_than,
    )


def mix_kernel(index_ref, own_ref, other_ref, x_ref, ctx_ref, gains_ref, normed_ref, inv_ref, low_ref, weight, sems):
    @pl.when(pl.program_id(0) == 0)
    def _():
        first = own_ref.shape[1] - weight.shape[1] // 2
        copies = column_copies(index_ref[0] & 1, own_ref, other_ref, first, weight, sems)
        for copy in copies:
            copy.start()
        for copy in copies:
            copy.wait()

    mixed = x_ref[...].astype(FULL) + matmul(ctx_ref[...], weight[...])
    normed, inv_std = norm_stats(mixed)
    normed_ref[...] = normed
    inv_ref[...] = inv_std
    low_ref[...] = (normed * gains_ref[0:1] + gains_ref[1:2]).astype(LOW)


def mix(exchange, halves, x, ctx, gains, later_than, tile=256):
    tokens, width = x.shape

    def some(n):
        return pl.BlockSpec((tile, n), lambda i, _: (i, 0))

    return call(
        exchange, "mix", mix_kernel, (tokens // tile,),
        [(far(halves[0]), anywhere()), (far(halves[1]), anywhere()), (far(x), some(width)), (far(ctx), some(width)),
         (gains, whole(gains.shape))],
        [((tokens, width), FULL, some(width), pltpu.HBM), ((tokens, 1), FULL, some(1), pltpu.HBM),
         ((tokens, width), LOW, some(width))],
        [pltpu.VMEM((width, width), LOW), pltpu.SemaphoreType.DMA((2,))],
        cost(2 * tokens * width * width, 10 * 10**6), (), later_than,
    )


def gelu_pair(h):
    below = 1.0 + (0.3275911 * 0.5 ** 0.5) * jnp.abs(h)
    t = pl.reciprocal(below, approx=True)
    t = t * (2.0 - below * t)
    bell = jnp.exp(h * h * -0.5)
    poly = 0.127414796 + t * (-0.142248368 + t * (0.7107068705 + t * (-0.7265760135 + t * 0.5307027145)))
    tail = poly * (t * bell)
    cdf = jnp.where(h >= 0, 1.0 - tail, tail)
    return h * cdf, cdf + h * (bell * 0.3989422804014327)


def up_kernel(index_ref, f_ref, w_ref, act_ref, slope_ref):
    value, slope = gelu_pair(matmul(f_ref[...], w_ref[...]))
    act_ref[...] = value.astype(LOW)
    slope_ref[...] = slope


def up_part(exchange, f, half, mine, ff, onto, later_than, tile=768):
    tokens, width = f.shape
    steps = ff // tile // 2

    def place(j, index_ref):
        core = index_ref[0] & 1
        return (0, (core if mine else 1 - core) * steps + j)

    out = pl.BlockSpec((tokens, tile), place)
    return call(
        exchange, "up_part", up_kernel, (steps,),
        [(f, whole((tokens, width))), (half, pl.BlockSpec((width, tile), lambda j, _: (0, j)))],
        [((tokens, ff), LOW, out, pltpu.HBM), ((tokens, ff), FULL, out, pltpu.HBM)],
        (), cost(tokens * width * ff, 13 * 10**6, tokens * ff // 2), onto, later_than,
    )


def down_kernel(index_ref, own_ref, other_ref, act_ref, normed_ref, og_ref, gains_ref,
                out_ref, g_ref, low_ref, sums_ref, weight, sems):
    @pl.when(pl.program_id(0) == 0)
    def _():
        sums_ref[...] = jnp.zeros_like(sums_ref)
        copies = column_copies(index_ref[0] & 1, own_ref, other_ref, 0, weight, sems)
        for copy in copies:
            copy.start()
        for copy in copies:
            copy.wait()

    first = normed_ref[...] * gains_ref[0:1] + gains_ref[1:2]
    normed, inv_std = norm_stats(first + matmul(act_ref[...], weight[...]))
    out_ref[...] = (normed * gains_ref[2:3] + gains_ref[3:4]).astype(LOW)
    top = og_ref[...].astype(FULL)
    grad = norm_pull(top, normed, inv_std, gains_ref[2:3])
    g_ref[...] = grad
    low_ref[...] = grad.astype(LOW)
    sums_ref[0:1] += jnp.sum(top * normed, axis=0, keepdims=True)
    sums_ref[1:2] += jnp.sum(top, axis=0, keepdims=True)


def down_part(exchange, halves, act, normed, og, gains, later_than, tile=256):
    tokens, ff = act.shape
    width = normed.shape[1]

    def some(n):
        return pl.BlockSpec((tile, n), lambda i, _: (i, 0))

    return call(
        exchange, "down_part", down_kernel, (tokens // tile,),
        [(far(halves[0]), anywhere()), (far(halves[1]), anywhere()), (far(act), some(ff)), (far(normed), some(width)), (far(og), some(width)),
         (gains, whole(gains.shape))],
        [((tokens, width), LOW, some(width)), ((tokens, width), FULL, some(width)), ((tokens, width), LOW, some(width)),
         ((8, width), FULL, kept_block((8, width)))],
        [pltpu.VMEM((ff, width), LOW), pltpu.SemaphoreType.DMA((2,))],
        cost(2 * tokens * width * ff, 23 * 10**6), (), later_than,
    )


def split_columns(index_ref, total, own_ref, other_ref):
    half = total.shape[1] // 2
    left, right = total[:, :half].astype(LOW), total[:, half:].astype(LOW)
    even = (index_ref[0] & 1) == 0
    own_ref[...] = jnp.where(even, left, right)
    other_ref[...] = jnp.where(even, right, left)


def outer_kernel(index_ref, left_ref, *refs):
    *right_refs, own_ref, other_ref = refs
    for kind, right_ref in enumerate(right_refs):

        @pl.when(pl.program_id(0) == kind)
        def _(right_ref=right_ref):
            split_columns(index_ref, matmul(left_ref[...], right_ref[...], 0, 0), own_ref, other_ref)


def outer_part(exchange, left, rights, name, later_than):
    tokens, depth = left.shape
    width = rights[0].shape[1]
    half = ((depth, len(rights) * width // 2), LOW, pl.BlockSpec((depth, width // 2), lambda j, _: (0, j)))
    return call(
        exchange, name, outer_kernel, (len(rights),),
        [(far(left), whole((tokens, depth)))] + [(r, whole((tokens, width))) for r in rights],
        [half] * 2, (), cost(2 * tokens * depth * width * len(rights), 9 * 10**6), (), later_than,
    )


def down_grad_kernel(index_ref, act_ref, g_ref, own_ref, other_ref):
    split_columns(index_ref, matmul(act_ref[...], g_ref[...], 0, 0), own_ref, other_ref)


def down_grad_part(exchange, act, g, later_than, tile=768):
    tokens, ff = act.shape
    width = g.shape[1]
    half = ((ff, width // 2), LOW, pl.BlockSpec((tile, width // 2), lambda j, _: (j, 0)))
    return call(
        exchange, "down_grad_part", down_grad_kernel, (ff // tile,),
        [(far(act), pl.BlockSpec((tokens, tile), lambda j, _: (0, j))), (g, whole((tokens, width)))],
        [half] * 2, (), cost(2 * tokens * width * ff, 13 * 10**6), (), later_than,
    )


def ff_back_kernel(index_ref, down_own, down_other, up_own, up_other, slope_ref, low_ref, f_ref, start_ref, normed_ref,
                   inv_ref, gains_ref, *refs):
    *grad_refs, g_one_ref, g_one_low_ref, sums_ref, total, w_down, sems = refs
    step = pl.program_id(0)
    steps = pl.num_programs(0)
    half = steps // 2
    core = index_ref[0] & 1
    tile = slope_ref.shape[1]

    def copies(at):
        place = jnp.where(at < half, (1 - core) * half + at, core * half + at - half)
        rows = pl.ds(pl.multiple_of(place * tile, tile), tile)
        return column_copies(core, down_own.at[rows], down_other.at[rows], 0, w_down.at[at % 2], sems.at[at % 2])

    @pl.when(step == 0)
    def _():
        for copy in copies(step):
            copy.start()
        total[...] = start_ref[...]

    @pl.when(step < steps - 1)
    def _():
        for copy in copies(step + 1):
            copy.start()

    for copy in copies(step):
        copy.wait()

    back = (matmul(low_ref[...], w_down[step % 2], 1, 1) * slope_ref[...]).astype(LOW)
    grads = matmul(f_ref[...], back, 0, 0).astype(LOW)
    for at, grad_ref in enumerate(grad_refs):

        @pl.when(step == at)
        def _(grad_ref=grad_ref):
            grad_ref[...] = grads

    def add(up_ref):
        total[...] += matmul(back, up_ref[...], 1, 1)

    pl.when(step < half)(lambda: add(up_other))
    pl.when(step >= half)(lambda: add(up_own))

    @pl.when(step == steps - 1)
    def _():
        top = total[...]
        normed = normed_ref[...]
        grad = norm_pull(top, normed, inv_ref[...], gains_ref[0:1])
        g_one_ref[...] = grad
        g_one_low_ref[...] = grad.astype(LOW)
        sums_ref[...] = jnp.zeros_like(sums_ref)
        sums_ref[0:1] = jnp.sum(top * normed, axis=0, keepdims=True)
        sums_ref[1:2] = jnp.sum(top, axis=0, keepdims=True)


def ff_back(exchange, down, up, slope, low, f, start, normed, inv, gains, later_than, tile=768):
    tokens, ff = slope.shape
    width = f.shape[1]
    steps = ff // tile
    half = steps // 2

    def place(j, index_ref):
        core = index_ref[0] & 1
        return (0, jnp.where(j < half, (1 - core) * half + j, core * half + j - half))

    full = whole((tokens, width))
    result = kept_block((tokens, width))
    return call(
        exchange, "ff_back", ff_back_kernel, (steps,),
        [(down[0], anywhere()), (down[1], anywhere()),
         (up[0], pl.BlockSpec((width, tile), lambda j, _: (0, jnp.maximum(j - half, 0)))),
         (up[1], pl.BlockSpec((width, tile), lambda j, _: (0, jnp.minimum(j, half - 1)))),
         (far(slope), pl.BlockSpec((tokens, tile), place)),
         (low, full), (far(f), full), (start, full), (far(normed), full), (far(inv), whole(inv.shape)), (gains, whole(gains.shape))],
        [((width, tile), LOW, whole((width, tile)))] * steps
        + [((tokens, width), FULL, result, pltpu.HBM), ((tokens, width), LOW, result, pltpu.HBM),
         ((8, width), FULL, kept_block((8, width)))],
        [pltpu.VMEM((tokens, width), FULL), pltpu.VMEM((2, tile, width), LOW), pltpu.SemaphoreType.DMA((2, 2))],
        cost(6 * tokens * width * ff, 40 * 10**6), (), later_than,
    )


def attend_back_kernel(index_ref, own_ref, other_ref, g_ref, q_ref, k_ref, v_ref, ck_ref, cv_ref, lse_ref,
                       seg_ref, comp_ref, proj_ref,
                       gq_ref, gk_ref, gv_ref, grad_ref, gctx, gq_t, gck, gcv, weight, sems):
    width = q_ref.shape[2]
    heads = width // HEAD_DIM
    scale = HEAD_DIM ** -0.5

    @pl.when(pl.program_id(0) == 0)
    def _():
        copies = column_copies(
            index_ref[0] & 1, own_ref, other_ref, own_ref.shape[1] - width // 2, weight, sems
        )
        for copy in copies:
            copy.start()
        for copy in copies:
            copy.wait()

    gctx[...] = matmul(g_ref[0], weight[...], 1, 1).astype(LOW)
    member = comp_ref[0] == seg_ref[0]
    ck_t = ck_ref[0].astype(FULL).T.astype(LOW)
    for pair in range(heads // 2):
        lanes = slice(pair * LANES, pair * LANES + LANES)
        queries, grads = q_ref[0, :, lanes], gctx[:, lanes]
        key_parts, value_parts = [], []
        for head in (2 * pair, 2 * pair + 1):
            rows = slice(head * HEAD_DIM, (head + 1) * HEAD_DIM)
            keys = head_lanes(ck_ref[0, :, lanes], head) * scale
            scores = matmul(keys.astype(LOW), queries, 1, 1)
            probs = jnp.exp(jnp.where(member, scores - lse_ref[0, head : head + 1, :], MASKED))
            grad_probs = matmul(head_lanes(cv_ref[0, :, lanes], head), grads, 1, 1)
            delta = jnp.sum(probs * grad_probs, axis=0, keepdims=True)
            grad_scores = (probs * (grad_probs - delta)).astype(LOW)
            gq_t[rows, :] = matmul(ck_t[rows, :], grad_scores) * scale
            key_parts.append(matmul(grad_scores, queries))
            value_parts.append(matmul(probs.astype(LOW), grads))
        lane = lax.broadcasted_iota(jnp.int32, key_parts[0].shape, 1) < HEAD_DIM
        gck[:, lanes] = (jnp.where(lane, *key_parts) * scale).astype(LOW)
        gcv[:, lanes] = jnp.where(lane, *value_parts).astype(LOW)
    gq_ref[...] = gq_t[...].T.astype(LOW)
    masked = jnp.where(member, proj_ref[...], jnp.zeros((), LOW))
    gk_ref[...] = matmul(masked, gck[...], 0, 0).astype(LOW)
    gv_ref[...] = matmul(masked, gcv[...], 0, 0).astype(LOW)
    part = matmul(gck[...], k_ref[0], 1, 1) + matmul(gcv[...], v_ref[0], 1, 1)
    part = jnp.where(member, part, 0.0)

    @pl.when(pl.program_id(0) == 0)
    def _():
        grad_ref[...] = part

    @pl.when(pl.program_id(0) > 0)
    def _():
        grad_ref[...] += part


def attend_back(exchange, halves, g, kept, seg, comp, proj, later_than):
    q, k, v, ck, cv, lse = kept
    rows, length, width = q.shape
    slots = comp.shape[1]
    heads = width // HEAD_DIM

    def at(*shape):
        return pl.BlockSpec((1,) + shape, lambda i, _: (i, 0, 0))

    tokens = ((rows * length, width), LOW, pl.BlockSpec((length, width), lambda i, _: (i, 0)))
    flops = rows * length * width * (2 * width + 4 * slots * 10)
    return call(
        exchange, "attend_back", attend_back_kernel, (rows,),
        [(far(halves[0]), anywhere()), (far(halves[1]), anywhere())] + [(a, at(length, width)) for a in (far(g), far(q), far(k), far(v))]
        + [(far(a), at(slots, width)) for a in (ck, cv)]
        + [(far(lse), at(heads, length)), (seg[:, None, :], at(1, length)), (comp[:, :, None], at(slots, 1)),
           (far(proj), whole((slots, length)))],
        [tokens] * 3 + [((slots, length), FULL, kept_block((slots, length)))],
        [pltpu.VMEM((length, width), LOW), pltpu.VMEM((width, length), FULL),
         pltpu.VMEM((slots, width), LOW), pltpu.VMEM((slots, width), LOW),
         pltpu.VMEM((width, width), LOW), pltpu.SemaphoreType.DMA((2,))],
        cost(flops, 15 * 10**6, rows * heads * slots * length), (), later_than,
    )


def input_kernel(index_ref, own_ref, other_ref, g_ref, gq_ref, gk_ref, gv_ref, out_ref, weights, sems):
    width = g_ref.shape[1]

    @pl.when(pl.program_id(0) == 0)
    def _():
        copies = []
        for kind in range(3):
            copies += column_copies(
                index_ref[0] & 1, own_ref, other_ref, kind * (width // 2), weights.at[kind], sems.at[kind]
            )
        for copy in copies:
            copy.start()
        for copy in copies:
            copy.wait()

    out_ref[...] = (
        g_ref[...]
        + matmul(gq_ref[...], weights[0], 1, 1)
        + matmul(gk_ref[...], weights[1], 1, 1)
        + matmul(gv_ref[...], weights[2], 1, 1)
    )


def input_part(exchange, halves, g, gq, gk, gv, later_than, tile=256):
    tokens, width = g.shape
    some = pl.BlockSpec((tile, width), lambda i, _: (i, 0))
    return call(
        exchange, "input_part", input_kernel, (tokens // tile,),
        [(far(halves[0]), anywhere()), (far(halves[1]), anywhere())] + [(far(a), some) for a in (g, gq, gk, gv)],
        [((tokens, width), FULL, some)],
        [pltpu.VMEM((3, width, width), LOW), pltpu.SemaphoreType.DMA((3, 2))],
        cost(6 * tokens * width * width, 15 * 10**6), (), later_than,
    )[0]


def adaptive(first, second, grad):
    first_new = BETA_ONE * first + (1.0 - BETA_ONE) * grad
    second_new = BETA_TWO * second + (1.0 - BETA_TWO) * grad * grad
    direction = (
        first_new
        / (1.0 - BETA_ONE**STEP)
        / (jnp.sqrt(second_new / (1.0 - BETA_TWO**STEP)) + EPSILON)
    )
    return (first_new, second_new, direction)


def store_halves(index_ref, columns, left, right, own_ref, other_ref):
    even = (index_ref[0] & 1) == 0
    own_ref[:, columns] = jnp.where(even, left, right).astype(LOW)
    other_ref[:, columns] = jnp.where(even, right, left).astype(LOW)


def store_matrix(index_ref, columns, matrix, own_ref, other_ref):
    half = matrix.shape[1] // 2
    store_halves(index_ref, columns, matrix[:, :half], matrix[:, half:], own_ref, other_ref)


def pack_attn_kernel(index_ref, weight_ref, comp_ref, norm_ref, own_ref, other_ref, side):
    kinds = weight_ref.shape[0] - 1
    half = weight_ref.shape[2] // 2
    rows, length = comp_ref.shape
    pieces = length // side.shape[1]
    own, own_columns = norm_ref.shape
    side[...] = jnp.zeros_like(side)
    for i in range(pieces):
        side[i * rows : (i + 1) * rows, :] = comp_ref[:, i * side.shape[1] : (i + 1) * side.shape[1]]
    side[pieces * rows : pieces * rows + own, :own_columns] = norm_ref[...]
    for kind in range(kinds):
        store_matrix(index_ref, slice(kind * half, (kind + 1) * half), weight_ref[kind], own_ref, other_ref)
    store_matrix(index_ref, slice(kinds * half, None), side[...], own_ref, other_ref)


def pack_up_kernel(index_ref, weight_ref, out_ref, own_ref, other_ref):
    split = weight_ref.shape[1] // 2
    store_matrix(index_ref, slice(0, split), weight_ref[...], own_ref, other_ref)
    store_matrix(index_ref, slice(split, None), out_ref[0], own_ref, other_ref)


def pack_down_kernel(index_ref, weight_ref, own_ref, other_ref):
    store_matrix(index_ref, slice(None), weight_ref[...], own_ref, other_ref)


def squares_row(array):
    total = jnp.sum(jnp.sum(array * array, axis=0, keepdims=True), axis=1, keepdims=True)
    return jnp.broadcast_to(total, (1, LANES))


def step_matrix(weight, first, second, grad, first_ref, second_ref, direction_ref, sums_ref, row):
    first_new, second_new, direction = adaptive(first, second, grad)
    direction = direction + DECAY * weight
    first_ref[...] = first_new
    second_ref[...] = second_new
    direction_ref[...] = direction
    sums_ref[row : row + 1] = squares_row(weight)
    sums_ref[row + 8 : row + 9] = squares_row(direction)


def joined_halves(index_ref, mine, got):
    even = (index_ref[0] & 1) == 0
    return jnp.concatenate([jnp.where(even, mine, got), jnp.where(even, got, mine)], axis=1)


def down_step_kernel(index_ref, mine_ref, got_ref, weight_ref, first_ref, second_ref,
                     first_new, second_new, direction, sums_ref):
    sums_ref[...] = jnp.zeros_like(sums_ref)
    grad = joined_halves(index_ref, mine_ref[...].astype(FULL), got_ref[...].astype(FULL))
    step_matrix(weight_ref[...], first_ref[...], second_ref[...], grad, first_new, second_new, direction, sums_ref, 5)


def up_step_kernel(index_ref, mine_ref, got_ref, weight_ref, first_ref, second_ref, out_weight, out_first, out_second,
                   first_new, second_new, direction, out_first_new, out_second_new, out_direction, sums_ref):
    sums_ref[...] = jnp.zeros_like(sums_ref)
    split = weight_ref.shape[1] // 2
    mine, got = mine_ref[...].astype(FULL), got_ref[...].astype(FULL)
    grad = joined_halves(index_ref, mine[:, :split], got[:, :split])
    step_matrix(weight_ref[...], first_ref[...], second_ref[...], grad, first_new, second_new, direction, sums_ref, 4)
    grad = joined_halves(index_ref, mine[:, split:], got[:, split:])
    step_matrix(out_weight[0], out_first[0], out_second[0], grad,
                out_first_new, out_second_new, out_direction, sums_ref, 3)


def attn_step_kernel(index_ref, mine_ref, got_ref, weight_ref, first_ref, second_ref,
                     comp_weight, comp_first, comp_second, norm_weight, norm_first, norm_second,
                     out_first_new, up_sums, down_sums,
                     first_new, second_new, direction, comp_first_new, comp_second_new, comp_direction,
                     norm_first_new, norm_second_new, norm_new, sent_ref, sums_ref):
    sums_ref[...] = up_sums[...] + down_sums[...]
    kinds = weight_ref.shape[0] - 1
    width = weight_ref.shape[2]
    half = width // 2
    mine, got = mine_ref[...].astype(FULL), got_ref[...].astype(FULL)
    for kind in range(kinds):
        columns = slice(kind * half, (kind + 1) * half)
        grad = joined_halves(index_ref, mine[:, columns], got[:, columns])
        step_matrix(weight_ref[kind], first_ref[kind], second_ref[kind], grad,
                    first_new.at[kind], second_new.at[kind], direction.at[kind], sums_ref, kind)
    first_new[kinds] = out_first_new[...]
    side = joined_halves(index_ref, mine[:, kinds * half :], got[:, kinds * half :])
    rows, length = comp_weight.shape
    pieces = length // side.shape[1]
    grad = jnp.concatenate([side[i * rows : (i + 1) * rows] for i in range(pieces)], axis=1)
    step_matrix(comp_weight[...], comp_first[...], comp_second[...], grad,
                comp_first_new, comp_second_new, comp_direction, sums_ref, 6)
    own, own_columns = norm_weight.shape
    grad = side[pieces * rows : pieces * rows + own, :own_columns]
    new, newer, way = adaptive(norm_first[...], norm_second[...], grad)
    norm_first_new[...] = new
    norm_second_new[...] = newer
    norm_new[...] = norm_weight[...] - RATE * way
    sent_ref[...] = jnp.broadcast_to(sums_ref[...][None], sent_ref.shape)


def finish_kernel(index_ref, got_ref, weight_ref, direction_ref, out_direction, up_weight, up_direction,
                  down_weight, down_direction, comp_weight, comp_direction,
                  attn_new, attn_copy, up_new, up_copy, down_new, down_copy, comp_new, comp_copy, norms_ref):
    totals = jnp.sqrt(jnp.sum(got_ref[...], axis=0))
    lane = lax.broadcasted_iota(jnp.int32, (1, LANES), 1)
    count = norms_ref.shape[1]
    for i in range(2):
        row = sum(jnp.where(lane == m, totals[8 * i + m : 8 * i + m + 1], 0.0) for m in range(count))
        norms_ref[i : i + 1, :] = row[:, :count]
    ratio = totals[:8] / (totals[8:] + EPSILON)

    def move(weight, direction, matrix, new_ref, copy_ref):
        new = weight - RATE * ratio[matrix : matrix + 1, :1] * direction
        new_ref[...] = new
        copy_ref[...] = new.astype(LOW)

    for kind in range(4):
        way = direction_ref[kind] if kind < 3 else out_direction[...]
        move(weight_ref[kind], way, kind, attn_new.at[kind], attn_copy.at[kind])
    move(up_weight[...], up_direction[...], 4, up_new, up_copy)
    move(down_weight[...], down_direction[...], 5, down_new, down_copy)
    move(comp_weight[...], comp_direction[...], 6, comp_new, comp_copy)


def elementwise(exchange, name, body, ins, shapes, later_than=(), scratch=()):
    pairs = []
    for a in ins:
        if isinstance(a, tuple):
            shape, kind = (1,) + a[0].shape[1:], a[1]
            pairs.append((a[0], pl.BlockSpec(shape, lambda *_, kind=kind: (kind, 0, 0))))
        else:
            pairs.append((a, whole(a.shape)))
    return call(
        exchange, name, body, (1,), pairs, [(shape, kind, whole(shape)) for shape, kind in shapes], scratch,
        cost(10**6, sum(a.size * 4 for a, _ in pairs)), (), later_than,
    )


def local(
    dp,
    fsdp,
    inputs,
    segment_ids,
    compressed_segment,
    out_grad,
    attn_weight,
    attn_first,
    attn_second,
    up_weight,
    up_first,
    up_second,
    down_weight,
    down_first,
    down_second,
    compress_weight,
    compress_first,
    compress_second,
    norm_params,
    norm_first,
    norm_second,
):
    exchange = Exchange(dp, fsdp)
    devices = dp * fsdp
    row_count, length, model_width = inputs.shape
    half_width = model_width // 2
    token_count = row_count * length
    norm_kinds, norm_own = norm_params.shape
    attn_kinds, attn_own, _ = attn_weight.shape
    compress_own = compress_weight.shape[0]
    pieces = 2 if 2 * compress_own + norm_kinds <= attn_own else 1
    side_width = length // pieces

    def side_rows(compress_part, norm_part):
        none = [(0, 0)] * (compress_part.ndim - 2)
        spare = attn_own - pieces * compress_own - norm_kinds
        norm_part = jnp.pad(norm_part, none + [(0, spare), (0, side_width - norm_own)])
        parts = [compress_part[..., i * side_width : (i + 1) * side_width] for i in range(pieces)]
        return jnp.concatenate(parts + [norm_part], axis=-2)

    def halves(array):
        middle = array.shape[-1] // 2
        return array[..., :middle], array[..., middle:]

    flat_in = inputs.reshape(token_count, model_width)
    ff = up_weight.shape[1]
    out_kind = attn_kinds - 1
    out_at = [(a, out_kind) for a in (attn_weight, attn_first, attn_second)]
    attn = Gather(
        exchange,
        *elementwise(
            exchange, "pack_attn", pack_attn_kernel, [attn_weight, compress_weight, norm_params],
            [((attn_own, out_kind * half_width + side_width // 2), LOW)] * 2, (),
            [pltpu.VMEM((attn_own, side_width), FULL)],
        ),
    )
    attn.begin()
    up = Gather(
        exchange,
        *elementwise(
            exchange, "pack_up", pack_up_kernel, [up_weight, out_at[0]],
            [((attn_own, (ff + model_width) // 2), LOW)] * 2, [attn.mine],
        ),
    )
    up.begin()
    attn.finish()
    attn.begin()
    up.finish()
    up.have = hold(exchange, up.have)
    up.spread()
    attn.finish()
    for _ in exchange.rest[1:]:
        attn.hop()
    attn.hop()
    attn.hop()
    attn.begin()
    down = Gather(
        exchange,
        *elementwise(
            exchange, "pack_down", pack_down_kernel, [down_weight], [((down_weight.shape[0], half_width), LOW)] * 2,
            [attn.have],
        ),
    )
    down.hop()
    down.begin()
    attn.finish()
    side_own, side_other = [part[:, -side_width // 2 :] for part in attn.halves]
    side = jnp.concatenate(
        [exchange.by_core(side_own, side_other), exchange.by_core(side_other, side_own)], axis=1
    ).reshape(devices, attn_own, side_width)
    compress_full = jnp.concatenate(
        [side[:, i * compress_own : (i + 1) * compress_own] for i in range(pieces)], axis=2
    ).reshape(-1, length)
    gains = (
        side[:, pieces * compress_own : pieces * compress_own + norm_kinds, :norm_own]
        .transpose(1, 0, 2)
        .reshape(norm_kinds, model_width)
        .astype(FULL)
    )
    gains = jnp.pad(gains, [(0, 8 - norm_kinds), (0, 0)])

    *kept, context = attend(
        exchange, attn.halves, inputs, segment_ids, compressed_segment, compress_full, [down.have]
    )
    context = context.reshape(token_count, model_width)
    down.finish()
    while len(down.hops) > 4:
        down.hop()
    down.begin()
    up.have = hold(exchange, up.have, [down.have])
    up.begin()
    up.finish()
    first_normed, first_inv, first_low = mix(exchange, up.halves, flat_in, context, gains, [down.have])
    down.finish()
    down.begin()
    hidden = up_part(exchange, first_low, up.halves[0], True, ff, (), [down.have])
    down.finish()
    down.begin()
    active, slope = up_part(exchange, first_low, up.halves[1], False, ff, hidden, [down.have])
    down.finish()
    down.hop()
    result, grad_second, grad_second_low, sums_two = down_part(
        exchange, down.halves, active, first_normed, out_grad.reshape(token_count, model_width), gains, []
    )

    down_sum, up_sum, attn_sum = Reduce(exchange), Reduce(exchange), Scatter(exchange)
    down_own, down_other = down_grad_part(exchange, active, grad_second_low, [])
    down_sum.add(down_own, down_other)
    down_sum.merge()
    *up_grads, grad_first, grad_first_low, sums_one = ff_back(
        exchange, down.halves, up.halves, slope, grad_second_low, first_low, grad_second,
        first_normed, first_inv, gains, [far(down_sum.merged)],
    )
    down_sum.plane()
    middle = len(up_grads) // 2
    for own, other in zip(up_grads[middle:], up_grads[:middle]):
        up_sum.add(own, other)
    out_own, out_other = outer_part(exchange, context, [grad_first_low], "out_grad_part", [])
    up_sum.add(out_own, out_other)
    up_sum.merge()
    *grads, comp_grad = attend_back(
        exchange, up.halves, grad_first_low.reshape(inputs.shape), kept,
        segment_ids, compressed_segment, compress_full, [far(up_sum.merged)] + [far(p) for p in down_sum.planes],
    )
    up_sum.plane()
    qkv_own, qkv_other = outer_part(exchange, flat_in, grads, "qkv_grad_part", [])
    norm_grad = jnp.concatenate([sums_one[:2], sums_two[:2]])
    side_grad = side_rows(
        comp_grad.reshape(devices, compress_own, length),
        norm_grad.reshape(norm_kinds, devices, norm_own).transpose(1, 0, 2),
    ).reshape(model_width, side_width).astype(LOW)
    side_left, side_right = halves(side_grad)
    attn_sum.add(qkv_own, qkv_other)
    attn_sum.add(exchange.by_core(side_left, side_right), exchange.by_core(side_right, side_left))
    attn_sum.merge()
    attn_sum.begin()
    up_sum.begin()
    input_grad = input_part(
        exchange, attn.halves, grad_first, *grads, [attn_sum.sent_now, up_sum.sent_now]
    )
    down_sum.line()

    up_sum.finish()
    up_sum.begin()
    attn_sum.finish()
    attn_sum.begin()
    gate(exchange, attn_sum.sent_now, up_sum.sent_now)
    up_sum.finish()
    up_sum.begin()
    attn_sum.finish()
    attn_sum.begin()
    gate(exchange, attn_sum.sent_now, up_sum.sent_now)
    attn_sum.finish()
    attn_sum.begin()
    out_shape = attn_weight.shape[1:]
    up_first_new, up_second_new, up_direction, out_first_new, out_second_new, out_direction, up_squares = elementwise(
        exchange, "up_step", up_step_kernel,
        [up_sum.mine, up_sum.got, up_weight, up_first, up_second] + out_at,
        [(up_weight.shape, FULL)] * 3 + [(out_shape, FULL)] * 3 + [((16, LANES), FULL)], [attn_sum.sent_now],
    )
    down_sum.begin()
    attn_sum.finish()
    attn_sum.begin()
    down_first_new, down_second_new, down_direction, down_squares = elementwise(
        exchange, "down_step", down_step_kernel,
        [down_sum.mine, down_sum.got, down_weight, down_first, down_second],
        [(down_weight.shape, FULL)] * 3 + [((16, LANES), FULL)], [attn_sum.sent_now],
    )
    attn_sum.finish()
    while attn_sum.hops:
        attn_sum.hop()
    three = (out_kind,) + out_shape
    (
        attn_first_new, attn_second_new, attn_direction,
        compress_first_new, compress_second_new, compress_direction,
        norm_first_new, norm_second_new, norm_new, sent, _,
    ) = elementwise(
        exchange, "attn_step", attn_step_kernel,
        [attn_sum.mine, attn_sum.got, attn_weight, attn_first, attn_second,
         compress_weight, compress_first, compress_second, norm_params, norm_first, norm_second,
         out_first_new, up_squares, down_squares],
        [(attn_weight.shape, FULL), (three, FULL), (three, FULL)] + [(compress_weight.shape, FULL)] * 3
        + [(norm_params.shape, FULL)] * 3 + [((devices, 16, LANES), FULL), ((16, LANES), FULL)],
    )
    got = lax.all_to_all(sent, AXES, split_axis=0, concat_axis=0, tiled=True)
    attn_new, attn_copy, up_new, up_copy, down_new, down_copy, compress_new, compress_copy, norms = elementwise(
        exchange, "finish", finish_kernel,
        [got, attn_weight, attn_direction, out_direction, up_weight, up_direction, down_weight, down_direction,
         compress_weight, compress_direction],
        [(a.shape, t) for a in (attn_weight, up_weight, down_weight, compress_weight) for t in (FULL, LOW)]
        + [((2, attn_kinds + 3), FULL)],
    )
    return (
        result.reshape(row_count, length, model_width),
        input_grad.reshape(row_count, length, model_width),
        attn_first_new,
        attn_second_new,
        out_second_new,
        attn_new,
        attn_copy,
        up_first_new,
        up_second_new,
        up_new,
        up_copy,
        down_first_new,
        down_second_new,
        down_new,
        down_copy,
        compress_first_new,
        compress_second_new,
        compress_new,
        compress_copy,
        norm_first_new,
        norm_second_new,
        norm_new,
        norms,
    )


def solution(mesh):
    rows, mid, flat = P(AXES, None), P(None, AXES, None), P(None, AXES)
    deep = P(AXES, None, None)

    def step(*args):
        return local(mesh.shape["dp"], mesh.shape["fsdp"], *args)

    return jax.shard_map(
        step,
        mesh=mesh,
        in_specs=(deep, rows, rows, deep) + (mid,) * 3 + (rows,) * 9 + (flat,) * 3,
        out_specs=(deep, deep, mid, mid, rows, mid, mid)
        + (rows,) * 12
        + (flat,) * 3
        + (P(),),
        check_vma=False,
    )
```

```python
import jax
import jax.numpy as jnp
from jax import lax
from jax.experimental import pallas as pl
from jax.experimental.pallas import tpu as pltpu
from jax.sharding import PartitionSpec as P

HEAD_DIM = 64
STEP = 10


BETA_ONE = 0.9
BETA_TWO = 0.999
EPSILON = 1e-06
DECAY = 0.01
RATE = 0.5
NORM_EPS = 1e-05
MASKED = -1e30

AXES = ("dp", "fsdp")
LOW = jnp.bfloat16
FULL = jnp.float32
MEGA = 1024 * 1024
ROOM = {"attend": 22, "attend_back": 22, "up_part": 26, "ff_back": 44, "down_part": 20}
LANES = 128


class Exchange:
    def __init__(self, dp, fsdp):
        self.count = dp * fsdp
        self.bits = self.count.bit_length() - 1
        self.x_bit = 1
        self.y_bit = fsdp.bit_length() - 1
        self.rest = [b for b in range(1, self.bits) if b not in (self.x_bit, self.y_bit)]
        self.index = lax.axis_index(AXES).astype(jnp.int32).reshape(1)
        self.first_index = self.index

    def value(self, bit):
        return (self.index[0] >> bit) & 1

    def known(self, bit):
        return (self.first_index[0] >> bit) & 1

    def flip(self, array, even_bit, odd_bit):
        pairs = [(i, i ^ (1 << (odd_bit if i & 1 else even_bit))) for i in range(self.count)]
        return lax.ppermute(array, AXES, pairs)

    def masks(self):
        return [
            sum(((k >> i) & 1) << bit for i, bit in enumerate(self.rest)) for k in range(1 << len(self.rest))
        ]

    def move(self, array, mask):
        return lax.ppermute(array, AXES, [(i, i ^ mask) for i in range(self.count)])

    def by_rest(self, pieces):
        for i, bit in enumerate(self.rest):
            turned = self.value(bit) == 1
            pieces = [jnp.where(turned, pieces[k ^ (1 << i)], p) for k, p in enumerate(pieces)]
        return pieces

    def by_core(self, even, odd):
        return jnp.where(self.value(0) == 0, even, odd)

    def joined(self, own, other, value, axis):
        return jnp.where(
            value == 0, jnp.stack([own, other], axis), jnp.stack([other, own], axis)
        )

    def groups(self, step, size):
        return [
            [base + low + step * i for i in range(size)]
            for base in range(0, self.count, step * size)
            for low in range(step)
        ]

    def pick(self, array, dim, value):
        return lax.dynamic_index_in_dim(array, value, dim, keepdims=False, allow_negative_indices=False)


class Gather:
    def __init__(self, exchange, mine, sent, together=False):
        self.exchange = exchange
        self.mine, self.sent = mine, sent
        self.hops = ["pair"] + (["far"] if together else exchange.rest[::-1]) + ["near", "last", "core"]
        self.place = 0

    def spread(self):
        ex = self.exchange
        self.hops = ["core"]
        self.have = lax.all_gather(
            self.have, AXES, axis=0, axis_index_groups=ex.groups(2, ex.count // 2), tiled=True
        )

    def begin(self):
        ex = self.exchange
        hop = self.hops[0]
        if hop == "pair":
            self.got = ex.flip(self.sent, 0, 0)
        elif hop == "near":
            self.got = ex.flip(self.have, ex.y_bit, ex.x_bit)
        elif hop == "last":
            self.got = ex.flip(self.have, ex.x_bit, ex.y_bit)
        elif hop == "core":
            self.got = ex.flip(self.have, 0, 0)
        elif hop == "far":
            self.got = [ex.move(self.have, mask) for mask in ex.masks()[1:]]
        else:
            self.got = ex.flip(self.have, hop, hop)

    def finish(self):
        ex = self.exchange
        hop = self.hops.pop(0)
        x_value, y_value = ex.known(ex.x_bit), ex.known(ex.y_bit)
        if hop == "far":
            self.have = jnp.stack(ex.by_rest([self.have] + self.got))
        elif hop == "pair":
            self.have = ex.joined(self.mine, self.got, ex.value(0), 0)
            self.have = self.have.reshape((-1,) + self.mine.shape[1:])
            self.block = self.have.shape
        elif hop == "near":
            self.have = ex.joined(self.have, self.got, ex.by_core(y_value, x_value), 0)
        elif hop == "last":
            have = ex.joined(self.have, self.got, ex.by_core(x_value, y_value), 0)
            have = have.reshape((2,) * (ex.bits - 1) + self.block)
            wanted = list(range(ex.bits - 1, 0, -1))
            tail = [len(wanted), len(wanted) + 1]
            forms = []
            for first, second in ((ex.x_bit, ex.y_bit), (ex.y_bit, ex.x_bit)):
                now = [first, second] + ex.rest[::-1]
                forms.append(have.transpose([now.index(b) for b in wanted] + tail))
            self.have = ex.by_core(*forms).reshape((ex.count // 2) * self.block[0], self.block[1])
        elif hop == "core":
            self.halves = self.have, self.got
        else:
            self.have = ex.joined(self.have, self.got, ex.value(hop), self.place)
            self.place += 1

    def hop(self):
        self.begin()
        self.finish()


class Scatter:
    def __init__(self, exchange):
        self.exchange = exchange
        self.own, self.sent = [], []
        self.hops = ["near", "next"] + exchange.rest + ["last"]
        self.place = len(exchange.rest)

    def add(self, own, other):
        self.own.append(own)
        self.sent.append(self.exchange.flip(other, 0, 0))

    def merge(self):
        parts = [(a.astype(FULL) + b.astype(FULL)).astype(LOW) for a, b in zip(self.own, self.sent)]
        view = parts[0] if len(parts) == 1 else jnp.concatenate(parts, axis=1)
        self.have = view.reshape((2,) * (self.exchange.bits - 1) + (-1, view.shape[1]))

    def part(self, x_now, y_now):
        ex = self.exchange
        bits = list(range(ex.bits - 1, 0, -1))
        dim_x, dim_y = bits.index(ex.x_bit), bits.index(ex.y_bit)
        even = ex.pick(jnp.moveaxis(self.have, (dim_x, dim_y), (0, 1)), 0, x_now)
        odd = ex.pick(jnp.moveaxis(self.have, (dim_y, dim_x), (0, 1)), 0, y_now)
        return ex.by_core(even, odd)

    def begin(self):
        ex = self.exchange
        hop = self.hops[0]
        x_value, y_value = ex.known(ex.x_bit), ex.known(ex.y_bit)
        if hop == "near":
            self.sent_now = self.part(1 - x_value, 1 - y_value)
            self.got = ex.flip(self.sent_now, ex.x_bit, ex.y_bit)
        elif hop == "next":
            value = ex.by_core(y_value, x_value)
            self.sent_now = ex.pick(self.have, 0, 1 - value).astype(LOW)
            self.got = ex.flip(self.sent_now, ex.y_bit, ex.x_bit)
        elif hop == "last":
            view = self.have.reshape(2, -1, self.have.shape[-1])
            self.sent_now = ex.pick(view, 0, 1 - ex.value(0)).astype(LOW)
            self.got = ex.flip(self.sent_now, 0, 0)
        else:
            self.place -= 1
            self.sent_now = ex.pick(self.have, self.place, 1 - ex.value(hop)).astype(LOW)
            self.got = ex.flip(self.sent_now, hop, hop)

    def finish(self):
        ex = self.exchange
        hop = self.hops.pop(0)
        x_value, y_value = ex.known(ex.x_bit), ex.known(ex.y_bit)
        if hop == "last":
            self.mine = ex.pick(self.have.reshape(2, -1, self.have.shape[-1]), 0, ex.value(0))
            return
        got = self.got.astype(FULL)
        if hop == "near":
            self.have = self.part(x_value, y_value).astype(FULL) + got
        elif hop == "next":
            self.have = ex.pick(self.have, 0, ex.by_core(y_value, x_value)) + got
        else:
            self.have = ex.pick(self.have, self.place, ex.value(hop)) + got

    def hop(self):
        self.begin()
        self.finish()


class Reduce:
    def __init__(self, exchange):
        self.exchange = exchange
        self.own, self.sent, self.planes = [], [], []
        self.far = 4
        self.near = exchange.count // 2 // self.far
        self.hops = [exchange.bits - 2, exchange.bits - 1, "last"]

    def add(self, own, other):
        self.own.append(own)
        self.sent.append(self.exchange.flip(other, 0, 0))

    def merge(self):
        parts = [a.astype(FULL) + b.astype(FULL) for a, b in zip(self.own, self.sent)]
        self.own, self.sent = [], []
        view = parts[0] if len(parts) == 1 else jnp.concatenate(parts, axis=-1)
        width = view.shape[-1]
        view = view.astype(LOW)
        if view.ndim == 2:
            view = view.reshape(self.far, self.near, -1, width).transpose(1, 0, 2, 3)
        self.merged = view.reshape(-1, width)

    def plane(self):
        groups = self.exchange.groups(2, self.near)
        self.planes.append(
            lax.psum_scatter(self.merged, AXES, scatter_dimension=0, axis_index_groups=groups, tiled=True)
        )

    def line(self):
        ex = self.exchange
        self.hops = ["last"]
        groups = ex.groups(2 * self.near, self.far)
        self.have = lax.psum_scatter(
            self.planes.pop(), AXES, scatter_dimension=0, axis_index_groups=groups, tiled=True
        )

    def begin(self):
        ex = self.exchange
        hop = self.hops[0]
        if self.planes:
            views = [p.reshape(2, 2, p.shape[0] // 4, p.shape[1]) for p in self.planes]
            self.have = views[0] if len(views) == 1 else jnp.concatenate(views, axis=3)
            self.planes = []
        if hop == "last":
            view = self.have.reshape(2, -1, self.have.shape[-1])
            self.sent_now = ex.pick(view, 0, 1 - ex.value(0)).astype(LOW)
            self.mine = ex.pick(view, 0, ex.value(0))
            self.got = ex.flip(self.sent_now, 0, 0)
        else:
            self.sent_now = ex.pick(self.have, len(self.hops) - 2, 1 - ex.value(hop)).astype(LOW)
            self.got = ex.flip(self.sent_now, hop, hop)

    def finish(self):
        ex = self.exchange
        hop = self.hops.pop(0)
        if hop != "last":
            self.have = ex.pick(self.have, len(self.hops) - 1, ex.value(hop)).astype(FULL) + self.got.astype(FULL)


def matmul(left, right, left_dim=1, right_dim=0):
    return lax.dot_general(
        left, right, (((left_dim,), (right_dim,)), ((), ())), preferred_element_type=FULL
    )


def cost(flops, moved, transcendentals=0):
    return pl.CostEstimate(flops=flops, bytes_accessed=moved, transcendentals=transcendentals)


def whole(shape):
    return pl.BlockSpec(shape, lambda *_: (0,) * len(shape), pipeline_mode=pl.Buffered(1))


def kept_block(shape):
    return pl.BlockSpec(shape, lambda *_: (0,) * len(shape))


def anywhere():
    return pl.BlockSpec(memory_space=pl.ANY)


def call(exchange, name, body, grid, ins, outs, scratch=(), work=None, onto=(), later_than=()):
    count_in, count_gone = len(ins), len(onto) + len(later_than)

    def kernel(index_ref, *refs):
        given = refs[:count_in]
        rest = refs[count_in + count_gone :]
        token_ref, results = rest[0], rest[1:]
        token_ref[0] = index_ref[0]
        body(index_ref, *given, *results)

    def out(shape, kind, place=None):
        return jax.ShapeDtypeStruct(shape, kind) if place is None else place(shape, kind)

    results = pl.pallas_call(
        kernel,
        grid_spec=pltpu.PrefetchScalarGridSpec(
            num_scalar_prefetch=1,
            grid=grid,
            in_specs=[spec for _, spec in ins] + [anywhere()] * count_gone,
            out_specs=[pl.BlockSpec(memory_space=pltpu.SMEM)] + [o[2] for o in outs],
            scratch_shapes=list(scratch),
        ),
        out_shape=[out((1,), jnp.int32)] + [out(o[0], o[1], *o[3:]) for o in outs],
        input_output_aliases={1 + count_in + i: 1 + i for i in range(len(onto))},
        compiler_params=pltpu.CompilerParams(vmem_limit_bytes=ROOM.get(name, 18) * MEGA),
        cost_estimate=work,
        name=name,
    )(exchange.index, *[a for a, _ in ins], *onto, *later_than)
    exchange.index = results[0]
    return results[1:]


def far(array):
    return pltpu.with_memory_space_constraint(array, pltpu.HBM)


def gate(exchange, *arrays):
    call(exchange, "gate", lambda index_ref: None, (1,), [], [], work=cost(1, 1), later_than=arrays)


def hold(exchange, array, later_than=()):
    return call(
        exchange, "hold", lambda index_ref, array_ref: None, (1,), [], [(array.shape, array.dtype, anywhere())],
        work=cost(1, 1), onto=[array], later_than=later_than,
    )[0]


def norm_stats(mixed):
    average = jnp.mean(mixed, axis=-1, keepdims=True)
    centered = mixed - average
    inv_std = lax.rsqrt(jnp.mean(centered * centered, axis=-1, keepdims=True) + NORM_EPS)
    return centered * inv_std, inv_std


def norm_pull(grad_out, normed, inv_std, gain):
    scaled = grad_out * gain
    return inv_std * (
        scaled
        - jnp.mean(scaled, axis=-1, keepdims=True)
        - normed * jnp.mean(scaled * normed, axis=-1, keepdims=True)
    )


def head_lanes(pair, head):
    lane = lax.broadcasted_iota(jnp.int32, pair.shape, 1)
    mine = (lane < HEAD_DIM) if head % 2 == 0 else (lane >= HEAD_DIM)
    return jnp.where(mine, pair, jnp.zeros((), pair.dtype))


def column_copies(core, own, other, first, target, sems):
    half = target.shape[1] // 2
    copies = []
    for i, (source, place) in enumerate(((own, core), (other, 1 - core))):
        at = pl.multiple_of(place * half, LANES)
        copies.append(
            pltpu.make_async_copy(
                source.at[:, first : first + half], target.at[:, pl.ds(at, half)], sems.at[i]
            )
        )
    return copies


def attend_kernel(index_ref, own_ref, other_ref, x_ref, seg_ref, comp_ref, proj_ref,
                  q_ref, k_ref, v_ref, ck_ref, cv_ref, lse_ref, ctx_ref, ctx_t, weights, sems):
    width = x_ref.shape[2]
    heads = width // HEAD_DIM
    copies = [
        column_copies(index_ref[0] & 1, own_ref, other_ref, kind * (width // 2), weights.at[kind], sems.at[kind])
        for kind in range(3)
    ]
    first = pl.program_id(0) == 0

    @pl.when(first)
    def _():
        for copy in sum(copies, []):
            copy.start()

    def arrive(kind):
        @pl.when(first)
        def _():
            for copy in copies[kind]:
                copy.wait()

    x = x_ref[0]
    arrive(0)
    q_ref[0] = matmul(x, weights[0]).astype(LOW)
    arrive(1)
    k_ref[0] = matmul(x, weights[1]).astype(LOW)
    arrive(2)
    v_ref[0] = matmul(x, weights[2]).astype(LOW)
    member = comp_ref[0] == seg_ref[0]
    masked = jnp.where(member, proj_ref[...], jnp.zeros((), LOW))
    ck_ref[0] = (matmul(masked, k_ref[0])).astype(LOW)
    cv = matmul(masked, v_ref[0])
    cv_ref[0] = cv.astype(LOW)
    cv_t = cv.T.astype(LOW)
    for head in range(heads):
        lanes = slice(head // 2 * LANES, head // 2 * LANES + LANES)
        rows = slice(head * HEAD_DIM, (head + 1) * HEAD_DIM)
        keys = head_lanes(ck_ref[0, :, lanes], head) * (HEAD_DIM ** -0.5)
        scores = matmul(keys.astype(LOW), q_ref[0, :, lanes], 1, 1)
        scores = jnp.where(member, scores, MASKED)
        highest = jnp.max(scores, axis=0, keepdims=True)
        weight = jnp.exp(scores - highest)
        total = jnp.sum(weight, axis=0, keepdims=True)
        lse_ref[0, head : head + 1, :] = highest + jnp.log(total)
        probs = (weight * (1.0 / total)).astype(LOW)
        ctx_t[rows, :] = matmul(cv_t[rows, :], probs)
    ctx_ref[0] = ctx_t[...].T.astype(LOW)


def attend(exchange, halves, x, seg, comp, proj, later_than):
    rows, length, width = x.shape
    slots = comp.shape[1]
    heads = width // HEAD_DIM

    def at(*shape):
        return pl.BlockSpec((1,) + shape, lambda i, _: (i, 0, 0))

    tokens = ((rows, length, width), LOW, at(length, width), pltpu.HBM)
    comps = ((rows, slots, width), LOW, at(slots, width), pltpu.HBM)
    flops = rows * (length * width * (2 * 3 * width + 4 * slots * 4) + slots * length * width * 4)
    return call(
        exchange, "attend", attend_kernel, (rows,),
        [(halves[0], anywhere()), (halves[1], anywhere()), (far(x), at(length, width)), (seg[:, None, :], at(1, length)),
         (comp[:, :, None], at(slots, 1)), (proj, whole((slots, length)))],
        [tokens] * 3 + [comps] * 2 + [((rows, heads, length), FULL, at(heads, length), pltpu.HBM), tokens],
        [pltpu.VMEM((width, length), FULL), pltpu.VMEM((3, width, width), LOW), pltpu.SemaphoreType.DMA((3, 2))],
        cost(flops, 20 * 10**6, rows * heads * slots * length), (), later_than,
    )


def mix_kernel(index_ref, own_ref, other_ref, x_ref, ctx_ref, gains_ref, normed_ref, inv_ref, low_ref, same_ref, weight, sems):
    @pl.when(pl.program_id(0) == 0)
    def _():
        first = own_ref.shape[1] - weight.shape[1] // 2
        copies = column_copies(index_ref[0] & 1, own_ref, other_ref, first, weight, sems)
        for copy in copies:
            copy.start()
        for copy in copies:
            copy.wait()

    mixed = x_ref[...].astype(FULL) + matmul(ctx_ref[...], weight[...])
    normed, inv_std = norm_stats(mixed)
    normed_ref[...] = normed
    inv_ref[...] = inv_std
    low_ref[...] = (normed * gains_ref[0:1].astype(FULL) + gains_ref[1:2].astype(FULL)).astype(LOW)
    same_ref[...] = low_ref[...]


def mix(exchange, halves, x, ctx, gains, later_than, tile=256):
    tokens, width = x.shape

    def some(n):
        return pl.BlockSpec((tile, n), lambda i, _: (i, 0))

    return call(
        exchange, "mix", mix_kernel, (tokens // tile,),
        [(halves[0], anywhere()), (halves[1], anywhere()), (far(x), some(width)), (far(ctx), some(width)),
         (gains, whole(gains.shape))],
        [((tokens, width), FULL, some(width), pltpu.HBM), ((tokens, 1), FULL, some(1), pltpu.HBM),
         ((tokens, width), LOW, some(width)), ((tokens, width), LOW, some(width), pltpu.HBM)],
        [pltpu.VMEM((width, width), LOW), pltpu.SemaphoreType.DMA((2,))],
        cost(2 * tokens * width * width, 10 * 10**6), (), later_than,
    )


def gelu_pair(h):
    t = pl.reciprocal(1.0 + (0.3275911 * 0.5**0.5) * jnp.abs(h), approx=True)
    bell = jnp.exp2(h * (h * (-0.5 * 1.4426950408889634)))
    poly = 0.127414796 + t * (-0.142248368 + t * (0.7107068705 + t * (-0.7265760135 + t * 0.5307027145)))
    tail = poly * (t * bell)
    cdf = jnp.where(h >= 0, 1.0 - tail, tail)
    return h * cdf, cdf + h * (bell * 0.3989422804014327)


def up_kernel(index_ref, f_ref, w_ref, act_ref, slope_ref):
    value, slope = gelu_pair(matmul(f_ref[...], w_ref[...]))
    act_ref[...] = value.astype(LOW)
    slope_ref[...] = slope


def up_part(exchange, f, half, mine, ff, onto, later_than, tile=768):
    tokens, width = f.shape
    steps = ff // tile // 2

    def place(j, index_ref):
        core = index_ref[0] & 1
        return (0, (core if mine else 1 - core) * steps + j)

    out = pl.BlockSpec((tokens, tile), place)
    return call(
        exchange, "up_part", up_kernel, (steps,),
        [(f, whole((tokens, width))), (half, pl.BlockSpec((width, tile), lambda j, _: (0, j)))],
        [((tokens, ff), LOW, out, pltpu.HBM), ((tokens, ff), FULL, out, pltpu.HBM)],
        (), cost(tokens * width * ff, 13 * 10**6, tokens * ff // 2), onto, later_than,
    )


def down_kernel(index_ref, own_ref, other_ref, act_ref, normed_ref, og_ref, gains_ref,
                out_ref, g_ref, low_ref, sums_ref, weight, sems):
    @pl.when(pl.program_id(0) == 0)
    def _():
        sums_ref[...] = jnp.zeros_like(sums_ref)
        copies = column_copies(index_ref[0] & 1, own_ref, other_ref, 0, weight, sems)
        for copy in copies:
            copy.start()
        for copy in copies:
            copy.wait()

    first = normed_ref[...] * gains_ref[0:1].astype(FULL) + gains_ref[1:2].astype(FULL)
    normed, inv_std = norm_stats(first + matmul(act_ref[...], weight[...]))
    out_ref[...] = (normed * gains_ref[2:3].astype(FULL) + gains_ref[3:4].astype(FULL)).astype(LOW)
    top = og_ref[...].astype(FULL)
    grad = norm_pull(top, normed, inv_std, gains_ref[2:3].astype(FULL))
    g_ref[...] = grad
    low_ref[...] = grad.astype(LOW)
    sums_ref[0:1] += jnp.sum(top * normed, axis=0, keepdims=True)
    sums_ref[1:2] += jnp.sum(top, axis=0, keepdims=True)


def down_part(exchange, halves, act, normed, og, gains, later_than, tile=256):
    tokens, ff = act.shape
    width = normed.shape[1]

    def some(n):
        return pl.BlockSpec((tile, n), lambda i, _: (i, 0))

    return call(
        exchange, "down_part", down_kernel, (tokens // tile,),
        [(halves[0], anywhere()), (halves[1], anywhere()), (far(act), some(ff)), (far(normed), some(width)), (far(og), some(width)),
         (gains, whole(gains.shape))],
        [((tokens, width), LOW, some(width), pltpu.HBM), ((tokens, width), FULL, some(width), pltpu.HBM),
         ((tokens, width), LOW, some(width)), ((8, width), FULL, kept_block((8, width)))],
        [pltpu.VMEM((ff, width), LOW), pltpu.SemaphoreType.DMA((2,))],
        cost(2 * tokens * width * ff, 23 * 10**6), (), later_than,
    )


def split_columns(index_ref, total, own_ref, other_ref):
    half = total.shape[1] // 2
    left, right = total[:, :half].astype(LOW), total[:, half:].astype(LOW)
    even = (index_ref[0] & 1) == 0
    store_rows(own_ref, jnp.where(even, left, right))
    store_rows(other_ref, jnp.where(even, right, left))


def store_rows(ref, rows):
    if len(ref.shape) == 2:
        ref[...] = rows
        return
    near, far_count = ref.shape[:2]
    parts = rows.reshape((far_count, near) + ref.shape[2:])
    for i in range(far_count):
        ref[:, i] = parts[i]


def by_plane(exchange, rows):
    far_count = 4
    chips = exchange.count // 2
    each = rows // chips
    return (chips // far_count, far_count, each) if each % 16 == 0 else None


def outer_kernel(index_ref, left_ref, *refs):
    *right_refs, own_ref, other_ref = refs
    for kind, right_ref in enumerate(right_refs):

        @pl.when(pl.program_id(0) == kind)
        def _(right_ref=right_ref):
            split_columns(index_ref, matmul(left_ref[...], right_ref[...], 0, 0), own_ref, other_ref)


def outer_part(exchange, left, rights, name, later_than, planes=False):
    tokens, depth = left.shape
    width = rights[0].shape[1]
    half = ((depth, len(rights) * width // 2), LOW, pl.BlockSpec((depth, width // 2), lambda j, _: (0, j)))
    plane = by_plane(exchange, depth)
    if planes and plane:
        spec = pl.BlockSpec(plane + (width // 2,), lambda j, _: (0, 0, 0, j))
        half = (plane + (len(rights) * width // 2,), LOW, spec)
    return call(
        exchange, name, outer_kernel, (len(rights),),
        [(far(left), whole((tokens, depth)))] + [(far(r) if planes else r, whole((tokens, width))) for r in rights],
        [half] * 2, (), cost(2 * tokens * depth * width * len(rights), 9 * 10**6), (), later_than,
    )


def down_grad_kernel(index_ref, act_ref, g_ref, own_ref, other_ref):
    split_columns(index_ref, matmul(act_ref[...], g_ref[...], 0, 0), own_ref, other_ref)


def down_grad_part(exchange, act, g, later_than, tile=768):
    tokens, ff = act.shape
    width = g.shape[1]
    half = ((ff, width // 2), LOW, pl.BlockSpec((tile, width // 2), lambda j, _: (j, 0)))
    plane = by_plane(exchange, ff)
    if plane and ff // plane[1] == tile:
        spec = pl.BlockSpec((plane[0], 1, plane[2], width // 2), lambda j, _: (0, j, 0, 0))
        half = (plane + (width // 2,), LOW, spec)
    return call(
        exchange, "down_grad_part", down_grad_kernel, (ff // tile,),
        [(far(act), pl.BlockSpec((tokens, tile), lambda j, _: (0, j))), (g, whole((tokens, width)))],
        [half] * 2, (), cost(2 * tokens * width * ff, 13 * 10**6), (), later_than,
    )


def ff_back_kernel(index_ref, down_own, down_other, up_own, up_other, slope_ref, low_ref, f_ref, start_ref, normed_ref,
                   inv_ref, gains_ref, *refs):
    own_ref, other_ref, g_one_ref, g_one_low_ref, sums_ref, total, w_down, normed, start, sems = refs
    step = pl.program_id(0)
    steps = pl.num_programs(0)
    half = steps // 2
    core = index_ref[0] & 1
    tile = slope_ref.shape[1]

    def copies(at):
        place = jnp.where(at < half, (1 - core) * half + at, core * half + at - half)
        rows = pl.ds(pl.multiple_of(place * tile, tile), tile)
        return column_copies(core, down_own.at[rows], down_other.at[rows], 0, w_down.at[at % 2], sems.at[at % 2])

    late = [
        pltpu.make_async_copy(normed_ref, normed, sems.at[2, 0]),
        pltpu.make_async_copy(start_ref, start, sems.at[2, 1]),
    ]

    @pl.when(step == 0)
    def _():
        for copy in copies(step):
            copy.start()
        for copy in late:
            copy.start()
        total[...] = jnp.zeros_like(total)

    @pl.when(step < steps - 1)
    def _():
        for copy in copies(step + 1):
            copy.start()

    for copy in copies(step):
        copy.wait()

    back = (matmul(low_ref[...], w_down[step % 2], 1, 1) * slope_ref[...]).astype(LOW)
    grads = matmul(f_ref[...], back, 0, 0).astype(LOW)
    pl.when(step < half)(lambda: store_rows(other_ref, grads))
    pl.when(step >= half)(lambda: store_rows(own_ref, grads))

    def add(up_ref):
        total[...] += matmul(back, up_ref[...], 1, 1)

    pl.when(step < half)(lambda: add(up_other))
    pl.when(step >= half)(lambda: add(up_own))

    @pl.when(step == steps - 1)
    def _():
        for copy in late:
            copy.wait()
        top = total[...] + start[...]
        grad = norm_pull(top, normed[...], inv_ref[...], gains_ref[0:1].astype(FULL))
        g_one_ref[...] = grad
        g_one_low_ref[...] = grad.astype(LOW)
        sums_ref[...] = jnp.zeros_like(sums_ref)
        sums_ref[0:1] = jnp.sum(top * normed[...], axis=0, keepdims=True)
        sums_ref[1:2] = jnp.sum(top, axis=0, keepdims=True)


def ff_back(exchange, down, up, slope, low, f, start, normed, inv, gains, later_than, tile=768):
    tokens, ff = slope.shape
    width = f.shape[1]
    steps = ff // tile
    half = steps // 2

    def place(j, index_ref):
        core = index_ref[0] & 1
        return (0, jnp.where(j < half, (1 - core) * half + j, core * half + j - half))

    full = whole((tokens, width))
    result = kept_block((tokens, width))
    shape = by_plane(exchange, width) or (width,)

    def columns(place):
        return pl.BlockSpec(shape + (tile,), lambda j, _: (0,) * len(shape) + (place(j),))

    return call(
        exchange, "ff_back", ff_back_kernel, (steps,),
        [(far(down[0]), anywhere()), (far(down[1]), anywhere()),
         (up[0], pl.BlockSpec((width, tile), lambda j, _: (0, jnp.maximum(j - half, 0)))),
         (up[1], pl.BlockSpec((width, tile), lambda j, _: (0, jnp.minimum(j, half - 1)))),
         (far(slope), pl.BlockSpec((tokens, tile), place)),
         (far(low), full), (far(f), full), (far(start), anywhere()), (far(normed), anywhere()), (far(inv), whole(inv.shape)), (gains, whole(gains.shape))],
        [(shape + (ff // 2,), LOW, columns(lambda j: jnp.maximum(j - half, 0))),
         (shape + (ff // 2,), LOW, columns(lambda j: jnp.minimum(j, half - 1)))]
        + [((tokens, width), FULL, result, pltpu.HBM), ((tokens, width), LOW, result, pltpu.HBM),
         ((8, width), FULL, kept_block((8, width)))],
        [pltpu.VMEM((tokens, width), FULL), pltpu.VMEM((2, tile, width), LOW), pltpu.VMEM((tokens, width), FULL),
         pltpu.VMEM((tokens, width), FULL),
         pltpu.SemaphoreType.DMA((3, 2))],
        cost(6 * tokens * width * ff, 40 * 10**6), (), later_than,
    )


def attend_back_kernel(index_ref, own_ref, other_ref, g_ref, q_ref, k_ref, v_ref, ck_ref, cv_ref, lse_ref,
                       seg_ref, comp_ref, proj_ref,
                       gq_ref, gk_ref, gv_ref, grad_ref, gctx, gq_t, gck, gcv, weight, sems):
    width = q_ref.shape[2]
    heads = width // HEAD_DIM
    scale = HEAD_DIM ** -0.5

    @pl.when(pl.program_id(0) == 0)
    def _():
        copies = column_copies(
            index_ref[0] & 1, own_ref, other_ref, own_ref.shape[1] - width // 2, weight, sems
        )
        for copy in copies:
            copy.start()
        for copy in copies:
            copy.wait()

    gctx[...] = matmul(g_ref[0], weight[...], 1, 1).astype(LOW)
    member = comp_ref[0] == seg_ref[0]
    ck_t = ck_ref[0].astype(FULL).T.astype(LOW)
    for pair in range(heads // 2):
        lanes = slice(pair * LANES, pair * LANES + LANES)
        queries, grads = q_ref[0, :, lanes], gctx[:, lanes]
        key_parts, value_parts = [], []
        for head in (2 * pair, 2 * pair + 1):
            rows = slice(head * HEAD_DIM, (head + 1) * HEAD_DIM)
            keys = head_lanes(ck_ref[0, :, lanes], head) * scale
            scores = matmul(keys.astype(LOW), queries, 1, 1)
            probs = jnp.exp(jnp.where(member, scores - lse_ref[0, head : head + 1, :], MASKED))
            grad_probs = matmul(head_lanes(cv_ref[0, :, lanes], head), grads, 1, 1)
            delta = jnp.sum(probs * grad_probs, axis=0, keepdims=True)
            grad_scores = (probs * (grad_probs - delta)).astype(LOW)
            gq_t[rows, :] = matmul(ck_t[rows, :], grad_scores) * scale
            key_parts.append(matmul(grad_scores, queries))
            value_parts.append(matmul(probs.astype(LOW), grads))
        lane = lax.broadcasted_iota(jnp.int32, key_parts[0].shape, 1) < HEAD_DIM
        gck[:, lanes] = (jnp.where(lane, *key_parts) * scale).astype(LOW)
        gcv[:, lanes] = jnp.where(lane, *value_parts).astype(LOW)
    gq_ref[...] = gq_t[...].T.astype(LOW)
    masked = jnp.where(member, proj_ref[...], jnp.zeros((), LOW))
    gk_ref[...] = matmul(masked, gck[...], 0, 0).astype(LOW)
    gv_ref[...] = matmul(masked, gcv[...], 0, 0).astype(LOW)
    part = matmul(gck[...], k_ref[0], 1, 1) + matmul(gcv[...], v_ref[0], 1, 1)
    part = jnp.where(member, part, 0.0)

    @pl.when(pl.program_id(0) == 0)
    def _():
        grad_ref[...] = part

    @pl.when(pl.program_id(0) > 0)
    def _():
        grad_ref[...] += part


def attend_back(exchange, halves, g, kept, seg, comp, proj, later_than):
    q, k, v, ck, cv, lse = kept
    rows, length, width = q.shape
    slots = comp.shape[1]
    heads = width // HEAD_DIM

    def at(*shape):
        return pl.BlockSpec((1,) + shape, lambda i, _: (i, 0, 0))

    tokens = ((rows * length, width), LOW, pl.BlockSpec((length, width), lambda i, _: (i, 0)))
    flops = rows * length * width * (2 * width + 4 * slots * 10)
    return call(
        exchange, "attend_back", attend_back_kernel, (rows,),
        [(far(halves[0]), anywhere()), (far(halves[1]), anywhere())] + [(a, at(length, width)) for a in (far(g), far(q), far(k), far(v))]
        + [(far(a), at(slots, width)) for a in (ck, cv)]
        + [(far(lse), at(heads, length)), (seg[:, None, :], at(1, length)), (comp[:, :, None], at(slots, 1)),
           (far(proj), whole((slots, length)))],
        [tokens] * 3 + [((slots, length), FULL, kept_block((slots, length)))],
        [pltpu.VMEM((length, width), LOW), pltpu.VMEM((width, length), FULL),
         pltpu.VMEM((slots, width), LOW), pltpu.VMEM((slots, width), LOW),
         pltpu.VMEM((width, width), LOW), pltpu.SemaphoreType.DMA((2,))],
        cost(flops, 15 * 10**6, rows * heads * slots * length), (), later_than,
    )


def input_kernel(index_ref, own_ref, other_ref, g_ref, gq_ref, gk_ref, gv_ref, out_ref, weights, sems):
    width = g_ref.shape[1]

    @pl.when(pl.program_id(0) == 0)
    def _():
        copies = []
        for kind in range(3):
            copies += column_copies(
                index_ref[0] & 1, own_ref, other_ref, kind * (width // 2), weights.at[kind], sems.at[kind]
            )
        for copy in copies:
            copy.start()
        for copy in copies:
            copy.wait()

    out_ref[...] = (
        g_ref[...]
        + matmul(gq_ref[...], weights[0], 1, 1)
        + matmul(gk_ref[...], weights[1], 1, 1)
        + matmul(gv_ref[...], weights[2], 1, 1)
    )


def input_part(exchange, halves, g, gq, gk, gv, later_than, tile=256):
    tokens, width = g.shape
    some = pl.BlockSpec((tile, width), lambda i, _: (i, 0))
    return call(
        exchange, "input_part", input_kernel, (tokens // tile,),
        [(far(halves[0]), anywhere()), (far(halves[1]), anywhere())] + [(far(a), some) for a in (g, gq, gk, gv)],
        [((tokens, width), FULL, some)],
        [pltpu.VMEM((3, width, width), LOW), pltpu.SemaphoreType.DMA((3, 2))],
        cost(6 * tokens * width * width, 15 * 10**6), (), later_than,
    )[0]


def adaptive(first, second, grad):
    first_new = BETA_ONE * first + (1.0 - BETA_ONE) * grad
    second_new = BETA_TWO * second + (1.0 - BETA_TWO) * grad * grad
    direction = (
        first_new
        / (1.0 - BETA_ONE**STEP)
        / (jnp.sqrt(second_new / (1.0 - BETA_TWO**STEP)) + EPSILON)
    )
    return (first_new, second_new, direction)


def store_halves(index_ref, columns, left, right, own_ref, other_ref):
    even = (index_ref[0] & 1) == 0
    own_ref[:, columns] = jnp.where(even, left, right).astype(LOW)
    other_ref[:, columns] = jnp.where(even, right, left).astype(LOW)


def store_matrix(index_ref, columns, matrix, own_ref, other_ref):
    half = matrix.shape[1] // 2
    store_halves(index_ref, columns, matrix[:, :half], matrix[:, half:], own_ref, other_ref)


def pack_attn_kernel(index_ref, weight_ref, comp_ref, norm_ref, own_ref, other_ref, side):
    kinds = weight_ref.shape[0] - 1
    half = weight_ref.shape[2] // 2
    rows, length = comp_ref.shape
    pieces = length // side.shape[1]
    own, own_columns = norm_ref.shape
    side[...] = jnp.zeros_like(side)
    for i in range(pieces):
        side[i * rows : (i + 1) * rows, :] = comp_ref[:, i * side.shape[1] : (i + 1) * side.shape[1]]
    side[pieces * rows : pieces * rows + own, :own_columns] = norm_ref[...]
    for kind in range(kinds):
        store_matrix(index_ref, slice(kind * half, (kind + 1) * half), weight_ref[kind], own_ref, other_ref)
    store_matrix(index_ref, slice(kinds * half, None), side[...], own_ref, other_ref)


def pack_up_kernel(index_ref, weight_ref, out_ref, own_ref, other_ref):
    split = weight_ref.shape[1] // 2
    store_matrix(index_ref, slice(0, split), weight_ref[...], own_ref, other_ref)
    store_matrix(index_ref, slice(split, None), out_ref[0], own_ref, other_ref)


def pack_down_kernel(index_ref, weight_ref, own_ref, other_ref):
    store_matrix(index_ref, slice(None), weight_ref[...], own_ref, other_ref)


def squares_row(array):
    total = jnp.sum(jnp.sum(array * array, axis=0, keepdims=True), axis=1, keepdims=True)
    return jnp.broadcast_to(total, (1, LANES))


def step_matrix(weight, first, second, grad, first_ref, second_ref, direction_ref, sums_ref, row):
    first_new, second_new, direction = adaptive(first, second, grad)
    direction = direction + DECAY * weight
    first_ref[...] = first_new
    second_ref[...] = second_new
    direction_ref[...] = direction
    sums_ref[row : row + 1] = squares_row(weight)
    sums_ref[row + 8 : row + 9] = squares_row(direction)


def joined_halves(index_ref, mine, got):
    even = (index_ref[0] & 1) == 0
    return jnp.concatenate([jnp.where(even, mine, got), jnp.where(even, got, mine)], axis=1)


def down_step_kernel(index_ref, mine_ref, got_ref, weight_ref, first_ref, second_ref,
                     first_new, second_new, direction, sums_ref):
    sums_ref[...] = jnp.zeros_like(sums_ref)
    grad = joined_halves(index_ref, mine_ref[...].astype(FULL), got_ref[...].astype(FULL))
    step_matrix(weight_ref[...], first_ref[...], second_ref[...], grad, first_new, second_new, direction, sums_ref, 5)


def up_step_kernel(index_ref, mine_ref, got_ref, weight_ref, first_ref, second_ref, out_weight, out_first, out_second,
                   first_new, second_new, direction, out_first_new, out_second_new, out_direction, sums_ref):
    sums_ref[...] = jnp.zeros_like(sums_ref)
    split = weight_ref.shape[1] // 2
    mine, got = mine_ref[...].astype(FULL), got_ref[...].astype(FULL)
    grad = joined_halves(index_ref, mine[:, :split], got[:, :split])
    step_matrix(weight_ref[...], first_ref[...], second_ref[...], grad, first_new, second_new, direction, sums_ref, 4)
    grad = joined_halves(index_ref, mine[:, split:], got[:, split:])
    step_matrix(out_weight[0], out_first[0], out_second[0], grad,
                out_first_new, out_second_new, out_direction, sums_ref, 3)


def attn_step_kernel(index_ref, mine_ref, got_ref, weight_ref, first_ref, second_ref,
                     comp_weight, comp_first, comp_second, norm_weight, norm_first, norm_second,
                     out_first_new, up_sums, down_sums,
                     first_new, second_new, direction, comp_first_new, comp_second_new, comp_direction,
                     norm_first_new, norm_second_new, norm_new, sent_ref, sums_ref):
    sums_ref[...] = up_sums[...] + down_sums[...]
    kinds = weight_ref.shape[0] - 1
    width = weight_ref.shape[2]
    half = width // 2
    mine, got = mine_ref[...].astype(FULL), got_ref[...].astype(FULL)
    for kind in range(kinds):
        columns = slice(kind * half, (kind + 1) * half)
        grad = joined_halves(index_ref, mine[:, columns], got[:, columns])
        step_matrix(weight_ref[kind], first_ref[kind], second_ref[kind], grad,
                    first_new.at[kind], second_new.at[kind], direction.at[kind], sums_ref, kind)
    first_new[kinds] = out_first_new[...]
    side = joined_halves(index_ref, mine[:, kinds * half :], got[:, kinds * half :])
    rows, length = comp_weight.shape
    pieces = length // side.shape[1]
    grad = jnp.concatenate([side[i * rows : (i + 1) * rows] for i in range(pieces)], axis=1)
    step_matrix(comp_weight[...], comp_first[...], comp_second[...], grad,
                comp_first_new, comp_second_new, comp_direction, sums_ref, 6)
    own, own_columns = norm_weight.shape
    grad = side[pieces * rows : pieces * rows + own, :own_columns]
    new, newer, way = adaptive(norm_first[...], norm_second[...], grad)
    norm_first_new[...] = new
    norm_second_new[...] = newer
    norm_new[...] = norm_weight[...] - RATE * way
    sent_ref[...] = jnp.broadcast_to(sums_ref[...][None], sent_ref.shape)


def finish_kernel(index_ref, got_ref, weight_ref, direction_ref, out_direction, up_weight, up_direction,
                  down_weight, down_direction, comp_weight, comp_direction,
                  attn_new, attn_copy, up_new, up_copy, down_new, down_copy, comp_new, comp_copy, norms_ref):
    totals = jnp.sqrt(jnp.sum(got_ref[...], axis=0))
    lane = lax.broadcasted_iota(jnp.int32, (1, LANES), 1)
    count = norms_ref.shape[1]
    for i in range(2):
        row = sum(jnp.where(lane == m, totals[8 * i + m : 8 * i + m + 1], 0.0) for m in range(count))
        norms_ref[i : i + 1, :] = row[:, :count]
    ratio = totals[:8] / (totals[8:] + EPSILON)

    def move(weight, direction, matrix, new_ref, copy_ref):
        new = weight - RATE * ratio[matrix : matrix + 1, :1] * direction
        new_ref[...] = new
        copy_ref[...] = new.astype(LOW)

    for kind in range(4):
        way = direction_ref[kind] if kind < 3 else out_direction[...]
        move(weight_ref[kind], way, kind, attn_new.at[kind], attn_copy.at[kind])
    move(up_weight[...], up_direction[...], 4, up_new, up_copy)
    move(down_weight[...], down_direction[...], 5, down_new, down_copy)
    move(comp_weight[...], comp_direction[...], 6, comp_new, comp_copy)


def elementwise(exchange, name, body, ins, shapes, later_than=(), scratch=()):
    pairs = []
    for a in ins:
        if isinstance(a, tuple):
            shape, kind = (1,) + a[0].shape[1:], a[1]
            pairs.append((far(a[0]), pl.BlockSpec(shape, lambda *_, kind=kind: (kind, 0, 0))))
        else:
            pairs.append((far(a) if name.startswith("pack") else a, whole(a.shape)))
    return call(
        exchange, name, body, (1,), pairs, [(shape, kind, whole(shape)) for shape, kind in shapes], scratch,
        cost(10**6, sum(a.size * 4 for a, _ in pairs)), (), later_than,
    )


def local(
    dp,
    fsdp,
    inputs,
    segment_ids,
    compressed_segment,
    out_grad,
    attn_weight,
    attn_first,
    attn_second,
    up_weight,
    up_first,
    up_second,
    down_weight,
    down_first,
    down_second,
    compress_weight,
    compress_first,
    compress_second,
    norm_params,
    norm_first,
    norm_second,
):
    exchange = Exchange(dp, fsdp)
    devices = dp * fsdp
    row_count, length, model_width = inputs.shape
    half_width = model_width // 2
    token_count = row_count * length
    norm_kinds, norm_own = norm_params.shape
    attn_kinds, attn_own, _ = attn_weight.shape
    compress_own = compress_weight.shape[0]
    pieces = 2 if 2 * compress_own + norm_kinds <= attn_own else 1
    side_width = length // pieces

    def side_rows(compress_part, norm_part):
        none = [(0, 0)] * (compress_part.ndim - 2)
        spare = attn_own - pieces * compress_own - norm_kinds
        norm_part = jnp.pad(norm_part, none + [(0, spare), (0, side_width - norm_own)])
        parts = [compress_part[..., i * side_width : (i + 1) * side_width] for i in range(pieces)]
        return jnp.concatenate(parts + [norm_part], axis=-2)

    def halves(array):
        middle = array.shape[-1] // 2
        return array[..., :middle], array[..., middle:]

    flat_in = inputs.reshape(token_count, model_width)
    ff = up_weight.shape[1]
    out_kind = attn_kinds - 1
    out_at = [(a, out_kind) for a in (attn_weight, attn_first, attn_second)]
    attn = Gather(
        exchange,
        *elementwise(
            exchange, "pack_attn", pack_attn_kernel, [attn_weight, compress_weight, norm_params],
            [((attn_own, out_kind * half_width + side_width // 2), LOW)] * 2, (),
            [pltpu.VMEM((attn_own, side_width), FULL)],
        ),
    )
    attn.begin()
    up = Gather(
        exchange,
        *elementwise(
            exchange, "pack_up", pack_up_kernel, [up_weight, out_at[0]],
            [((attn_own, (ff + model_width) // 2), LOW)] * 2, [attn.mine],
        ),
    )
    up.begin()
    attn.finish()
    attn.begin()
    up.finish()
    up.have = hold(exchange, up.have)
    up.spread()
    attn.finish()
    for _ in exchange.rest[1:]:
        attn.hop()
    attn.hop()
    attn.hop()
    attn.begin()
    down = Gather(
        exchange,
        *elementwise(
            exchange, "pack_down", pack_down_kernel, [down_weight], [((down_weight.shape[0], half_width), LOW)] * 2,
            [attn.have],
        ),
        together=True,
    )
    down.hop()
    down.begin()
    attn.finish()
    side_own, side_other = [part[:, -side_width // 2 :] for part in attn.halves]
    side = jnp.concatenate(
        [exchange.by_core(side_own, side_other), exchange.by_core(side_other, side_own)], axis=1
    ).reshape(devices, attn_own, side_width)
    compress_full = jnp.concatenate(
        [side[:, i * compress_own : (i + 1) * compress_own] for i in range(pieces)], axis=2
    ).reshape(-1, length)
    gains = (
        side[:, pieces * compress_own : pieces * compress_own + norm_kinds, :norm_own]
        .transpose(1, 0, 2)
        .reshape(norm_kinds, model_width)
    )

    *kept, context = attend(
        exchange, attn.halves, inputs, segment_ids, compressed_segment, compress_full, [down.have]
    )
    context = context.reshape(token_count, model_width)
    down.finish()
    down.begin()
    up.have = hold(exchange, up.have, [down.have])
    up.begin()
    up.finish()
    first_normed, first_inv, first_low, first_low_far = mix(exchange, up.halves, flat_in, context, gains, [down.have])
    down.finish()
    down.begin()
    hidden = up_part(exchange, first_low, up.halves[0], True, ff, (), [down.have])
    down.finish()
    down.begin()
    active, slope = up_part(exchange, first_low, up.halves[1], False, ff, hidden, [down.have])
    down.finish()
    result, grad_second, grad_second_low, sums_two = down_part(
        exchange, down.halves, active, first_normed, out_grad.reshape(token_count, model_width), gains, []
    )

    down_sum, up_sum, attn_sum = Reduce(exchange), Reduce(exchange), Scatter(exchange)
    down_own, down_other = down_grad_part(exchange, active, grad_second_low, [])
    down_sum.add(down_own, down_other)
    down_sum.merge()
    up_own, up_other, grad_first, grad_first_low, sums_one = ff_back(
        exchange, down.halves, up.halves, slope, grad_second_low, first_low_far, grad_second,
        first_normed, first_inv, gains, [far(down_sum.merged)],
    )
    down_sum.plane()
    up_sum.add(up_own, up_other)
    out_own, out_other = outer_part(exchange, context, [grad_first_low], "out_grad_part", [], True)
    up_sum.add(out_own, out_other)
    up_sum.merge()
    *grads, comp_grad = attend_back(
        exchange, up.halves, grad_first_low.reshape(inputs.shape), kept,
        segment_ids, compressed_segment, compress_full, [far(up_sum.merged)] + [far(p) for p in down_sum.planes],
    )
    up_sum.plane()
    qkv_own, qkv_other = outer_part(exchange, flat_in, grads, "qkv_grad_part", [])
    norm_grad = jnp.concatenate([sums_one[:2], sums_two[:2]])
    side_grad = side_rows(
        comp_grad.reshape(devices, compress_own, length),
        norm_grad.reshape(norm_kinds, devices, norm_own).transpose(1, 0, 2),
    ).reshape(model_width, side_width).astype(LOW)
    side_left, side_right = halves(side_grad)
    attn_sum.add(qkv_own, qkv_other)
    attn_sum.add(exchange.by_core(side_left, side_right), exchange.by_core(side_right, side_left))
    attn_sum.merge()
    attn_sum.begin()
    up_sum.begin()
    input_grad = input_part(
        exchange, attn.halves, grad_first, *grads, [attn_sum.sent_now, up_sum.sent_now]
    )
    down_sum.line()

    up_sum.finish()
    up_sum.begin()
    attn_sum.finish()
    attn_sum.begin()
    gate(exchange, attn_sum.sent_now, up_sum.sent_now)
    up_sum.finish()
    up_sum.begin()
    attn_sum.finish()
    attn_sum.begin()
    gate(exchange, attn_sum.sent_now, up_sum.sent_now)
    attn_sum.finish()
    attn_sum.begin()
    out_shape = attn_weight.shape[1:]
    up_first_new, up_second_new, up_direction, out_first_new, out_second_new, out_direction, up_squares = elementwise(
        exchange, "up_step", up_step_kernel,
        [up_sum.mine, up_sum.got, up_weight, up_first, up_second] + out_at,
        [(up_weight.shape, FULL)] * 3 + [(out_shape, FULL)] * 3 + [((16, LANES), FULL)], [attn_sum.sent_now],
    )
    down_sum.begin()
    attn_sum.finish()
    attn_sum.begin()
    down_first_new, down_second_new, down_direction, down_squares = elementwise(
        exchange, "down_step", down_step_kernel,
        [down_sum.mine, down_sum.got, down_weight, down_first, down_second],
        [(down_weight.shape, FULL)] * 3 + [((16, LANES), FULL)], [attn_sum.sent_now],
    )
    attn_sum.finish()
    while attn_sum.hops:
        attn_sum.hop()
    three = (out_kind,) + out_shape
    (
        attn_first_new, attn_second_new, attn_direction,
        compress_first_new, compress_second_new, compress_direction,
        norm_first_new, norm_second_new, norm_new, sent, _,
    ) = elementwise(
        exchange, "attn_step", attn_step_kernel,
        [attn_sum.mine, attn_sum.got, attn_weight, attn_first, attn_second,
         compress_weight, compress_first, compress_second, norm_params, norm_first, norm_second,
         out_first_new, up_squares, down_squares],
        [(attn_weight.shape, FULL), (three, FULL), (three, FULL)] + [(compress_weight.shape, FULL)] * 3
        + [(norm_params.shape, FULL)] * 3 + [((devices, 16, LANES), FULL), ((16, LANES), FULL)],
    )
    got = lax.all_to_all(sent, AXES, split_axis=0, concat_axis=0, tiled=True)
    attn_new, attn_copy, up_new, up_copy, down_new, down_copy, compress_new, compress_copy, norms = elementwise(
        exchange, "finish", finish_kernel,
        [got, attn_weight, attn_direction, out_direction, up_weight, up_direction, down_weight, down_direction,
         compress_weight, compress_direction],
        [(a.shape, t) for a in (attn_weight, up_weight, down_weight, compress_weight) for t in (FULL, LOW)]
        + [((2, attn_kinds + 3), FULL)],
    )
    return (
        result.reshape(row_count, length, model_width),
        input_grad.reshape(row_count, length, model_width),
        attn_first_new,
        attn_second_new,
        out_second_new,
        attn_new,
        attn_copy,
        up_first_new,
        up_second_new,
        up_new,
        up_copy,
        down_first_new,
        down_second_new,
        down_new,
        down_copy,
        compress_first_new,
        compress_second_new,
        compress_new,
        compress_copy,
        norm_first_new,
        norm_second_new,
        norm_new,
        norms,
    )


def solution(mesh):
    rows, mid, flat = P(AXES, None), P(None, AXES, None), P(None, AXES)
    deep = P(AXES, None, None)

    def step(*args):
        return local(mesh.shape["dp"], mesh.shape["fsdp"], *args)

    return jax.shard_map(
        step,
        mesh=mesh,
        in_specs=(deep, rows, rows, deep) + (mid,) * 3 + (rows,) * 9 + (flat,) * 3,
        out_specs=(deep, deep, mid, mid, rows, mid, mid)
        + (rows,) * 12
        + (flat,) * 3
        + (P(),),
        check_vma=False,
    )
```

```python
import jax
import jax.numpy as jnp
from jax import lax
from jax.experimental import pallas as pl
from jax.experimental.pallas import tpu as pltpu
from jax.sharding import PartitionSpec as P

HEAD_DIM = 64
STEP = 10


BETA_ONE = 0.9
BETA_TWO = 0.999
EPSILON = 1e-06
DECAY = 0.01
RATE = 0.5
NORM_EPS = 1e-05
MASKED = -1e30

AXES = ("dp", "fsdp")
LOW = jnp.bfloat16
FULL = jnp.float32
MEGA = 1024 * 1024
ROOM = {"attend": 22, "attend_back": 22, "up_part": 26, "ff_back": 44, "down_part": 20}
LANES = 128


class Exchange:
    def __init__(self, dp, fsdp):
        self.count = dp * fsdp
        self.bits = self.count.bit_length() - 1
        self.x_bit = 1
        self.y_bit = fsdp.bit_length() - 1
        self.rest = [b for b in range(1, self.bits) if b not in (self.x_bit, self.y_bit)]
        self.index = lax.axis_index(AXES).astype(jnp.int32).reshape(1)
        self.first_index = self.index

    def value(self, bit):
        return (self.index[0] >> bit) & 1

    def known(self, bit):
        return (self.first_index[0] >> bit) & 1

    def flip(self, array, even_bit, odd_bit):
        pairs = [(i, i ^ (1 << (odd_bit if i & 1 else even_bit))) for i in range(self.count)]
        return lax.ppermute(array, AXES, pairs)

    def masks(self):
        return [
            sum(((k >> i) & 1) << bit for i, bit in enumerate(self.rest)) for k in range(1 << len(self.rest))
        ]

    def move(self, array, mask):
        return lax.ppermute(array, AXES, [(i, i ^ mask) for i in range(self.count)])

    def by_rest(self, pieces):
        for i, bit in enumerate(self.rest):
            turned = self.value(bit) == 1
            pieces = [jnp.where(turned, pieces[k ^ (1 << i)], p) for k, p in enumerate(pieces)]
        return pieces

    def by_core(self, even, odd):
        return jnp.where(self.value(0) == 0, even, odd)

    def joined(self, own, other, value, axis):
        return jnp.where(
            value == 0, jnp.stack([own, other], axis), jnp.stack([other, own], axis)
        )

    def groups(self, step, size):
        return [
            [base + low + step * i for i in range(size)]
            for base in range(0, self.count, step * size)
            for low in range(step)
        ]

    def pick(self, array, dim, value):
        return lax.dynamic_index_in_dim(array, value, dim, keepdims=False, allow_negative_indices=False)


class Gather:
    def __init__(self, exchange, mine, sent, together=False):
        self.exchange = exchange
        self.mine, self.sent = mine, sent
        self.hops = ["pair"] + (["far"] if together else exchange.rest[::-1]) + ["near", "last", "core"]
        self.place = 0

    def spread(self):
        ex = self.exchange
        self.hops = ["core"]
        self.have = lax.all_gather(
            self.have, AXES, axis=0, axis_index_groups=ex.groups(2, ex.count // 2), tiled=True
        )

    def begin(self):
        ex = self.exchange
        hop = self.hops[0]
        if hop == "pair":
            self.got = ex.flip(self.sent, 0, 0)
        elif hop == "near":
            self.got = ex.flip(self.have, ex.y_bit, ex.x_bit)
        elif hop == "last":
            self.got = ex.flip(self.have, ex.x_bit, ex.y_bit)
        elif hop == "core":
            self.got = ex.flip(self.have, 0, 0)
        elif hop == "far":
            self.got = [ex.move(self.have, mask) for mask in ex.masks()[1:]]
        else:
            self.got = ex.flip(self.have, hop, hop)

    def finish(self):
        ex = self.exchange
        hop = self.hops.pop(0)
        x_value, y_value = ex.known(ex.x_bit), ex.known(ex.y_bit)
        if hop == "far":
            self.have = jnp.stack(ex.by_rest([self.have] + self.got))
        elif hop == "pair":
            self.have = ex.joined(self.mine, self.got, ex.value(0), 0)
            self.have = self.have.reshape((-1,) + self.mine.shape[1:])
            self.block = self.have.shape
        elif hop == "near":
            self.have = ex.joined(self.have, self.got, ex.by_core(y_value, x_value), 0)
        elif hop == "last":
            have = ex.joined(self.have, self.got, ex.by_core(x_value, y_value), 0)
            have = have.reshape((2,) * (ex.bits - 1) + self.block)
            wanted = list(range(ex.bits - 1, 0, -1))
            tail = [len(wanted), len(wanted) + 1]
            forms = []
            for first, second in ((ex.x_bit, ex.y_bit), (ex.y_bit, ex.x_bit)):
                now = [first, second] + ex.rest[::-1]
                forms.append(have.transpose([now.index(b) for b in wanted] + tail))
            self.have = ex.by_core(*forms).reshape((ex.count // 2) * self.block[0], self.block[1])
        elif hop == "core":
            self.halves = self.have, self.got
        else:
            self.have = ex.joined(self.have, self.got, ex.value(hop), self.place)
            self.place += 1

    def hop(self):
        self.begin()
        self.finish()


class Scatter:
    def __init__(self, exchange):
        self.exchange = exchange
        self.own, self.sent = [], []
        self.hops = ["near", "next"] + exchange.rest + ["last"]
        self.place = len(exchange.rest)

    def add(self, own, other):
        self.own.append(own)
        self.sent.append(self.exchange.flip(other, 0, 0))

    def merge(self):
        parts = [(a.astype(FULL) + b.astype(FULL)).astype(LOW) for a, b in zip(self.own, self.sent)]
        view = parts[0] if len(parts) == 1 else jnp.concatenate(parts, axis=1)
        self.have = view.reshape((2,) * (self.exchange.bits - 1) + (-1, view.shape[1]))

    def part(self, x_now, y_now):
        ex = self.exchange
        bits = list(range(ex.bits - 1, 0, -1))
        dim_x, dim_y = bits.index(ex.x_bit), bits.index(ex.y_bit)
        even = ex.pick(jnp.moveaxis(self.have, (dim_x, dim_y), (0, 1)), 0, x_now)
        odd = ex.pick(jnp.moveaxis(self.have, (dim_y, dim_x), (0, 1)), 0, y_now)
        return ex.by_core(even, odd)

    def begin(self):
        ex = self.exchange
        hop = self.hops[0]
        x_value, y_value = ex.known(ex.x_bit), ex.known(ex.y_bit)
        if hop == "near":
            self.sent_now = self.part(1 - x_value, 1 - y_value)
            self.got = ex.flip(self.sent_now, ex.x_bit, ex.y_bit)
        elif hop == "next":
            value = ex.by_core(y_value, x_value)
            self.sent_now = ex.pick(self.have, 0, 1 - value).astype(LOW)
            self.got = ex.flip(self.sent_now, ex.y_bit, ex.x_bit)
        elif hop == "last":
            view = self.have.reshape(2, -1, self.have.shape[-1])
            self.sent_now = ex.pick(view, 0, 1 - ex.value(0)).astype(LOW)
            self.got = ex.flip(self.sent_now, 0, 0)
        else:
            self.place -= 1
            self.sent_now = ex.pick(self.have, self.place, 1 - ex.value(hop)).astype(LOW)
            self.got = ex.flip(self.sent_now, hop, hop)

    def finish(self):
        ex = self.exchange
        hop = self.hops.pop(0)
        x_value, y_value = ex.known(ex.x_bit), ex.known(ex.y_bit)
        if hop == "last":
            self.mine = ex.pick(self.have.reshape(2, -1, self.have.shape[-1]), 0, ex.value(0))
            return
        got = self.got.astype(FULL)
        if hop == "near":
            self.have = self.part(x_value, y_value).astype(FULL) + got
        elif hop == "next":
            self.have = ex.pick(self.have, 0, ex.by_core(y_value, x_value)) + got
        else:
            self.have = ex.pick(self.have, self.place, ex.value(hop)) + got

    def hop(self):
        self.begin()
        self.finish()


class Reduce:
    def __init__(self, exchange):
        self.exchange = exchange
        self.own, self.sent, self.planes = [], [], []
        self.far = 4
        self.near = exchange.count // 2 // self.far
        self.hops = [exchange.bits - 2, exchange.bits - 1, "last"]

    def add(self, own, other):
        self.own.append(own)
        self.sent.append(self.exchange.flip(other, 0, 0))

    def merge(self):
        parts = [a.astype(FULL) + b.astype(FULL) for a, b in zip(self.own, self.sent)]
        self.own, self.sent = [], []
        view = parts[0] if len(parts) == 1 else jnp.concatenate(parts, axis=-1)
        width = view.shape[-1]
        view = view.astype(LOW)
        if view.ndim == 2:
            view = view.reshape(self.far, self.near, -1, width).transpose(1, 0, 2, 3)
        self.merged = view.reshape(-1, width)

    def plane(self):
        groups = self.exchange.groups(2, self.near)
        self.planes.append(
            lax.psum_scatter(self.merged, AXES, scatter_dimension=0, axis_index_groups=groups, tiled=True)
        )

    def line(self):
        ex = self.exchange
        self.hops = ["last"]
        groups = ex.groups(2 * self.near, self.far)
        self.have = lax.psum_scatter(
            self.planes.pop(), AXES, scatter_dimension=0, axis_index_groups=groups, tiled=True
        )

    def begin(self):
        ex = self.exchange
        hop = self.hops[0]
        if self.planes:
            views = [p.reshape(2, 2, p.shape[0] // 4, p.shape[1]) for p in self.planes]
            self.have = views[0] if len(views) == 1 else jnp.concatenate(views, axis=3)
            self.planes = []
        if hop == "last":
            view = self.have.reshape(2, -1, self.have.shape[-1])
            self.sent_now = ex.pick(view, 0, 1 - ex.value(0)).astype(LOW)
            self.mine = ex.pick(view, 0, ex.value(0))
            self.got = ex.flip(self.sent_now, 0, 0)
        else:
            self.sent_now = ex.pick(self.have, len(self.hops) - 2, 1 - ex.value(hop)).astype(LOW)
            self.got = ex.flip(self.sent_now, hop, hop)

    def finish(self):
        ex = self.exchange
        hop = self.hops.pop(0)
        if hop != "last":
            self.have = ex.pick(self.have, len(self.hops) - 1, ex.value(hop)).astype(FULL) + self.got.astype(FULL)


def matmul(left, right, left_dim=1, right_dim=0):
    return lax.dot_general(
        left, right, (((left_dim,), (right_dim,)), ((), ())), preferred_element_type=FULL
    )


def cost(flops, moved, transcendentals=0):
    return pl.CostEstimate(flops=flops, bytes_accessed=moved, transcendentals=transcendentals)


def whole(shape):
    return pl.BlockSpec(shape, lambda *_: (0,) * len(shape), pipeline_mode=pl.Buffered(1))


def kept_block(shape):
    return pl.BlockSpec(shape, lambda *_: (0,) * len(shape))


def anywhere():
    return pl.BlockSpec(memory_space=pl.ANY)


def call(exchange, name, body, grid, ins, outs, scratch=(), work=None, onto=(), later_than=()):
    count_in, count_gone = len(ins), len(onto) + len(later_than)

    def kernel(index_ref, *refs):
        given = refs[:count_in]
        rest = refs[count_in + count_gone :]
        token_ref, results = rest[0], rest[1:]
        token_ref[0] = index_ref[0]
        body(index_ref, *given, *results)

    def out(shape, kind, place=None):
        return jax.ShapeDtypeStruct(shape, kind) if place is None else place(shape, kind)

    results = pl.pallas_call(
        kernel,
        grid_spec=pltpu.PrefetchScalarGridSpec(
            num_scalar_prefetch=1,
            grid=grid,
            in_specs=[spec for _, spec in ins] + [anywhere()] * count_gone,
            out_specs=[pl.BlockSpec(memory_space=pltpu.SMEM)] + [o[2] for o in outs],
            scratch_shapes=list(scratch),
        ),
        out_shape=[out((1,), jnp.int32)] + [out(o[0], o[1], *o[3:]) for o in outs],
        input_output_aliases={1 + count_in + i: 1 + i for i in range(len(onto))},
        compiler_params=pltpu.CompilerParams(vmem_limit_bytes=ROOM.get(name, 18) * MEGA),
        cost_estimate=work,
        name=name,
    )(exchange.index, *[a for a, _ in ins], *onto, *later_than)
    exchange.index = results[0]
    return results[1:]


def far(array):
    return pltpu.with_memory_space_constraint(array, pltpu.HBM)


def gate(exchange, *arrays):
    call(exchange, "gate", lambda index_ref: None, (1,), [], [], work=cost(1, 1), later_than=arrays)


def hold(exchange, array, later_than=()):
    return call(
        exchange, "hold", lambda index_ref, array_ref: None, (1,), [], [(array.shape, array.dtype, anywhere())],
        work=cost(1, 1), onto=[array], later_than=later_than,
    )[0]


def norm_stats(mixed):
    average = jnp.mean(mixed, axis=-1, keepdims=True)
    centered = mixed - average
    inv_std = lax.rsqrt(jnp.mean(centered * centered, axis=-1, keepdims=True) + NORM_EPS)
    return centered * inv_std, inv_std


def norm_pull(grad_out, normed, inv_std, gain):
    scaled = grad_out * gain
    return inv_std * (
        scaled
        - jnp.mean(scaled, axis=-1, keepdims=True)
        - normed * jnp.mean(scaled * normed, axis=-1, keepdims=True)
    )


def head_lanes(pair, head):
    lane = lax.broadcasted_iota(jnp.int32, pair.shape, 1)
    mine = (lane < HEAD_DIM) if head % 2 == 0 else (lane >= HEAD_DIM)
    return jnp.where(mine, pair, jnp.zeros((), pair.dtype))


def column_copies(core, own, other, first, target, sems):
    half = target.shape[1] // 2
    copies = []
    for i, (source, place) in enumerate(((own, core), (other, 1 - core))):
        at = pl.multiple_of(place * half, LANES)
        copies.append(
            pltpu.make_async_copy(
                source.at[:, first : first + half], target.at[:, pl.ds(at, half)], sems.at[i]
            )
        )
    return copies


def attend_kernel(index_ref, own_ref, other_ref, x_ref, seg_ref, comp_ref, proj_ref,
                  q_ref, k_ref, v_ref, ck_ref, cv_ref, lse_ref, ctx_ref, ctx_t, weights, sems):
    width = x_ref.shape[2]
    heads = width // HEAD_DIM
    copies = [
        column_copies(index_ref[0] & 1, own_ref, other_ref, kind * (width // 2), weights.at[kind], sems.at[kind])
        for kind in range(3)
    ]
    first = pl.program_id(0) == 0

    @pl.when(first)
    def _():
        for copy in sum(copies, []):
            copy.start()

    def arrive(kind):
        @pl.when(first)
        def _():
            for copy in copies[kind]:
                copy.wait()

    x = x_ref[0]
    arrive(0)
    q_ref[0] = matmul(x, weights[0]).astype(LOW)
    arrive(1)
    k_ref[0] = matmul(x, weights[1]).astype(LOW)
    arrive(2)
    v_ref[0] = matmul(x, weights[2]).astype(LOW)
    member = comp_ref[0] == seg_ref[0]
    masked = jnp.where(member, proj_ref[...], jnp.zeros((), LOW))
    ck_ref[0] = (matmul(masked, k_ref[0])).astype(LOW)
    cv = matmul(masked, v_ref[0])
    cv_ref[0] = cv.astype(LOW)
    cv_t = cv.T.astype(LOW)
    for head in range(heads):
        lanes = slice(head // 2 * LANES, head // 2 * LANES + LANES)
        rows = slice(head * HEAD_DIM, (head + 1) * HEAD_DIM)
        keys = head_lanes(ck_ref[0, :, lanes], head) * (HEAD_DIM ** -0.5)
        scores = matmul(keys.astype(LOW), q_ref[0, :, lanes], 1, 1)
        scores = jnp.where(member, scores, MASKED)
        highest = jnp.max(scores, axis=0, keepdims=True)
        weight = jnp.exp(scores - highest)
        total = jnp.sum(weight, axis=0, keepdims=True)
        lse_ref[0, head : head + 1, :] = highest + jnp.log(total)
        ctx_t[rows, :] = matmul(cv_t[rows, :], weight.astype(LOW)) * (1.0 / total)
    ctx_ref[0] = ctx_t[...].T.astype(LOW)


def attend(exchange, halves, x, seg, comp, proj, later_than):
    rows, length, width = x.shape
    slots = comp.shape[1]
    heads = width // HEAD_DIM

    def at(*shape):
        return pl.BlockSpec((1,) + shape, lambda i, _: (i, 0, 0))

    tokens = ((rows, length, width), LOW, at(length, width), pltpu.HBM)
    comps = ((rows, slots, width), LOW, at(slots, width), pltpu.HBM)
    flops = rows * (length * width * (2 * 3 * width + 4 * slots * 4) + slots * length * width * 4)
    return call(
        exchange, "attend", attend_kernel, (rows,),
        [(halves[0], anywhere()), (halves[1], anywhere()), (far(x), at(length, width)), (seg[:, None, :], at(1, length)),
         (comp[:, :, None], at(slots, 1)), (proj, whole((slots, length)))],
        [tokens] * 3 + [comps] * 2 + [((rows, heads, length), FULL, at(heads, length), pltpu.HBM), tokens],
        [pltpu.VMEM((width, length), FULL), pltpu.VMEM((3, width, width), LOW), pltpu.SemaphoreType.DMA((3, 2))],
        cost(flops, 20 * 10**6, rows * heads * slots * length), (), later_than,
    )


def mix_kernel(index_ref, own_ref, other_ref, x_ref, ctx_ref, gains_ref, normed_ref, inv_ref, low_ref, same_ref, weight, sems):
    @pl.when(pl.program_id(0) == 0)
    def _():
        first = own_ref.shape[1] - weight.shape[1] // 2
        copies = column_copies(index_ref[0] & 1, own_ref, other_ref, first, weight, sems)
        for copy in copies:
            copy.start()
        for copy in copies:
            copy.wait()

    mixed = x_ref[...].astype(FULL) + matmul(ctx_ref[...], weight[...])
    normed, inv_std = norm_stats(mixed)
    normed_ref[...] = normed
    inv_ref[...] = inv_std
    low_ref[...] = (normed * gains_ref[0:1].astype(FULL) + gains_ref[1:2].astype(FULL)).astype(LOW)
    same_ref[...] = low_ref[...]


def mix(exchange, halves, x, ctx, gains, later_than, tile=512):
    tokens, width = x.shape

    def some(n):
        return pl.BlockSpec((tile, n), lambda i, _: (i, 0))

    return call(
        exchange, "mix", mix_kernel, (tokens // tile,),
        [(halves[0], anywhere()), (halves[1], anywhere()), (far(x), some(width)), (far(ctx), some(width)),
         (gains, whole(gains.shape))],
        [((tokens, width), FULL, some(width), pltpu.HBM), ((tokens, 1), FULL, some(1), pltpu.HBM),
         ((tokens, width), LOW, some(width)), ((tokens, width), LOW, some(width), pltpu.HBM)],
        [pltpu.VMEM((width, width), LOW), pltpu.SemaphoreType.DMA((2,))],
        cost(2 * tokens * width * width, 10 * 10**6), (), later_than,
    )


def gelu_pair(h):
    t = pl.reciprocal(1.0 + (0.3275911 * 0.5**0.5) * jnp.abs(h), approx=True)
    bell = jnp.exp2(h * (h * (-0.5 * 1.4426950408889634)))
    poly = 0.127414796 + t * (-0.142248368 + t * (0.7107068705 + t * (-0.7265760135 + t * 0.5307027145)))
    tail = poly * (t * bell)
    cdf = jnp.where(h >= 0, 1.0 - tail, tail)
    return h * cdf, cdf + h * (bell * 0.3989422804014327)


def up_kernel(index_ref, f_ref, w_ref, act_ref, slope_ref):
    value, slope = gelu_pair(matmul(f_ref[...], w_ref[...]))
    act_ref[...] = value.astype(LOW)
    slope_ref[...] = slope.astype(LOW)


def up_part(exchange, f, half, mine, ff, onto, later_than, tile=768):
    tokens, width = f.shape
    steps = ff // tile // 2

    def place(j, index_ref):
        core = index_ref[0] & 1
        return (0, (core if mine else 1 - core) * steps + j)

    out = pl.BlockSpec((tokens, tile), place)
    return call(
        exchange, "up_part", up_kernel, (steps,),
        [(f, whole((tokens, width))), (half, pl.BlockSpec((width, tile), lambda j, _: (0, j)))],
        [((tokens, ff), LOW, out, pltpu.HBM)] * 2,
        (), cost(tokens * width * ff, 13 * 10**6, tokens * ff // 2), onto, later_than,
    )


def down_kernel(index_ref, own_ref, other_ref, act_ref, normed_ref, og_ref, gains_ref,
                out_ref, g_ref, low_ref, sums_ref, weight, sems):
    @pl.when(pl.program_id(0) == 0)
    def _():
        sums_ref[...] = jnp.zeros_like(sums_ref)
        copies = column_copies(index_ref[0] & 1, own_ref, other_ref, 0, weight, sems)
        for copy in copies:
            copy.start()
        for copy in copies:
            copy.wait()

    first = normed_ref[...] * gains_ref[0:1].astype(FULL) + gains_ref[1:2].astype(FULL)
    normed, inv_std = norm_stats(first + matmul(act_ref[...], weight[...]))
    out_ref[...] = (normed * gains_ref[2:3].astype(FULL) + gains_ref[3:4].astype(FULL)).astype(LOW)
    top = og_ref[...].astype(FULL)
    grad = norm_pull(top, normed, inv_std, gains_ref[2:3].astype(FULL))
    g_ref[...] = grad
    low_ref[...] = grad.astype(LOW)
    sums_ref[0:1] += jnp.sum(top * normed, axis=0, keepdims=True)
    sums_ref[1:2] += jnp.sum(top, axis=0, keepdims=True)


def down_part(exchange, halves, act, normed, og, gains, later_than, tile=256):
    tokens, ff = act.shape
    width = normed.shape[1]

    def some(n):
        return pl.BlockSpec((tile, n), lambda i, _: (i, 0))

    return call(
        exchange, "down_part", down_kernel, (tokens // tile,),
        [(halves[0], anywhere()), (halves[1], anywhere()), (far(act), some(ff)), (far(normed), some(width)), (far(og), some(width)),
         (gains, whole(gains.shape))],
        [((tokens, width), LOW, some(width), pltpu.HBM), ((tokens, width), FULL, some(width), pltpu.HBM),
         ((tokens, width), LOW, some(width)), ((8, width), FULL, kept_block((8, width)))],
        [pltpu.VMEM((ff, width), LOW), pltpu.SemaphoreType.DMA((2,))],
        cost(2 * tokens * width * ff, 23 * 10**6), (), later_than,
    )


def split_columns(index_ref, total, own_ref, other_ref):
    half = total.shape[1] // 2
    left, right = total[:, :half].astype(LOW), total[:, half:].astype(LOW)
    even = (index_ref[0] & 1) == 0
    store_rows(own_ref, jnp.where(even, left, right))
    store_rows(other_ref, jnp.where(even, right, left))


def store_rows(ref, rows):
    if len(ref.shape) == 2:
        ref[...] = rows
        return
    near, far_count = ref.shape[:2]
    parts = rows.reshape((far_count, near) + ref.shape[2:])
    for i in range(far_count):
        ref[:, i] = parts[i]


def by_plane(exchange, rows):
    far_count = 4
    chips = exchange.count // 2
    each = rows // chips
    return (chips // far_count, far_count, each) if each % 16 == 0 else None


def outer_kernel(index_ref, left_ref, *refs):
    *right_refs, own_ref, other_ref = refs
    for kind, right_ref in enumerate(right_refs):

        @pl.when(pl.program_id(0) == kind)
        def _(right_ref=right_ref):
            split_columns(index_ref, matmul(left_ref[...], right_ref[...], 0, 0), own_ref, other_ref)


def outer_part(exchange, left, rights, name, later_than, planes=False):
    tokens, depth = left.shape
    width = rights[0].shape[1]
    half = ((depth, len(rights) * width // 2), LOW, pl.BlockSpec((depth, width // 2), lambda j, _: (0, j)))
    plane = by_plane(exchange, depth)
    if planes and plane:
        spec = pl.BlockSpec(plane + (width // 2,), lambda j, _: (0, 0, 0, j))
        half = (plane + (len(rights) * width // 2,), LOW, spec)
    return call(
        exchange, name, outer_kernel, (len(rights),),
        [(far(left), whole((tokens, depth)))] + [(far(r) if planes else r, whole((tokens, width))) for r in rights],
        [half] * 2, (), cost(2 * tokens * depth * width * len(rights), 9 * 10**6), (), later_than,
    )


def down_grad_kernel(index_ref, act_ref, g_ref, own_ref, other_ref):
    split_columns(index_ref, matmul(act_ref[...], g_ref[...], 0, 0), own_ref, other_ref)


def down_grad_part(exchange, act, g, later_than, tile=768):
    tokens, ff = act.shape
    width = g.shape[1]
    half = ((ff, width // 2), LOW, pl.BlockSpec((tile, width // 2), lambda j, _: (j, 0)))
    plane = by_plane(exchange, ff)
    if plane and ff // plane[1] == tile:
        spec = pl.BlockSpec((plane[0], 1, plane[2], width // 2), lambda j, _: (0, j, 0, 0))
        half = (plane + (width // 2,), LOW, spec)
    return call(
        exchange, "down_grad_part", down_grad_kernel, (ff // tile,),
        [(far(act), pl.BlockSpec((tokens, tile), lambda j, _: (0, j))), (g, whole((tokens, width)))],
        [half] * 2, (), cost(2 * tokens * width * ff, 13 * 10**6), (), later_than,
    )


def ff_back_kernel(index_ref, down_own, down_other, up_own, up_other, slope_ref, low_ref, f_ref, start_ref, normed_ref,
                   inv_ref, gains_ref, *refs):
    own_ref, other_ref, g_one_ref, g_one_low_ref, sums_ref, total, w_down, normed, start, sems = refs
    step = pl.program_id(0)
    steps = pl.num_programs(0)
    half = steps // 2
    core = index_ref[0] & 1
    tile = slope_ref.shape[1]

    def copies(at):
        place = jnp.where(at < half, (1 - core) * half + at, core * half + at - half)
        rows = pl.ds(pl.multiple_of(place * tile, tile), tile)
        return column_copies(core, down_own.at[rows], down_other.at[rows], 0, w_down.at[at % 2], sems.at[at % 2])

    late = [
        pltpu.make_async_copy(normed_ref, normed, sems.at[2, 0]),
        pltpu.make_async_copy(start_ref, start, sems.at[2, 1]),
    ]

    @pl.when(step == 0)
    def _():
        for copy in copies(step):
            copy.start()
        for copy in late:
            copy.start()
        total[...] = jnp.zeros_like(total)

    @pl.when(step < steps - 1)
    def _():
        for copy in copies(step + 1):
            copy.start()

    for copy in copies(step):
        copy.wait()

    back = (matmul(low_ref[...], w_down[step % 2], 1, 1) * slope_ref[...].astype(FULL)).astype(LOW)
    grads = matmul(f_ref[...], back, 0, 0).astype(LOW)
    pl.when(step < half)(lambda: store_rows(other_ref, grads))
    pl.when(step >= half)(lambda: store_rows(own_ref, grads))

    def add(up_ref):
        total[...] += matmul(back, up_ref[...], 1, 1)

    pl.when(step < half)(lambda: add(up_other))
    pl.when(step >= half)(lambda: add(up_own))

    @pl.when(step == steps - 1)
    def _():
        for copy in late:
            copy.wait()
        top = total[...] + start[...]
        grad = norm_pull(top, normed[...], inv_ref[...], gains_ref[0:1].astype(FULL))
        g_one_ref[...] = grad
        g_one_low_ref[...] = grad.astype(LOW)
        sums_ref[...] = jnp.zeros_like(sums_ref)
        sums_ref[0:1] = jnp.sum(top * normed[...], axis=0, keepdims=True)
        sums_ref[1:2] = jnp.sum(top, axis=0, keepdims=True)


def ff_back(exchange, down, up, slope, low, f, start, normed, inv, gains, later_than, tile=768):
    tokens, ff = slope.shape
    width = f.shape[1]
    steps = ff // tile
    half = steps // 2

    def place(j, index_ref):
        core = index_ref[0] & 1
        return (0, jnp.where(j < half, (1 - core) * half + j, core * half + j - half))

    full = whole((tokens, width))
    result = kept_block((tokens, width))
    shape = by_plane(exchange, width) or (width,)

    def columns(place):
        return pl.BlockSpec(shape + (tile,), lambda j, _: (0,) * len(shape) + (place(j),))

    return call(
        exchange, "ff_back", ff_back_kernel, (steps,),
        [(far(down[0]), anywhere()), (far(down[1]), anywhere()),
         (up[0], pl.BlockSpec((width, tile), lambda j, _: (0, jnp.maximum(j - half, 0)))),
         (up[1], pl.BlockSpec((width, tile), lambda j, _: (0, jnp.minimum(j, half - 1)))),
         (far(slope), pl.BlockSpec((tokens, tile), place)),
         (far(low), full), (far(f), full), (far(start), anywhere()), (far(normed), anywhere()), (far(inv), whole(inv.shape)), (gains, whole(gains.shape))],
        [(shape + (ff // 2,), LOW, columns(lambda j: jnp.maximum(j - half, 0))),
         (shape + (ff // 2,), LOW, columns(lambda j: jnp.minimum(j, half - 1)))]
        + [((tokens, width), FULL, result, pltpu.HBM), ((tokens, width), LOW, result, pltpu.HBM),
         ((8, width), FULL, kept_block((8, width)))],
        [pltpu.VMEM((tokens, width), FULL), pltpu.VMEM((2, tile, width), LOW), pltpu.VMEM((tokens, width), FULL),
         pltpu.VMEM((tokens, width), FULL),
         pltpu.SemaphoreType.DMA((3, 2))],
        cost(6 * tokens * width * ff, 40 * 10**6), (), later_than,
    )


def attend_back_kernel(index_ref, own_ref, other_ref, g_ref, q_ref, k_ref, v_ref, ck_ref, cv_ref, lse_ref,
                       seg_ref, comp_ref, proj_ref,
                       gq_ref, gk_ref, gv_ref, grad_ref, gctx, gq_t, gck, gcv, weight, sems):
    width = q_ref.shape[2]
    heads = width // HEAD_DIM
    scale = HEAD_DIM ** -0.5

    @pl.when(pl.program_id(0) == 0)
    def _():
        copies = column_copies(
            index_ref[0] & 1, own_ref, other_ref, own_ref.shape[1] - width // 2, weight, sems
        )
        for copy in copies:
            copy.start()
        for copy in copies:
            copy.wait()

    gctx[...] = matmul(g_ref[0], weight[...], 1, 1).astype(LOW)
    member = comp_ref[0] == seg_ref[0]
    ck_t = ck_ref[0].astype(FULL).T.astype(LOW)
    for pair in range(heads // 2):
        lanes = slice(pair * LANES, pair * LANES + LANES)
        queries, grads = q_ref[0, :, lanes], gctx[:, lanes]
        key_parts, value_parts = [], []
        for head in (2 * pair, 2 * pair + 1):
            rows = slice(head * HEAD_DIM, (head + 1) * HEAD_DIM)
            keys = head_lanes(ck_ref[0, :, lanes], head) * scale
            scores = matmul(keys.astype(LOW), queries, 1, 1)
            probs = jnp.exp(jnp.where(member, scores - lse_ref[0, head : head + 1, :], MASKED))
            grad_probs = matmul(head_lanes(cv_ref[0, :, lanes], head), grads, 1, 1)
            delta = jnp.sum(probs * grad_probs, axis=0, keepdims=True)
            grad_scores = (probs * (grad_probs - delta)).astype(LOW)
            gq_t[rows, :] = matmul(ck_t[rows, :], grad_scores) * scale
            key_parts.append(matmul(grad_scores, queries))
            value_parts.append(matmul(probs.astype(LOW), grads))
        lane = lax.broadcasted_iota(jnp.int32, key_parts[0].shape, 1) < HEAD_DIM
        gck[:, lanes] = (jnp.where(lane, *key_parts) * scale).astype(LOW)
        gcv[:, lanes] = jnp.where(lane, *value_parts).astype(LOW)
    gq_ref[...] = gq_t[...].T.astype(LOW)
    masked = jnp.where(member, proj_ref[...], jnp.zeros((), LOW))
    gk_ref[...] = matmul(masked, gck[...], 0, 0).astype(LOW)
    gv_ref[...] = matmul(masked, gcv[...], 0, 0).astype(LOW)
    part = matmul(gck[...], k_ref[0], 1, 1) + matmul(gcv[...], v_ref[0], 1, 1)
    part = jnp.where(member, part, 0.0)

    @pl.when(pl.program_id(0) == 0)
    def _():
        grad_ref[...] = part

    @pl.when(pl.program_id(0) > 0)
    def _():
        grad_ref[...] += part


def attend_back(exchange, halves, g, kept, seg, comp, proj, later_than):
    q, k, v, ck, cv, lse = kept
    rows, length, width = q.shape
    slots = comp.shape[1]
    heads = width // HEAD_DIM

    def at(*shape):
        return pl.BlockSpec((1,) + shape, lambda i, _: (i, 0, 0))

    tokens = ((rows * length, width), LOW, pl.BlockSpec((length, width), lambda i, _: (i, 0)))
    flops = rows * length * width * (2 * width + 4 * slots * 10)
    return call(
        exchange, "attend_back", attend_back_kernel, (rows,),
        [(far(halves[0]), anywhere()), (far(halves[1]), anywhere())] + [(a, at(length, width)) for a in (far(g), far(q), far(k), far(v))]
        + [(far(a), at(slots, width)) for a in (ck, cv)]
        + [(far(lse), at(heads, length)), (seg[:, None, :], at(1, length)), (comp[:, :, None], at(slots, 1)),
           (far(proj), whole((slots, length)))],
        [tokens] * 3 + [((slots, length), FULL, kept_block((slots, length)))],
        [pltpu.VMEM((length, width), LOW), pltpu.VMEM((width, length), FULL),
         pltpu.VMEM((slots, width), LOW), pltpu.VMEM((slots, width), LOW),
         pltpu.VMEM((width, width), LOW), pltpu.SemaphoreType.DMA((2,))],
        cost(flops, 15 * 10**6, rows * heads * slots * length), (), later_than,
    )


def input_kernel(index_ref, own_ref, other_ref, g_ref, gq_ref, gk_ref, gv_ref, out_ref, weights, sems):
    width = g_ref.shape[1]

    @pl.when(pl.program_id(0) == 0)
    def _():
        copies = []
        for kind in range(3):
            copies += column_copies(
                index_ref[0] & 1, own_ref, other_ref, kind * (width // 2), weights.at[kind], sems.at[kind]
            )
        for copy in copies:
            copy.start()
        for copy in copies:
            copy.wait()

    out_ref[...] = (
        g_ref[...]
        + matmul(gq_ref[...], weights[0], 1, 1)
        + matmul(gk_ref[...], weights[1], 1, 1)
        + matmul(gv_ref[...], weights[2], 1, 1)
    )


def input_part(exchange, halves, g, gq, gk, gv, later_than, tile=256):
    tokens, width = g.shape
    some = pl.BlockSpec((tile, width), lambda i, _: (i, 0))
    return call(
        exchange, "input_part", input_kernel, (tokens // tile,),
        [(far(halves[0]), anywhere()), (far(halves[1]), anywhere())] + [(far(a), some) for a in (g, gq, gk, gv)],
        [((tokens, width), FULL, some)],
        [pltpu.VMEM((3, width, width), LOW), pltpu.SemaphoreType.DMA((3, 2))],
        cost(6 * tokens * width * width, 15 * 10**6), (), later_than,
    )[0]


def adaptive(first, second, grad):
    first_new = BETA_ONE * first + (1.0 - BETA_ONE) * grad
    second_new = BETA_TWO * second + (1.0 - BETA_TWO) * grad * grad
    direction = (
        first_new
        / (1.0 - BETA_ONE**STEP)
        / (jnp.sqrt(second_new / (1.0 - BETA_TWO**STEP)) + EPSILON)
    )
    return (first_new, second_new, direction)


def store_halves(index_ref, columns, left, right, own_ref, other_ref):
    even = (index_ref[0] & 1) == 0
    own_ref[:, columns] = jnp.where(even, left, right).astype(LOW)
    other_ref[:, columns] = jnp.where(even, right, left).astype(LOW)


def store_matrix(index_ref, columns, matrix, own_ref, other_ref):
    half = matrix.shape[1] // 2
    store_halves(index_ref, columns, matrix[:, :half], matrix[:, half:], own_ref, other_ref)


def pack_attn_kernel(index_ref, weight_ref, comp_ref, norm_ref, own_ref, other_ref, side):
    kinds = weight_ref.shape[0] - 1
    half = weight_ref.shape[2] // 2
    rows, length = comp_ref.shape
    pieces = length // side.shape[1]
    own, own_columns = norm_ref.shape
    side[...] = jnp.zeros_like(side)
    for i in range(pieces):
        side[i * rows : (i + 1) * rows, :] = comp_ref[:, i * side.shape[1] : (i + 1) * side.shape[1]]
    side[pieces * rows : pieces * rows + own, :own_columns] = norm_ref[...]
    for kind in range(kinds):
        store_matrix(index_ref, slice(kind * half, (kind + 1) * half), weight_ref[kind], own_ref, other_ref)
    store_matrix(index_ref, slice(kinds * half, None), side[...], own_ref, other_ref)


def pack_up_kernel(index_ref, weight_ref, out_ref, own_ref, other_ref):
    split = weight_ref.shape[1] // 2
    store_matrix(index_ref, slice(0, split), weight_ref[...], own_ref, other_ref)
    store_matrix(index_ref, slice(split, None), out_ref[0], own_ref, other_ref)


def pack_down_kernel(index_ref, weight_ref, own_ref, other_ref):
    store_matrix(index_ref, slice(None), weight_ref[...], own_ref, other_ref)


def squares_row(array):
    total = jnp.sum(jnp.sum(array * array, axis=0, keepdims=True), axis=1, keepdims=True)
    return jnp.broadcast_to(total, (1, LANES))


def step_matrix(weight, first, second, grad, first_ref, second_ref, direction_ref, sums_ref, row):
    first_new, second_new, direction = adaptive(first, second, grad)
    direction = direction + DECAY * weight
    first_ref[...] = first_new
    second_ref[...] = second_new
    direction_ref[...] = direction
    sums_ref[row : row + 1] = squares_row(weight)
    sums_ref[row + 8 : row + 9] = squares_row(direction)


def joined_halves(index_ref, mine, got):
    even = (index_ref[0] & 1) == 0
    return jnp.concatenate([jnp.where(even, mine, got), jnp.where(even, got, mine)], axis=1)


def down_step_kernel(index_ref, mine_ref, got_ref, weight_ref, first_ref, second_ref,
                     first_new, second_new, direction, sums_ref):
    sums_ref[...] = jnp.zeros_like(sums_ref)
    grad = joined_halves(index_ref, mine_ref[...].astype(FULL), got_ref[...].astype(FULL))
    step_matrix(weight_ref[...], first_ref[...], second_ref[...], grad, first_new, second_new, direction, sums_ref, 5)


def up_step_kernel(index_ref, mine_ref, got_ref, weight_ref, first_ref, second_ref, out_weight, out_first, out_second,
                   first_new, second_new, direction, out_first_new, out_second_new, out_direction, sums_ref):
    sums_ref[...] = jnp.zeros_like(sums_ref)
    split = weight_ref.shape[1] // 2
    mine, got = mine_ref[...].astype(FULL), got_ref[...].astype(FULL)
    grad = joined_halves(index_ref, mine[:, :split], got[:, :split])
    step_matrix(weight_ref[...], first_ref[...], second_ref[...], grad, first_new, second_new, direction, sums_ref, 4)
    grad = joined_halves(index_ref, mine[:, split:], got[:, split:])
    step_matrix(out_weight[0], out_first[0], out_second[0], grad,
                out_first_new, out_second_new, out_direction, sums_ref, 3)


def attn_step_kernel(index_ref, mine_ref, got_ref, weight_ref, first_ref, second_ref,
                     comp_weight, comp_first, comp_second, norm_weight, norm_first, norm_second,
                     out_first_new, up_sums, down_sums,
                     first_new, second_new, direction, comp_first_new, comp_second_new, comp_direction,
                     norm_first_new, norm_second_new, norm_new, sent_ref, sums_ref):
    sums_ref[...] = up_sums[...] + down_sums[...]
    kinds = weight_ref.shape[0] - 1
    width = weight_ref.shape[2]
    half = width // 2
    mine, got = mine_ref[...].astype(FULL), got_ref[...].astype(FULL)
    for kind in range(kinds):
        columns = slice(kind * half, (kind + 1) * half)
        grad = joined_halves(index_ref, mine[:, columns], got[:, columns])
        step_matrix(weight_ref[kind], first_ref[kind], second_ref[kind], grad,
                    first_new.at[kind], second_new.at[kind], direction.at[kind], sums_ref, kind)
    first_new[kinds] = out_first_new[...]
    side = joined_halves(index_ref, mine[:, kinds * half :], got[:, kinds * half :])
    rows, length = comp_weight.shape
    pieces = length // side.shape[1]
    grad = jnp.concatenate([side[i * rows : (i + 1) * rows] for i in range(pieces)], axis=1)
    step_matrix(comp_weight[...], comp_first[...], comp_second[...], grad,
                comp_first_new, comp_second_new, comp_direction, sums_ref, 6)
    own, own_columns = norm_weight.shape
    grad = side[pieces * rows : pieces * rows + own, :own_columns]
    new, newer, way = adaptive(norm_first[...], norm_second[...], grad)
    norm_first_new[...] = new
    norm_second_new[...] = newer
    norm_new[...] = norm_weight[...] - RATE * way
    sent_ref[...] = jnp.broadcast_to(sums_ref[...][None], sent_ref.shape)


def finish_kernel(index_ref, got_ref, weight_ref, direction_ref, out_direction, up_weight, up_direction,
                  down_weight, down_direction, comp_weight, comp_direction,
                  attn_new, attn_copy, up_new, up_copy, down_new, down_copy, comp_new, comp_copy, norms_ref):
    totals = jnp.sqrt(jnp.sum(got_ref[...], axis=0))
    lane = lax.broadcasted_iota(jnp.int32, (1, LANES), 1)
    count = norms_ref.shape[1]
    for i in range(2):
        row = sum(jnp.where(lane == m, totals[8 * i + m : 8 * i + m + 1], 0.0) for m in range(count))
        norms_ref[i : i + 1, :] = row[:, :count]
    ratio = totals[:8] / (totals[8:] + EPSILON)

    def move(weight, direction, matrix, new_ref, copy_ref):
        new = weight - RATE * ratio[matrix : matrix + 1, :1] * direction
        new_ref[...] = new
        copy_ref[...] = new.astype(LOW)

    for kind in range(4):
        way = direction_ref[kind] if kind < 3 else out_direction[...]
        move(weight_ref[kind], way, kind, attn_new.at[kind], attn_copy.at[kind])
    move(up_weight[...], up_direction[...], 4, up_new, up_copy)
    move(down_weight[...], down_direction[...], 5, down_new, down_copy)
    move(comp_weight[...], comp_direction[...], 6, comp_new, comp_copy)


def elementwise(exchange, name, body, ins, shapes, later_than=(), scratch=()):
    pairs = []
    for a in ins:
        if isinstance(a, tuple):
            shape, kind = (1,) + a[0].shape[1:], a[1]
            pairs.append((far(a[0]), pl.BlockSpec(shape, lambda *_, kind=kind: (kind, 0, 0))))
        else:
            pairs.append((far(a) if name.startswith("pack") else a, whole(a.shape)))
    return call(
        exchange, name, body, (1,), pairs, [(shape, kind, whole(shape)) for shape, kind in shapes], scratch,
        cost(10**6, sum(a.size * 4 for a, _ in pairs)), (), later_than,
    )


def local(
    dp,
    fsdp,
    inputs,
    segment_ids,
    compressed_segment,
    out_grad,
    attn_weight,
    attn_first,
    attn_second,
    up_weight,
    up_first,
    up_second,
    down_weight,
    down_first,
    down_second,
    compress_weight,
    compress_first,
    compress_second,
    norm_params,
    norm_first,
    norm_second,
):
    exchange = Exchange(dp, fsdp)
    devices = dp * fsdp
    row_count, length, model_width = inputs.shape
    half_width = model_width // 2
    token_count = row_count * length
    norm_kinds, norm_own = norm_params.shape
    attn_kinds, attn_own, _ = attn_weight.shape
    compress_own = compress_weight.shape[0]
    pieces = 2 if 2 * compress_own + norm_kinds <= attn_own else 1
    side_width = length // pieces

    def side_rows(compress_part, norm_part):
        none = [(0, 0)] * (compress_part.ndim - 2)
        spare = attn_own - pieces * compress_own - norm_kinds
        norm_part = jnp.pad(norm_part, none + [(0, spare), (0, side_width - norm_own)])
        parts = [compress_part[..., i * side_width : (i + 1) * side_width] for i in range(pieces)]
        return jnp.concatenate(parts + [norm_part], axis=-2)

    def halves(array):
        middle = array.shape[-1] // 2
        return array[..., :middle], array[..., middle:]

    flat_in = inputs.reshape(token_count, model_width)
    ff = up_weight.shape[1]
    out_kind = attn_kinds - 1
    out_at = [(a, out_kind) for a in (attn_weight, attn_first, attn_second)]
    attn = Gather(
        exchange,
        *elementwise(
            exchange, "pack_attn", pack_attn_kernel, [attn_weight, compress_weight, norm_params],
            [((attn_own, out_kind * half_width + side_width // 2), LOW)] * 2, (),
            [pltpu.VMEM((attn_own, side_width), FULL)],
        ),
    )
    attn.begin()
    up = Gather(
        exchange,
        *elementwise(
            exchange, "pack_up", pack_up_kernel, [up_weight, out_at[0]],
            [((attn_own, (ff + model_width) // 2), LOW)] * 2, [attn.mine],
        ),
    )
    up.begin()
    attn.finish()
    attn.begin()
    up.finish()
    up.have = hold(exchange, up.have)
    up.spread()
    attn.finish()
    for _ in exchange.rest[1:]:
        attn.hop()
    attn.hop()
    attn.hop()
    attn.begin()
    down = Gather(
        exchange,
        *elementwise(
            exchange, "pack_down", pack_down_kernel, [down_weight], [((down_weight.shape[0], half_width), LOW)] * 2,
            [attn.have],
        ),
        together=True,
    )
    down.hop()
    down.begin()
    attn.finish()
    side_own, side_other = [part[:, -side_width // 2 :] for part in attn.halves]
    side = jnp.concatenate(
        [exchange.by_core(side_own, side_other), exchange.by_core(side_other, side_own)], axis=1
    ).reshape(devices, attn_own, side_width)
    compress_full = jnp.concatenate(
        [side[:, i * compress_own : (i + 1) * compress_own] for i in range(pieces)], axis=2
    ).reshape(-1, length)
    gains = (
        side[:, pieces * compress_own : pieces * compress_own + norm_kinds, :norm_own]
        .transpose(1, 0, 2)
        .reshape(norm_kinds, model_width)
    )

    *kept, context = attend(
        exchange, attn.halves, inputs, segment_ids, compressed_segment, compress_full, [down.have]
    )
    context = context.reshape(token_count, model_width)
    down.finish()
    down.begin()
    up.have = hold(exchange, up.have, [down.have])
    up.begin()
    up.finish()
    first_normed, first_inv, first_low, first_low_far = mix(exchange, up.halves, flat_in, context, gains, [down.have])
    down.finish()
    down.begin()
    hidden = up_part(exchange, first_low, up.halves[0], True, ff, (), [down.have])
    down.finish()
    down.begin()
    active, slope = up_part(exchange, first_low, up.halves[1], False, ff, hidden, [down.have])
    down.finish()
    result, grad_second, grad_second_low, sums_two = down_part(
        exchange, down.halves, active, first_normed, out_grad.reshape(token_count, model_width), gains, []
    )

    down_sum, up_sum, attn_sum = Reduce(exchange), Reduce(exchange), Scatter(exchange)
    down_own, down_other = down_grad_part(exchange, active, grad_second_low, [])
    down_sum.add(down_own, down_other)
    down_sum.merge()
    up_own, up_other, grad_first, grad_first_low, sums_one = ff_back(
        exchange, down.halves, up.halves, slope, grad_second_low, first_low_far, grad_second,
        first_normed, first_inv, gains, [far(down_sum.merged)],
    )
    down_sum.plane()
    up_sum.add(up_own, up_other)
    out_own, out_other = outer_part(exchange, context, [grad_first_low], "out_grad_part", [], True)
    up_sum.add(out_own, out_other)
    up_sum.merge()
    *grads, comp_grad = attend_back(
        exchange, up.halves, grad_first_low.reshape(inputs.shape), kept,
        segment_ids, compressed_segment, compress_full, [far(up_sum.merged)] + [far(p) for p in down_sum.planes],
    )
    up_sum.plane()
    qkv_own, qkv_other = outer_part(exchange, flat_in, grads, "qkv_grad_part", [])
    norm_grad = jnp.concatenate([sums_one[:2], sums_two[:2]])
    side_grad = side_rows(
        comp_grad.reshape(devices, compress_own, length),
        norm_grad.reshape(norm_kinds, devices, norm_own).transpose(1, 0, 2),
    ).reshape(model_width, side_width).astype(LOW)
    side_left, side_right = halves(side_grad)
    attn_sum.add(qkv_own, qkv_other)
    attn_sum.add(exchange.by_core(side_left, side_right), exchange.by_core(side_right, side_left))
    attn_sum.merge()
    attn_sum.begin()
    up_sum.begin()
    input_grad = input_part(
        exchange, attn.halves, grad_first, *grads, [attn_sum.sent_now, up_sum.sent_now]
    )
    down_sum.line()

    up_sum.finish()
    up_sum.begin()
    attn_sum.finish()
    attn_sum.begin()
    gate(exchange, attn_sum.sent_now, up_sum.sent_now)
    up_sum.finish()
    up_sum.begin()
    attn_sum.finish()
    attn_sum.begin()
    gate(exchange, attn_sum.sent_now, up_sum.sent_now)
    attn_sum.finish()
    attn_sum.begin()
    out_shape = attn_weight.shape[1:]
    up_first_new, up_second_new, up_direction, out_first_new, out_second_new, out_direction, up_squares = elementwise(
        exchange, "up_step", up_step_kernel,
        [up_sum.mine, up_sum.got, up_weight, up_first, up_second] + out_at,
        [(up_weight.shape, FULL)] * 3 + [(out_shape, FULL)] * 3 + [((16, LANES), FULL)], [attn_sum.sent_now],
    )
    down_sum.begin()
    attn_sum.finish()
    attn_sum.begin()
    down_first_new, down_second_new, down_direction, down_squares = elementwise(
        exchange, "down_step", down_step_kernel,
        [down_sum.mine, down_sum.got, down_weight, down_first, down_second],
        [(down_weight.shape, FULL)] * 3 + [((16, LANES), FULL)], [attn_sum.sent_now],
    )
    attn_sum.finish()
    while attn_sum.hops:
        attn_sum.hop()
    three = (out_kind,) + out_shape
    (
        attn_first_new, attn_second_new, attn_direction,
        compress_first_new, compress_second_new, compress_direction,
        norm_first_new, norm_second_new, norm_new, sent, _,
    ) = elementwise(
        exchange, "attn_step", attn_step_kernel,
        [attn_sum.mine, attn_sum.got, attn_weight, attn_first, attn_second,
         compress_weight, compress_first, compress_second, norm_params, norm_first, norm_second,
         out_first_new, up_squares, down_squares],
        [(attn_weight.shape, FULL), (three, FULL), (three, FULL)] + [(compress_weight.shape, FULL)] * 3
        + [(norm_params.shape, FULL)] * 3 + [((devices, 16, LANES), FULL), ((16, LANES), FULL)],
    )
    got = lax.all_to_all(sent, AXES, split_axis=0, concat_axis=0, tiled=True)
    attn_new, attn_copy, up_new, up_copy, down_new, down_copy, compress_new, compress_copy, norms = elementwise(
        exchange, "finish", finish_kernel,
        [got, attn_weight, attn_direction, out_direction, up_weight, up_direction, down_weight, down_direction,
         compress_weight, compress_direction],
        [(a.shape, t) for a in (attn_weight, up_weight, down_weight, compress_weight) for t in (FULL, LOW)]
        + [((2, attn_kinds + 3), FULL)],
    )
    return (
        result.reshape(row_count, length, model_width),
        input_grad.reshape(row_count, length, model_width),
        attn_first_new,
        attn_second_new,
        out_second_new,
        attn_new,
        attn_copy,
        up_first_new,
        up_second_new,
        up_new,
        up_copy,
        down_first_new,
        down_second_new,
        down_new,
        down_copy,
        compress_first_new,
        compress_second_new,
        compress_new,
        compress_copy,
        norm_first_new,
        norm_second_new,
        norm_new,
        norms,
    )


def solution(mesh):
    rows, mid, flat = P(AXES, None), P(None, AXES, None), P(None, AXES)
    deep = P(AXES, None, None)

    def step(*args):
        return local(mesh.shape["dp"], mesh.shape["fsdp"], *args)

    return jax.shard_map(
        step,
        mesh=mesh,
        in_specs=(deep, rows, rows, deep) + (mid,) * 3 + (rows,) * 9 + (flat,) * 3,
        out_specs=(deep, deep, mid, mid, rows, mid, mid)
        + (rows,) * 12
        + (flat,) * 3
        + (P(),),
        check_vma=False,
    )
```

```python
import jax
import jax.numpy as jnp
from jax import lax
from jax.experimental import pallas as pl
from jax.experimental.pallas import tpu as pltpu
from jax.sharding import PartitionSpec as P

HEAD_DIM = 64
STEP = 10


BETA_ONE = 0.9
BETA_TWO = 0.999
EPSILON = 1e-06
DECAY = 0.01
RATE = 0.5
NORM_EPS = 1e-05
MASKED = -1e30

AXES = ("dp", "fsdp")
LOW = jnp.bfloat16
FULL = jnp.float32
MEGA = 1024 * 1024
ROOM = {"attend": 22, "attend_back": 22, "up_part": 26, "ff_back": 44, "down_part": 20}
LANES = 128


class Exchange:
    def __init__(self, dp, fsdp):
        self.count = dp * fsdp
        self.bits = self.count.bit_length() - 1
        self.x_bit = 1
        self.y_bit = fsdp.bit_length() - 1
        self.rest = [b for b in range(1, self.bits) if b not in (self.x_bit, self.y_bit)]
        self.index = lax.axis_index(AXES).astype(jnp.int32).reshape(1)
        self.first_index = self.index

    def value(self, bit):
        return (self.index[0] >> bit) & 1

    def known(self, bit):
        return (self.first_index[0] >> bit) & 1

    def flip(self, array, even_bit, odd_bit):
        pairs = [(i, i ^ (1 << (odd_bit if i & 1 else even_bit))) for i in range(self.count)]
        return lax.ppermute(array, AXES, pairs)

    def masks(self):
        return [
            sum(((k >> i) & 1) << bit for i, bit in enumerate(self.rest)) for k in range(1 << len(self.rest))
        ]

    def move(self, array, mask):
        return lax.ppermute(array, AXES, [(i, i ^ mask) for i in range(self.count)])

    def by_rest(self, pieces):
        for i, bit in enumerate(self.rest):
            turned = self.value(bit) == 1
            pieces = [jnp.where(turned, pieces[k ^ (1 << i)], p) for k, p in enumerate(pieces)]
        return pieces

    def by_core(self, even, odd):
        return jnp.where(self.value(0) == 0, even, odd)

    def joined(self, own, other, value, axis):
        return jnp.where(
            value == 0, jnp.stack([own, other], axis), jnp.stack([other, own], axis)
        )

    def groups(self, step, size):
        return [
            [base + low + step * i for i in range(size)]
            for base in range(0, self.count, step * size)
            for low in range(step)
        ]

    def pick(self, array, dim, value):
        return lax.dynamic_index_in_dim(array, value, dim, keepdims=False, allow_negative_indices=False)


class Gather:
    def __init__(self, exchange, mine, sent, together=False):
        self.exchange = exchange
        self.mine, self.sent = mine, sent
        self.hops = ["pair"] + (["far"] if together else exchange.rest[::-1]) + ["near", "last", "core"]
        self.place = 0

    def spread(self):
        ex = self.exchange
        self.hops = ["core"]
        self.have = lax.all_gather(
            self.have, AXES, axis=0, axis_index_groups=ex.groups(2, ex.count // 2), tiled=True
        )

    def begin(self):
        ex = self.exchange
        hop = self.hops[0]
        if hop == "pair":
            self.got = ex.flip(self.sent, 0, 0)
        elif hop == "near":
            self.got = ex.flip(self.have, ex.y_bit, ex.x_bit)
        elif hop == "last":
            self.got = ex.flip(self.have, ex.x_bit, ex.y_bit)
        elif hop == "core":
            self.got = ex.flip(self.have, 0, 0)
        elif hop == "far":
            self.got = [ex.move(self.have, mask) for mask in ex.masks()[1:]]
        else:
            self.got = ex.flip(self.have, hop, hop)

    def finish(self):
        ex = self.exchange
        hop = self.hops.pop(0)
        x_value, y_value = ex.known(ex.x_bit), ex.known(ex.y_bit)
        if hop == "far":
            self.have = jnp.stack(ex.by_rest([self.have] + self.got))
        elif hop == "pair":
            self.have = ex.joined(self.mine, self.got, ex.value(0), 0)
            self.have = self.have.reshape((-1,) + self.mine.shape[1:])
            self.block = self.have.shape
        elif hop == "near":
            self.have = ex.joined(self.have, self.got, ex.by_core(y_value, x_value), 0)
        elif hop == "last":
            have = ex.joined(self.have, self.got, ex.by_core(x_value, y_value), 0)
            have = have.reshape((2,) * (ex.bits - 1) + self.block)
            wanted = list(range(ex.bits - 1, 0, -1))
            tail = [len(wanted), len(wanted) + 1]
            forms = []
            for first, second in ((ex.x_bit, ex.y_bit), (ex.y_bit, ex.x_bit)):
                now = [first, second] + ex.rest[::-1]
                forms.append(have.transpose([now.index(b) for b in wanted] + tail))
            self.have = ex.by_core(*forms).reshape((ex.count // 2) * self.block[0], self.block[1])
        elif hop == "core":
            self.halves = self.have, self.got
        else:
            self.have = ex.joined(self.have, self.got, ex.value(hop), self.place)
            self.place += 1

    def hop(self):
        self.begin()
        self.finish()

    def parts_begin(self):
        ex = self.exchange
        self.begin()
        self.other_have = ex.flip(self.have, 0, 0)

    def parts_finish(self):
        self.got = hold(self.exchange, self.got)
        self.parts = [self.have, self.got, self.other_have, self.exchange.flip(self.got, 0, 0)]


def part_copies(exchange, index, parts, plane, target, sems):
    near_bits = [b for b in exchange.rest if b < exchange.bits - 2]
    half = target.shape[2] // 2
    x_value, y_value = (index >> exchange.x_bit) & 1, (index >> exchange.y_bit) & 1
    copies = []
    for i, source in enumerate(parts):
        core = index & 1 if i < 2 else 1 - (index & 1)
        columns = pl.ds(pl.multiple_of(core * half, LANES), half)
        for other in (0, 1):
            x_at = jnp.where(core == 0, x_value ^ (i % 2), other)
            y_at = jnp.where(core == 0, other, y_value ^ (i % 2))
            for low in range(1 << len(near_bits)):
                chip = (x_at << (exchange.x_bit - 1)) + (y_at << (exchange.y_bit - 1))
                chip += sum(((low >> k) & 1) << (b - 1) for k, b in enumerate(near_bits))
                copies.append(
                    pltpu.make_async_copy(
                        source.at[other, (plane << len(near_bits)) + low], target.at[chip, :, columns], sems.at[len(copies)]
                    )
                )
    return copies


class Scatter:
    def __init__(self, exchange):
        self.exchange = exchange
        self.own, self.sent = [], []
        self.hops = ["near", "next"] + exchange.rest + ["last"]
        self.place = len(exchange.rest)

    def add(self, own, other):
        self.own.append(own)
        self.sent.append(self.exchange.flip(other, 0, 0))

    def merge(self):
        parts = [(a.astype(FULL) + b.astype(FULL)).astype(LOW) for a, b in zip(self.own, self.sent)]
        view = parts[0] if len(parts) == 1 else jnp.concatenate(parts, axis=1)
        self.have = view.reshape((2,) * (self.exchange.bits - 1) + (-1, view.shape[1]))

    def part(self, x_now, y_now):
        ex = self.exchange
        bits = list(range(ex.bits - 1, 0, -1))
        dim_x, dim_y = bits.index(ex.x_bit), bits.index(ex.y_bit)
        even = ex.pick(jnp.moveaxis(self.have, (dim_x, dim_y), (0, 1)), 0, x_now)
        odd = ex.pick(jnp.moveaxis(self.have, (dim_y, dim_x), (0, 1)), 0, y_now)
        return ex.by_core(even, odd)

    def begin(self):
        ex = self.exchange
        hop = self.hops[0]
        x_value, y_value = ex.known(ex.x_bit), ex.known(ex.y_bit)
        if hop == "near":
            self.sent_now = self.part(1 - x_value, 1 - y_value)
            self.got = ex.flip(self.sent_now, ex.x_bit, ex.y_bit)
        elif hop == "next":
            value = ex.by_core(y_value, x_value)
            self.sent_now = ex.pick(self.have, 0, 1 - value).astype(LOW)
            self.got = ex.flip(self.sent_now, ex.y_bit, ex.x_bit)
        elif hop == "last":
            view = self.have.reshape(2, -1, self.have.shape[-1])
            self.sent_now = ex.pick(view, 0, 1 - ex.value(0)).astype(LOW)
            self.got = ex.flip(self.sent_now, 0, 0)
        else:
            self.place -= 1
            self.sent_now = ex.pick(self.have, self.place, 1 - ex.value(hop)).astype(LOW)
            self.got = ex.flip(self.sent_now, hop, hop)

    def finish(self):
        ex = self.exchange
        hop = self.hops.pop(0)
        x_value, y_value = ex.known(ex.x_bit), ex.known(ex.y_bit)
        if hop == "last":
            self.mine = ex.pick(self.have.reshape(2, -1, self.have.shape[-1]), 0, ex.value(0))
            return
        got = self.got.astype(FULL)
        if hop == "near":
            self.have = self.part(x_value, y_value).astype(FULL) + got
        elif hop == "next":
            self.have = ex.pick(self.have, 0, ex.by_core(y_value, x_value)) + got
        else:
            self.have = ex.pick(self.have, self.place, ex.value(hop)) + got

    def hop(self):
        self.begin()
        self.finish()


class Reduce:
    def __init__(self, exchange):
        self.exchange = exchange
        self.own, self.sent, self.planes = [], [], []
        self.far = 4
        self.near = exchange.count // 2 // self.far
        self.hops = [exchange.bits - 2, exchange.bits - 1, "last"]

    def add(self, own, other):
        self.own.append(own)
        self.sent.append(self.exchange.flip(other, 0, 0))

    def merge(self):
        parts = [a.astype(FULL) + b.astype(FULL) for a, b in zip(self.own, self.sent)]
        self.own, self.sent = [], []
        view = parts[0] if len(parts) == 1 else jnp.concatenate(parts, axis=-1)
        width = view.shape[-1]
        view = view.astype(LOW)
        if view.ndim == 2:
            view = view.reshape(self.far, self.near, -1, width).transpose(1, 0, 2, 3)
        self.merged = view.reshape(-1, width)

    def plane(self):
        groups = self.exchange.groups(2, self.near)
        self.planes.append(
            lax.psum_scatter(self.merged, AXES, scatter_dimension=0, axis_index_groups=groups, tiled=True)
        )

    def line(self):
        ex = self.exchange
        self.hops = ["last"]
        groups = ex.groups(2 * self.near, self.far)
        self.have = lax.psum_scatter(
            self.planes.pop(), AXES, scatter_dimension=0, axis_index_groups=groups, tiled=True
        )

    def begin(self):
        ex = self.exchange
        hop = self.hops[0]
        if self.planes:
            views = [p.reshape(2, 2, p.shape[0] // 4, p.shape[1]) for p in self.planes]
            self.have = views[0] if len(views) == 1 else jnp.concatenate(views, axis=3)
            self.planes = []
        if hop == "last":
            view = self.have.reshape(2, -1, self.have.shape[-1])
            self.sent_now = ex.pick(view, 0, 1 - ex.value(0)).astype(LOW)
            self.mine = ex.pick(view, 0, ex.value(0))
            self.got = ex.flip(self.sent_now, 0, 0)
        else:
            self.sent_now = ex.pick(self.have, len(self.hops) - 2, 1 - ex.value(hop)).astype(LOW)
            self.got = ex.flip(self.sent_now, hop, hop)

    def finish(self):
        ex = self.exchange
        hop = self.hops.pop(0)
        if hop != "last":
            self.have = ex.pick(self.have, len(self.hops) - 1, ex.value(hop)).astype(FULL) + self.got.astype(FULL)


def matmul(left, right, left_dim=1, right_dim=0):
    return lax.dot_general(
        left, right, (((left_dim,), (right_dim,)), ((), ())), preferred_element_type=FULL
    )


def cost(flops, moved, transcendentals=0):
    return pl.CostEstimate(flops=flops, bytes_accessed=moved, transcendentals=transcendentals)


def whole(shape):
    return pl.BlockSpec(shape, lambda *_: (0,) * len(shape), pipeline_mode=pl.Buffered(1))


def kept_block(shape):
    return pl.BlockSpec(shape, lambda *_: (0,) * len(shape))


def anywhere():
    return pl.BlockSpec(memory_space=pl.ANY)


def call(exchange, name, body, grid, ins, outs, scratch=(), work=None, onto=(), later_than=()):
    count_in, count_gone = len(ins), len(onto) + len(later_than)

    def kernel(index_ref, *refs):
        given = refs[:count_in]
        rest = refs[count_in + count_gone :]
        token_ref, results = rest[0], rest[1:]
        token_ref[0] = index_ref[0]
        body(index_ref, *given, *results)

    def out(shape, kind, place=None):
        return jax.ShapeDtypeStruct(shape, kind) if place is None else place(shape, kind)

    results = pl.pallas_call(
        kernel,
        grid_spec=pltpu.PrefetchScalarGridSpec(
            num_scalar_prefetch=1,
            grid=grid,
            in_specs=[spec for _, spec in ins] + [anywhere()] * count_gone,
            out_specs=[pl.BlockSpec(memory_space=pltpu.SMEM)] + [o[2] for o in outs],
            scratch_shapes=list(scratch),
        ),
        out_shape=[out((1,), jnp.int32)] + [out(o[0], o[1], *o[3:]) for o in outs],
        input_output_aliases={1 + count_in + i: 1 + i for i in range(len(onto))},
        compiler_params=pltpu.CompilerParams(vmem_limit_bytes=ROOM.get(name, 18) * MEGA),
        cost_estimate=work,
        name=name,
    )(exchange.index, *[a for a, _ in ins], *onto, *later_than)
    exchange.index = results[0]
    return results[1:]


def far(array):
    return pltpu.with_memory_space_constraint(array, pltpu.HBM)


def gate(exchange, *arrays):
    call(exchange, "gate", lambda index_ref: None, (1,), [], [], work=cost(1, 1), later_than=arrays)


def hold(exchange, array, later_than=()):
    return call(
        exchange, "hold", lambda index_ref, array_ref: None, (1,), [], [(array.shape, array.dtype, anywhere())],
        work=cost(1, 1), onto=[array], later_than=later_than,
    )[0]


def norm_stats(mixed):
    average = jnp.mean(mixed, axis=-1, keepdims=True)
    centered = mixed - average
    inv_std = lax.rsqrt(jnp.mean(centered * centered, axis=-1, keepdims=True) + NORM_EPS)
    return centered * inv_std, inv_std


def norm_pull(grad_out, normed, inv_std, gain):
    scaled = grad_out * gain
    return inv_std * (
        scaled
        - jnp.mean(scaled, axis=-1, keepdims=True)
        - normed * jnp.mean(scaled * normed, axis=-1, keepdims=True)
    )


def head_lanes(pair, head):
    lane = lax.broadcasted_iota(jnp.int32, pair.shape, 1)
    mine = (lane < HEAD_DIM) if head % 2 == 0 else (lane >= HEAD_DIM)
    return jnp.where(mine, pair, jnp.zeros((), pair.dtype))


def column_copies(core, own, other, first, target, sems):
    half = target.shape[1] // 2
    copies = []
    for i, (source, place) in enumerate(((own, core), (other, 1 - core))):
        at = pl.multiple_of(place * half, LANES)
        copies.append(
            pltpu.make_async_copy(
                source.at[:, first : first + half], target.at[:, pl.ds(at, half)], sems.at[i]
            )
        )
    return copies


def attend_kernel(index_ref, own_ref, other_ref, x_ref, seg_ref, comp_ref, proj_ref,
                  q_ref, k_ref, v_ref, ck_ref, cv_ref, lse_ref, ctx_ref, ctx_t, weights, sems):
    width = x_ref.shape[2]
    heads = width // HEAD_DIM
    copies = [
        column_copies(index_ref[0] & 1, own_ref, other_ref, kind * (width // 2), weights.at[kind], sems.at[kind])
        for kind in range(3)
    ]
    first = pl.program_id(0) == 0

    @pl.when(first)
    def _():
        for copy in sum(copies, []):
            copy.start()

    def arrive(kind):
        @pl.when(first)
        def _():
            for copy in copies[kind]:
                copy.wait()

    x = x_ref[0]
    arrive(0)
    q_ref[0] = matmul(x, weights[0]).astype(LOW)
    arrive(1)
    k_ref[0] = matmul(x, weights[1]).astype(LOW)
    arrive(2)
    v_ref[0] = matmul(x, weights[2]).astype(LOW)
    member = comp_ref[0] == seg_ref[0]
    masked = jnp.where(member, proj_ref[...], jnp.zeros((), LOW))
    ck_ref[0] = (matmul(masked, k_ref[0])).astype(LOW)
    cv = matmul(masked, v_ref[0])
    cv_ref[0] = cv.astype(LOW)
    cv_t = cv.T.astype(LOW)
    for head in range(heads):
        lanes = slice(head // 2 * LANES, head // 2 * LANES + LANES)
        rows = slice(head * HEAD_DIM, (head + 1) * HEAD_DIM)
        keys = head_lanes(ck_ref[0, :, lanes], head) * (HEAD_DIM ** -0.5)
        scores = matmul(keys.astype(LOW), q_ref[0, :, lanes], 1, 1)
        scores = jnp.where(member, scores, MASKED)
        highest = jnp.max(scores, axis=0, keepdims=True)
        weight = jnp.exp(scores - highest)
        total = jnp.sum(weight, axis=0, keepdims=True)
        lse_ref[0, head : head + 1, :] = highest + jnp.log(total)
        ctx_t[rows, :] = matmul(cv_t[rows, :], weight.astype(LOW)) * (1.0 / total)
    ctx_ref[0] = ctx_t[...].T.astype(LOW)


def attend(exchange, halves, x, seg, comp, proj, later_than):
    rows, length, width = x.shape
    slots = comp.shape[1]
    heads = width // HEAD_DIM

    def at(*shape):
        return pl.BlockSpec((1,) + shape, lambda i, _: (i, 0, 0))

    tokens = ((rows, length, width), LOW, at(length, width), pltpu.HBM)
    comps = ((rows, slots, width), LOW, at(slots, width), pltpu.HBM)
    flops = rows * (length * width * (2 * 3 * width + 4 * slots * 4) + slots * length * width * 4)
    return call(
        exchange, "attend", attend_kernel, (rows,),
        [(halves[0], anywhere()), (halves[1], anywhere()), (far(x), at(length, width)), (seg[:, None, :], at(1, length)),
         (comp[:, :, None], at(slots, 1)), (proj, whole((slots, length)))],
        [tokens] * 3 + [comps] * 2 + [((rows, heads, length), FULL, at(heads, length), pltpu.HBM), tokens],
        [pltpu.VMEM((width, length), FULL), pltpu.VMEM((3, width, width), LOW), pltpu.SemaphoreType.DMA((3, 2))],
        cost(flops, 20 * 10**6, rows * heads * slots * length), (), later_than,
    )


def mix_kernel(index_ref, own_ref, other_ref, x_ref, ctx_ref, gains_ref, normed_ref, inv_ref, low_ref, same_ref, weight, sems):
    @pl.when(pl.program_id(0) == 0)
    def _():
        first = own_ref.shape[1] - weight.shape[1] // 2
        copies = column_copies(index_ref[0] & 1, own_ref, other_ref, first, weight, sems)
        for copy in copies:
            copy.start()
        for copy in copies:
            copy.wait()

    mixed = x_ref[...].astype(FULL) + matmul(ctx_ref[...], weight[...])
    normed, inv_std = norm_stats(mixed)
    normed_ref[...] = normed
    inv_ref[...] = inv_std
    low_ref[...] = (normed * gains_ref[0:1].astype(FULL) + gains_ref[1:2].astype(FULL)).astype(LOW)
    same_ref[...] = low_ref[...]


def mix(exchange, halves, x, ctx, gains, later_than, tile=512):
    tokens, width = x.shape

    def some(n):
        return pl.BlockSpec((tile, n), lambda i, _: (i, 0))

    return call(
        exchange, "mix", mix_kernel, (tokens // tile,),
        [(halves[0], anywhere()), (halves[1], anywhere()), (far(x), some(width)), (far(ctx), some(width)),
         (gains, whole(gains.shape))],
        [((tokens, width), FULL, some(width), pltpu.HBM), ((tokens, 1), FULL, some(1), pltpu.HBM),
         ((tokens, width), LOW, some(width)), ((tokens, width), LOW, some(width), pltpu.HBM)],
        [pltpu.VMEM((width, width), LOW), pltpu.SemaphoreType.DMA((2,))],
        cost(2 * tokens * width * width, 10 * 10**6), (), later_than,
    )


def gelu_pair(h):
    t = pl.reciprocal(1.0 + (0.3275911 * 0.5**0.5) * jnp.abs(h), approx=True)
    bell = jnp.exp2(h * (h * (-0.5 * 1.4426950408889634)))
    poly = 0.127414796 + t * (-0.142248368 + t * (0.7107068705 + t * (-0.7265760135 + t * 0.5307027145)))
    tail = poly * (t * bell)
    cdf = jnp.where(h >= 0, 1.0 - tail, tail)
    return h * cdf, cdf + h * (bell * 0.3989422804014327)


def up_kernel(index_ref, f_ref, w_ref, act_ref, slope_ref):
    value, slope = gelu_pair(matmul(f_ref[...], w_ref[...]))
    act_ref[...] = value.astype(LOW)
    slope_ref[...] = slope.astype(LOW)


def up_part(exchange, f, half, mine, ff, onto, later_than, tile=768):
    tokens, width = f.shape
    steps = ff // tile // 2

    def place(j, index_ref):
        core = index_ref[0] & 1
        return (0, (core if mine else 1 - core) * steps + j)

    out = pl.BlockSpec((tokens, tile), place)
    return call(
        exchange, "up_part", up_kernel, (steps,),
        [(f, whole((tokens, width))), (half, pl.BlockSpec((width, tile), lambda j, _: (0, j)))],
        [((tokens, ff), LOW, out, pltpu.HBM)] * 2,
        (), cost(tokens * width * ff, 13 * 10**6, tokens * ff // 2), onto, later_than,
    )


def down_kernel(exchange, index_ref, part_0, part_1, part_2, part_3, act_ref, normed_ref, og_ref, gains_ref,
                out_ref, g_ref, low_ref, sums_ref, weight, sems):
    @pl.when(pl.program_id(0) == 0)
    def _():
        sums_ref[...] = jnp.zeros_like(sums_ref)
        copies = []
        for plane in range(weight.shape[0]):
            copies += part_copies(
                exchange, index_ref[0], (part_0, part_1, part_2, part_3), plane, weight.at[plane], sems.at[plane]
            )
        for copy in copies:
            copy.start()
        for copy in copies:
            copy.wait()

    first = normed_ref[...] * gains_ref[0:1].astype(FULL) + gains_ref[1:2].astype(FULL)
    normed, inv_std = norm_stats(first + matmul(act_ref[...], weight[...].reshape(-1, first.shape[1])))
    out_ref[...] = (normed * gains_ref[2:3].astype(FULL) + gains_ref[3:4].astype(FULL)).astype(LOW)
    top = og_ref[...].astype(FULL)
    grad = norm_pull(top, normed, inv_std, gains_ref[2:3].astype(FULL))
    g_ref[...] = grad
    low_ref[...] = grad.astype(LOW)
    sums_ref[0:1] += jnp.sum(top * normed, axis=0, keepdims=True)
    sums_ref[1:2] += jnp.sum(top, axis=0, keepdims=True)


def plane_shape(exchange, rows, width):
    chips = exchange.count // 2
    return (chips // 4, rows // chips, width)


def down_part(exchange, parts, act, normed, og, gains, later_than, tile=256):
    tokens, ff = act.shape
    width = normed.shape[1]
    plane = plane_shape(exchange, ff, width)

    def some(n):
        return pl.BlockSpec((tile, n), lambda i, _: (i, 0))

    return call(
        exchange, "down_part", lambda *refs: down_kernel(exchange, *refs), (tokens // tile,),
        [(p, anywhere()) for p in parts] + [(far(act), some(ff)), (far(normed), some(width)), (far(og), some(width)),
         (gains, whole(gains.shape))],
        [((tokens, width), LOW, some(width), pltpu.HBM), ((tokens, width), FULL, some(width), pltpu.HBM),
         ((tokens, width), LOW, some(width)), ((8, width), FULL, kept_block((8, width)))],
        [pltpu.VMEM((4,) + plane, LOW), pltpu.SemaphoreType.DMA((4, 2 * plane[0]))],
        cost(2 * tokens * width * ff, 23 * 10**6), (), later_than,
    )


def split_columns(index_ref, total, own_ref, other_ref):
    half = total.shape[1] // 2
    left, right = total[:, :half].astype(LOW), total[:, half:].astype(LOW)
    even = (index_ref[0] & 1) == 0
    store_rows(own_ref, jnp.where(even, left, right))
    store_rows(other_ref, jnp.where(even, right, left))


def store_rows(ref, rows):
    if len(ref.shape) == 2:
        ref[...] = rows
        return
    near, far_count = ref.shape[:2]
    parts = rows.reshape((far_count, near) + ref.shape[2:])
    for i in range(far_count):
        ref[:, i] = parts[i]


def by_plane(exchange, rows):
    far_count = 4
    chips = exchange.count // 2
    each = rows // chips
    return (chips // far_count, far_count, each) if each % 16 == 0 else None


def outer_kernel(index_ref, left_ref, *refs):
    *right_refs, own_ref, other_ref = refs
    for kind, right_ref in enumerate(right_refs):

        @pl.when(pl.program_id(0) == kind)
        def _(right_ref=right_ref):
            split_columns(index_ref, matmul(left_ref[...], right_ref[...], 0, 0), own_ref, other_ref)


def outer_part(exchange, left, rights, name, later_than, planes=False):
    tokens, depth = left.shape
    width = rights[0].shape[1]
    half = ((depth, len(rights) * width // 2), LOW, pl.BlockSpec((depth, width // 2), lambda j, _: (0, j)))
    plane = by_plane(exchange, depth)
    if planes and plane:
        spec = pl.BlockSpec(plane + (width // 2,), lambda j, _: (0, 0, 0, j))
        half = (plane + (len(rights) * width // 2,), LOW, spec)
    return call(
        exchange, name, outer_kernel, (len(rights),),
        [(far(left), whole((tokens, depth)))] + [(far(r) if planes else r, whole((tokens, width))) for r in rights],
        [half] * 2, (), cost(2 * tokens * depth * width * len(rights), 9 * 10**6), (), later_than,
    )


def down_grad_kernel(index_ref, act_ref, g_ref, own_ref, other_ref):
    split_columns(index_ref, matmul(act_ref[...], g_ref[...], 0, 0), own_ref, other_ref)


def down_grad_part(exchange, act, g, later_than, tile=768):
    tokens, ff = act.shape
    width = g.shape[1]
    half = ((ff, width // 2), LOW, pl.BlockSpec((tile, width // 2), lambda j, _: (j, 0)))
    plane = by_plane(exchange, ff)
    if plane and ff // plane[1] == tile:
        spec = pl.BlockSpec((plane[0], 1, plane[2], width // 2), lambda j, _: (0, j, 0, 0))
        half = (plane + (width // 2,), LOW, spec)
    return call(
        exchange, "down_grad_part", down_grad_kernel, (ff // tile,),
        [(far(act), pl.BlockSpec((tokens, tile), lambda j, _: (0, j))), (g, whole((tokens, width)))],
        [half] * 2, (), cost(2 * tokens * width * ff, 13 * 10**6), (), later_than,
    )


def ff_back_kernel(exchange, index_ref, part_0, part_1, part_2, part_3, up_own, up_other, slope_ref, low_ref, f_ref, start_ref, normed_ref,
                   inv_ref, gains_ref, *refs):
    own_ref, other_ref, g_one_ref, g_one_low_ref, sums_ref, total, w_down, normed, start, sems = refs
    step = pl.program_id(0)
    steps = pl.num_programs(0)
    half = steps // 2
    core = index_ref[0] & 1
    tile = slope_ref.shape[1]

    def copies(at):
        place = jnp.where(at < half, (1 - core) * half + at, core * half + at - half)
        parts = (part_0, part_1, part_2, part_3)
        return part_copies(exchange, index_ref[0], parts, place, w_down.at[at % 2], sems.at[at % 2])

    late = [
        pltpu.make_async_copy(normed_ref, normed, sems.at[2, 0]),
        pltpu.make_async_copy(start_ref, start, sems.at[2, 1]),
    ]

    @pl.when(step == 0)
    def _():
        for copy in copies(step):
            copy.start()
        for copy in late:
            copy.start()
        total[...] = jnp.zeros_like(total)

    @pl.when(step < steps - 1)
    def _():
        for copy in copies(step + 1):
            copy.start()

    for copy in copies(step):
        copy.wait()

    back = (matmul(low_ref[...], w_down[step % 2].reshape(tile, -1), 1, 1) * slope_ref[...].astype(FULL)).astype(LOW)
    grads = matmul(f_ref[...], back, 0, 0).astype(LOW)
    pl.when(step < half)(lambda: store_rows(other_ref, grads))
    pl.when(step >= half)(lambda: store_rows(own_ref, grads))

    def add(up_ref):
        total[...] += matmul(back, up_ref[...], 1, 1)

    pl.when(step < half)(lambda: add(up_other))
    pl.when(step >= half)(lambda: add(up_own))

    @pl.when(step == steps - 1)
    def _():
        for copy in late:
            copy.wait()
        top = total[...] + start[...]
        grad = norm_pull(top, normed[...], inv_ref[...], gains_ref[0:1].astype(FULL))
        g_one_ref[...] = grad
        g_one_low_ref[...] = grad.astype(LOW)
        sums_ref[...] = jnp.zeros_like(sums_ref)
        sums_ref[0:1] = jnp.sum(top * normed[...], axis=0, keepdims=True)
        sums_ref[1:2] = jnp.sum(top, axis=0, keepdims=True)


def ff_back(exchange, down, up, slope, low, f, start, normed, inv, gains, later_than, tile=768):
    tokens, ff = slope.shape
    width = f.shape[1]
    steps = ff // tile
    half = steps // 2

    def place(j, index_ref):
        core = index_ref[0] & 1
        return (0, jnp.where(j < half, (1 - core) * half + j, core * half + j - half))

    plane = plane_shape(exchange, ff, width)
    full = whole((tokens, width))
    result = kept_block((tokens, width))
    shape = by_plane(exchange, width) or (width,)

    def columns(place):
        return pl.BlockSpec(shape + (tile,), lambda j, _: (0,) * len(shape) + (place(j),))

    return call(
        exchange, "ff_back", lambda *refs: ff_back_kernel(exchange, *refs), (steps,),
        [(far(p), anywhere()) for p in down] + [
         (up[0], pl.BlockSpec((width, tile), lambda j, _: (0, jnp.maximum(j - half, 0)))),
         (up[1], pl.BlockSpec((width, tile), lambda j, _: (0, jnp.minimum(j, half - 1)))),
         (far(slope), pl.BlockSpec((tokens, tile), place)),
         (far(low), full), (far(f), full), (far(start), anywhere()), (far(normed), anywhere()), (far(inv), whole(inv.shape)), (gains, whole(gains.shape))],
        [(shape + (ff // 2,), LOW, columns(lambda j: jnp.maximum(j - half, 0))),
         (shape + (ff // 2,), LOW, columns(lambda j: jnp.minimum(j, half - 1)))]
        + [((tokens, width), FULL, result, pltpu.HBM), ((tokens, width), LOW, result, pltpu.HBM),
         ((8, width), FULL, kept_block((8, width)))],
        [pltpu.VMEM((tokens, width), FULL), pltpu.VMEM((2,) + plane, LOW), pltpu.VMEM((tokens, width), FULL),
         pltpu.VMEM((tokens, width), FULL),
         pltpu.SemaphoreType.DMA((3, 2 * plane[0]))],
        cost(6 * tokens * width * ff, 40 * 10**6), (), later_than,
    )


def attend_back_kernel(index_ref, own_ref, other_ref, g_ref, q_ref, k_ref, v_ref, ck_ref, cv_ref, lse_ref,
                       seg_ref, comp_ref, proj_ref,
                       gq_ref, gk_ref, gv_ref, grad_ref, gctx, gq_t, gck, gcv, weight, sems):
    width = q_ref.shape[2]
    heads = width // HEAD_DIM
    scale = HEAD_DIM ** -0.5

    @pl.when(pl.program_id(0) == 0)
    def _():
        copies = column_copies(
            index_ref[0] & 1, own_ref, other_ref, own_ref.shape[1] - width // 2, weight, sems
        )
        for copy in copies:
            copy.start()
        for copy in copies:
            copy.wait()

    gctx[...] = matmul(g_ref[0], weight[...], 1, 1).astype(LOW)
    member = comp_ref[0] == seg_ref[0]
    ck_t = ck_ref[0].astype(FULL).T.astype(LOW)
    for pair in range(heads // 2):
        lanes = slice(pair * LANES, pair * LANES + LANES)
        queries, grads = q_ref[0, :, lanes], gctx[:, lanes]
        key_parts, value_parts = [], []
        for head in (2 * pair, 2 * pair + 1):
            rows = slice(head * HEAD_DIM, (head + 1) * HEAD_DIM)
            keys = head_lanes(ck_ref[0, :, lanes], head) * scale
            scores = matmul(keys.astype(LOW), queries, 1, 1)
            probs = jnp.exp(jnp.where(member, scores - lse_ref[0, head : head + 1, :], MASKED))
            grad_probs = matmul(head_lanes(cv_ref[0, :, lanes], head), grads, 1, 1)
            delta = jnp.sum(probs * grad_probs, axis=0, keepdims=True)
            grad_scores = (probs * (grad_probs - delta)).astype(LOW)
            gq_t[rows, :] = matmul(ck_t[rows, :], grad_scores) * scale
            key_parts.append(matmul(grad_scores, queries))
            value_parts.append(matmul(probs.astype(LOW), grads))
        lane = lax.broadcasted_iota(jnp.int32, key_parts[0].shape, 1) < HEAD_DIM
        gck[:, lanes] = (jnp.where(lane, *key_parts) * scale).astype(LOW)
        gcv[:, lanes] = jnp.where(lane, *value_parts).astype(LOW)
    gq_ref[...] = gq_t[...].T.astype(LOW)
    masked = jnp.where(member, proj_ref[...], jnp.zeros((), LOW))
    gk_ref[...] = matmul(masked, gck[...], 0, 0).astype(LOW)
    gv_ref[...] = matmul(masked, gcv[...], 0, 0).astype(LOW)
    part = matmul(gck[...], k_ref[0], 1, 1) + matmul(gcv[...], v_ref[0], 1, 1)
    part = jnp.where(member, part, 0.0)

    @pl.when(pl.program_id(0) == 0)
    def _():
        grad_ref[...] = part

    @pl.when(pl.program_id(0) > 0)
    def _():
        grad_ref[...] += part


def attend_back(exchange, halves, g, kept, seg, comp, proj, later_than):
    q, k, v, ck, cv, lse = kept
    rows, length, width = q.shape
    slots = comp.shape[1]
    heads = width // HEAD_DIM

    def at(*shape):
        return pl.BlockSpec((1,) + shape, lambda i, _: (i, 0, 0))

    tokens = ((rows * length, width), LOW, pl.BlockSpec((length, width), lambda i, _: (i, 0)))
    flops = rows * length * width * (2 * width + 4 * slots * 10)
    return call(
        exchange, "attend_back", attend_back_kernel, (rows,),
        [(far(halves[0]), anywhere()), (far(halves[1]), anywhere())] + [(a, at(length, width)) for a in (far(g), far(q), far(k), far(v))]
        + [(far(a), at(slots, width)) for a in (ck, cv)]
        + [(far(lse), at(heads, length)), (seg[:, None, :], at(1, length)), (comp[:, :, None], at(slots, 1)),
           (far(proj), whole((slots, length)))],
        [tokens] * 3 + [((slots, length), FULL, kept_block((slots, length)))],
        [pltpu.VMEM((length, width), LOW), pltpu.VMEM((width, length), FULL),
         pltpu.VMEM((slots, width), LOW), pltpu.VMEM((slots, width), LOW),
         pltpu.VMEM((width, width), LOW), pltpu.SemaphoreType.DMA((2,))],
        cost(flops, 15 * 10**6, rows * heads * slots * length), (), later_than,
    )


def input_kernel(index_ref, own_ref, other_ref, g_ref, gq_ref, gk_ref, gv_ref, out_ref, weights, sems):
    width = g_ref.shape[1]

    @pl.when(pl.program_id(0) == 0)
    def _():
        copies = []
        for kind in range(3):
            copies += column_copies(
                index_ref[0] & 1, own_ref, other_ref, kind * (width // 2), weights.at[kind], sems.at[kind]
            )
        for copy in copies:
            copy.start()
        for copy in copies:
            copy.wait()

    out_ref[...] = (
        g_ref[...]
        + matmul(gq_ref[...], weights[0], 1, 1)
        + matmul(gk_ref[...], weights[1], 1, 1)
        + matmul(gv_ref[...], weights[2], 1, 1)
    )


def input_part(exchange, halves, g, gq, gk, gv, later_than, tile=256):
    tokens, width = g.shape
    some = pl.BlockSpec((tile, width), lambda i, _: (i, 0))
    return call(
        exchange, "input_part", input_kernel, (tokens // tile,),
        [(far(halves[0]), anywhere()), (far(halves[1]), anywhere())] + [(far(a), some) for a in (g, gq, gk, gv)],
        [((tokens, width), FULL, some)],
        [pltpu.VMEM((3, width, width), LOW), pltpu.SemaphoreType.DMA((3, 2))],
        cost(6 * tokens * width * width, 15 * 10**6), (), later_than,
    )[0]


def adaptive(first, second, grad):
    first_new = BETA_ONE * first + (1.0 - BETA_ONE) * grad
    second_new = BETA_TWO * second + (1.0 - BETA_TWO) * grad * grad
    direction = (
        first_new
        / (1.0 - BETA_ONE**STEP)
        / (jnp.sqrt(second_new / (1.0 - BETA_TWO**STEP)) + EPSILON)
    )
    return (first_new, second_new, direction)


def store_halves(index_ref, columns, left, right, own_ref, other_ref):
    even = (index_ref[0] & 1) == 0
    own_ref[:, columns] = jnp.where(even, left, right).astype(LOW)
    other_ref[:, columns] = jnp.where(even, right, left).astype(LOW)


def store_matrix(index_ref, columns, matrix, own_ref, other_ref):
    half = matrix.shape[1] // 2
    store_halves(index_ref, columns, matrix[:, :half], matrix[:, half:], own_ref, other_ref)


def pack_attn_kernel(index_ref, weight_ref, comp_ref, norm_ref, own_ref, other_ref, side):
    kinds = weight_ref.shape[0] - 1
    half = weight_ref.shape[2] // 2
    rows, length = comp_ref.shape
    pieces = length // side.shape[1]
    own, own_columns = norm_ref.shape
    side[...] = jnp.zeros_like(side)
    for i in range(pieces):
        side[i * rows : (i + 1) * rows, :] = comp_ref[:, i * side.shape[1] : (i + 1) * side.shape[1]]
    side[pieces * rows : pieces * rows + own, :own_columns] = norm_ref[...]
    for kind in range(kinds):
        store_matrix(index_ref, slice(kind * half, (kind + 1) * half), weight_ref[kind], own_ref, other_ref)
    store_matrix(index_ref, slice(kinds * half, None), side[...], own_ref, other_ref)


def pack_up_kernel(index_ref, weight_ref, out_ref, own_ref, other_ref):
    split = weight_ref.shape[1] // 2
    store_matrix(index_ref, slice(0, split), weight_ref[...], own_ref, other_ref)
    store_matrix(index_ref, slice(split, None), out_ref[0], own_ref, other_ref)


def pack_down_kernel(index_ref, weight_ref, own_ref, other_ref):
    store_matrix(index_ref, slice(None), weight_ref[...], own_ref, other_ref)


def squares_row(array):
    total = jnp.sum(jnp.sum(array * array, axis=0, keepdims=True), axis=1, keepdims=True)
    return jnp.broadcast_to(total, (1, LANES))


def step_matrix(weight, first, second, grad, first_ref, second_ref, direction_ref, sums_ref, row):
    first_new, second_new, direction = adaptive(first, second, grad)
    direction = direction + DECAY * weight
    first_ref[...] = first_new
    second_ref[...] = second_new
    direction_ref[...] = direction
    sums_ref[row : row + 1] = squares_row(weight)
    sums_ref[row + 8 : row + 9] = squares_row(direction)


def joined_halves(index_ref, mine, got):
    even = (index_ref[0] & 1) == 0
    return jnp.concatenate([jnp.where(even, mine, got), jnp.where(even, got, mine)], axis=1)


def down_step_kernel(index_ref, mine_ref, got_ref, weight_ref, first_ref, second_ref,
                     first_new, second_new, direction, sums_ref):
    sums_ref[...] = jnp.zeros_like(sums_ref)
    grad = joined_halves(index_ref, mine_ref[...].astype(FULL), got_ref[...].astype(FULL))
    step_matrix(weight_ref[...], first_ref[...], second_ref[...], grad, first_new, second_new, direction, sums_ref, 5)


def up_step_kernel(index_ref, mine_ref, got_ref, weight_ref, first_ref, second_ref, out_weight, out_first, out_second,
                   first_new, second_new, direction, out_first_new, out_second_new, out_direction, sums_ref):
    sums_ref[...] = jnp.zeros_like(sums_ref)
    split = weight_ref.shape[1] // 2
    mine, got = mine_ref[...].astype(FULL), got_ref[...].astype(FULL)
    grad = joined_halves(index_ref, mine[:, :split], got[:, :split])
    step_matrix(weight_ref[...], first_ref[...], second_ref[...], grad, first_new, second_new, direction, sums_ref, 4)
    grad = joined_halves(index_ref, mine[:, split:], got[:, split:])
    step_matrix(out_weight[0], out_first[0], out_second[0], grad,
                out_first_new, out_second_new, out_direction, sums_ref, 3)


def attn_step_kernel(index_ref, mine_ref, got_ref, weight_ref, first_ref, second_ref,
                     comp_weight, comp_first, comp_second, norm_weight, norm_first, norm_second,
                     out_first_new, up_sums, down_sums,
                     first_new, second_new, direction, comp_first_new, comp_second_new, comp_direction,
                     norm_first_new, norm_second_new, norm_new, sent_ref, sums_ref):
    sums_ref[...] = up_sums[...] + down_sums[...]
    kinds = weight_ref.shape[0] - 1
    width = weight_ref.shape[2]
    half = width // 2
    mine, got = mine_ref[...].astype(FULL), got_ref[...].astype(FULL)
    for kind in range(kinds):
        columns = slice(kind * half, (kind + 1) * half)
        grad = joined_halves(index_ref, mine[:, columns], got[:, columns])
        step_matrix(weight_ref[kind], first_ref[kind], second_ref[kind], grad,
                    first_new.at[kind], second_new.at[kind], direction.at[kind], sums_ref, kind)
    first_new[kinds] = out_first_new[...]
    side = joined_halves(index_ref, mine[:, kinds * half :], got[:, kinds * half :])
    rows, length = comp_weight.shape
    pieces = length // side.shape[1]
    grad = jnp.concatenate([side[i * rows : (i + 1) * rows] for i in range(pieces)], axis=1)
    step_matrix(comp_weight[...], comp_first[...], comp_second[...], grad,
                comp_first_new, comp_second_new, comp_direction, sums_ref, 6)
    own, own_columns = norm_weight.shape
    grad = side[pieces * rows : pieces * rows + own, :own_columns]
    new, newer, way = adaptive(norm_first[...], norm_second[...], grad)
    norm_first_new[...] = new
    norm_second_new[...] = newer
    norm_new[...] = norm_weight[...] - RATE * way
    sent_ref[...] = jnp.broadcast_to(sums_ref[...][None], sent_ref.shape)


def finish_kernel(index_ref, got_ref, weight_ref, direction_ref, out_direction, up_weight, up_direction,
                  down_weight, down_direction, comp_weight, comp_direction,
                  attn_new, attn_copy, up_new, up_copy, down_new, down_copy, comp_new, comp_copy, norms_ref):
    totals = jnp.sqrt(jnp.sum(got_ref[...], axis=0))
    lane = lax.broadcasted_iota(jnp.int32, (1, LANES), 1)
    count = norms_ref.shape[1]
    for i in range(2):
        row = sum(jnp.where(lane == m, totals[8 * i + m : 8 * i + m + 1], 0.0) for m in range(count))
        norms_ref[i : i + 1, :] = row[:, :count]
    ratio = totals[:8] / (totals[8:] + EPSILON)

    def move(weight, direction, matrix, new_ref, copy_ref):
        new = weight - RATE * ratio[matrix : matrix + 1, :1] * direction
        new_ref[...] = new
        copy_ref[...] = new.astype(LOW)

    for kind in range(4):
        way = direction_ref[kind] if kind < 3 else out_direction[...]
        move(weight_ref[kind], way, kind, attn_new.at[kind], attn_copy.at[kind])
    move(up_weight[...], up_direction[...], 4, up_new, up_copy)
    move(down_weight[...], down_direction[...], 5, down_new, down_copy)
    move(comp_weight[...], comp_direction[...], 6, comp_new, comp_copy)


def elementwise(exchange, name, body, ins, shapes, later_than=(), scratch=()):
    pairs = []
    for a in ins:
        if isinstance(a, tuple):
            shape, kind = (1,) + a[0].shape[1:], a[1]
            pairs.append((far(a[0]), pl.BlockSpec(shape, lambda *_, kind=kind: (kind, 0, 0))))
        else:
            pairs.append((far(a) if name.startswith("pack") else a, whole(a.shape)))
    return call(
        exchange, name, body, (1,), pairs, [(shape, kind, whole(shape)) for shape, kind in shapes], scratch,
        cost(10**6, sum(a.size * 4 for a, _ in pairs)), (), later_than,
    )


def local(
    dp,
    fsdp,
    inputs,
    segment_ids,
    compressed_segment,
    out_grad,
    attn_weight,
    attn_first,
    attn_second,
    up_weight,
    up_first,
    up_second,
    down_weight,
    down_first,
    down_second,
    compress_weight,
    compress_first,
    compress_second,
    norm_params,
    norm_first,
    norm_second,
):
    exchange = Exchange(dp, fsdp)
    devices = dp * fsdp
    row_count, length, model_width = inputs.shape
    half_width = model_width // 2
    token_count = row_count * length
    norm_kinds, norm_own = norm_params.shape
    attn_kinds, attn_own, _ = attn_weight.shape
    compress_own = compress_weight.shape[0]
    pieces = 2 if 2 * compress_own + norm_kinds <= attn_own else 1
    side_width = length // pieces

    def side_rows(compress_part, norm_part):
        none = [(0, 0)] * (compress_part.ndim - 2)
        spare = attn_own - pieces * compress_own - norm_kinds
        norm_part = jnp.pad(norm_part, none + [(0, spare), (0, side_width - norm_own)])
        parts = [compress_part[..., i * side_width : (i + 1) * side_width] for i in range(pieces)]
        return jnp.concatenate(parts + [norm_part], axis=-2)

    def halves(array):
        middle = array.shape[-1] // 2
        return array[..., :middle], array[..., middle:]

    flat_in = inputs.reshape(token_count, model_width)
    ff = up_weight.shape[1]
    out_kind = attn_kinds - 1
    out_at = [(a, out_kind) for a in (attn_weight, attn_first, attn_second)]
    attn = Gather(
        exchange,
        *elementwise(
            exchange, "pack_attn", pack_attn_kernel, [attn_weight, compress_weight, norm_params],
            [((attn_own, out_kind * half_width + side_width // 2), LOW)] * 2, (),
            [pltpu.VMEM((attn_own, side_width), FULL)],
        ),
    )
    attn.begin()
    up = Gather(
        exchange,
        *elementwise(
            exchange, "pack_up", pack_up_kernel, [up_weight, out_at[0]],
            [((attn_own, (ff + model_width) // 2), LOW)] * 2, [attn.mine],
        ),
    )
    up.begin()
    attn.finish()
    attn.begin()
    up.finish()
    up.have = hold(exchange, up.have)
    up.spread()
    attn.finish()
    for _ in exchange.rest[1:]:
        attn.hop()
    attn.hop()
    attn.hop()
    attn.begin()
    down = Gather(
        exchange,
        *elementwise(
            exchange, "pack_down", pack_down_kernel, [down_weight], [((down_weight.shape[0], half_width), LOW)] * 2,
            [attn.have],
        ),
        together=True,
    )
    down.hop()
    down.begin()
    attn.finish()
    side_own, side_other = [part[:, -side_width // 2 :] for part in attn.halves]
    side = jnp.concatenate(
        [exchange.by_core(side_own, side_other), exchange.by_core(side_other, side_own)], axis=1
    ).reshape(devices, attn_own, side_width)
    compress_full = jnp.concatenate(
        [side[:, i * compress_own : (i + 1) * compress_own] for i in range(pieces)], axis=2
    ).reshape(-1, length)
    gains = (
        side[:, pieces * compress_own : pieces * compress_own + norm_kinds, :norm_own]
        .transpose(1, 0, 2)
        .reshape(norm_kinds, model_width)
    )

    *kept, context = attend(
        exchange, attn.halves, inputs, segment_ids, compressed_segment, compress_full, [down.have]
    )
    context = context.reshape(token_count, model_width)
    down.finish()
    down.begin()
    up.have = hold(exchange, up.have, [down.have])
    up.begin()
    up.finish()
    first_normed, first_inv, first_low, first_low_far = mix(exchange, up.halves, flat_in, context, gains, [down.have])
    down.finish()
    down.parts_begin()
    hidden = up_part(exchange, first_low, up.halves[0], True, ff, (), [down.have])
    down.parts_finish()
    active, slope = up_part(exchange, first_low, up.halves[1], False, ff, hidden, [down.got])
    result, grad_second, grad_second_low, sums_two = down_part(
        exchange, down.parts, active, first_normed, out_grad.reshape(token_count, model_width), gains, []
    )

    down_sum, up_sum, attn_sum = Reduce(exchange), Reduce(exchange), Scatter(exchange)
    down_own, down_other = down_grad_part(exchange, active, grad_second_low, [])
    down_sum.add(down_own, down_other)
    down_sum.merge()
    up_own, up_other, grad_first, grad_first_low, sums_one = ff_back(
        exchange, down.parts, up.halves, slope, grad_second_low, first_low_far, grad_second,
        first_normed, first_inv, gains, [far(down_sum.merged)],
    )
    down_sum.plane()
    up_sum.add(up_own, up_other)
    out_own, out_other = outer_part(exchange, context, [grad_first_low], "out_grad_part", [], True)
    up_sum.add(out_own, out_other)
    up_sum.merge()
    *grads, comp_grad = attend_back(
        exchange, up.halves, grad_first_low.reshape(inputs.shape), kept,
        segment_ids, compressed_segment, compress_full, [far(up_sum.merged)] + [far(p) for p in down_sum.planes],
    )
    up_sum.plane()
    qkv_own, qkv_other = outer_part(exchange, flat_in, grads, "qkv_grad_part", [])
    norm_grad = jnp.concatenate([sums_one[:2], sums_two[:2]])
    side_grad = side_rows(
        comp_grad.reshape(devices, compress_own, length),
        norm_grad.reshape(norm_kinds, devices, norm_own).transpose(1, 0, 2),
    ).reshape(model_width, side_width).astype(LOW)
    side_left, side_right = halves(side_grad)
    attn_sum.add(qkv_own, qkv_other)
    attn_sum.add(exchange.by_core(side_left, side_right), exchange.by_core(side_right, side_left))
    attn_sum.merge()
    attn_sum.begin()
    up_sum.begin()
    input_grad = input_part(
        exchange, attn.halves, grad_first, *grads, [attn_sum.sent_now, up_sum.sent_now]
    )
    down_sum.line()

    up_sum.finish()
    up_sum.begin()
    attn_sum.finish()
    attn_sum.begin()
    gate(exchange, attn_sum.sent_now, up_sum.sent_now)
    up_sum.finish()
    up_sum.begin()
    attn_sum.finish()
    attn_sum.begin()
    gate(exchange, attn_sum.sent_now, up_sum.sent_now)
    attn_sum.finish()
    attn_sum.begin()
    out_shape = attn_weight.shape[1:]
    up_first_new, up_second_new, up_direction, out_first_new, out_second_new, out_direction, up_squares = elementwise(
        exchange, "up_step", up_step_kernel,
        [up_sum.mine, up_sum.got, up_weight, up_first, up_second] + out_at,
        [(up_weight.shape, FULL)] * 3 + [(out_shape, FULL)] * 3 + [((16, LANES), FULL)], [attn_sum.sent_now],
    )
    down_sum.begin()
    attn_sum.finish()
    attn_sum.begin()
    down_first_new, down_second_new, down_direction, down_squares = elementwise(
        exchange, "down_step", down_step_kernel,
        [down_sum.mine, down_sum.got, down_weight, down_first, down_second],
        [(down_weight.shape, FULL)] * 3 + [((16, LANES), FULL)], [attn_sum.sent_now],
    )
    attn_sum.finish()
    while attn_sum.hops:
        attn_sum.hop()
    three = (out_kind,) + out_shape
    (
        attn_first_new, attn_second_new, attn_direction,
        compress_first_new, compress_second_new, compress_direction,
        norm_first_new, norm_second_new, norm_new, sent, _,
    ) = elementwise(
        exchange, "attn_step", attn_step_kernel,
        [attn_sum.mine, attn_sum.got, attn_weight, attn_first, attn_second,
         compress_weight, compress_first, compress_second, norm_params, norm_first, norm_second,
         out_first_new, up_squares, down_squares],
        [(attn_weight.shape, FULL), (three, FULL), (three, FULL)] + [(compress_weight.shape, FULL)] * 3
        + [(norm_params.shape, FULL)] * 3 + [((devices, 16, LANES), FULL), ((16, LANES), FULL)],
    )
    got = lax.all_to_all(sent, AXES, split_axis=0, concat_axis=0, tiled=True)
    attn_new, attn_copy, up_new, up_copy, down_new, down_copy, compress_new, compress_copy, norms = elementwise(
        exchange, "finish", finish_kernel,
        [got, attn_weight, attn_direction, out_direction, up_weight, up_direction, down_weight, down_direction,
         compress_weight, compress_direction],
        [(a.shape, t) for a in (attn_weight, up_weight, down_weight, compress_weight) for t in (FULL, LOW)]
        + [((2, attn_kinds + 3), FULL)],
    )
    return (
        result.reshape(row_count, length, model_width),
        input_grad.reshape(row_count, length, model_width),
        attn_first_new,
        attn_second_new,
        out_second_new,
        attn_new,
        attn_copy,
        up_first_new,
        up_second_new,
        up_new,
        up_copy,
        down_first_new,
        down_second_new,
        down_new,
        down_copy,
        compress_first_new,
        compress_second_new,
        compress_new,
        compress_copy,
        norm_first_new,
        norm_second_new,
        norm_new,
        norms,
    )


def solution(mesh):
    rows, mid, flat = P(AXES, None), P(None, AXES, None), P(None, AXES)
    deep = P(AXES, None, None)

    def step(*args):
        return local(mesh.shape["dp"], mesh.shape["fsdp"], *args)

    return jax.shard_map(
        step,
        mesh=mesh,
        in_specs=(deep, rows, rows, deep) + (mid,) * 3 + (rows,) * 9 + (flat,) * 3,
        out_specs=(deep, deep, mid, mid, rows, mid, mid)
        + (rows,) * 12
        + (flat,) * 3
        + (P(),),
        check_vma=False,
    )
```
